32 devices in a mesh: depth: 8 (over z, x), row: 4 (over y, core).
Axes of the slice: x: 2, y: 2, z: 4, core: 2. Of those that a mesh axis runs over, the one named last changes fastest.
Arguments:
- fields: bfloat16 [4, 64, 128, 256], P(None, 'depth', 'row'), may hold values from -48 to 48
- w_in: float32 [32, 12], replicated, may hold values from -1.75 to 1.75
- b_in: float32 [32], replicated, may hold values from -3 to 3
- w_out: float32 [4, 32], replicated, may hold values from -1 to 1
- b_out: float32 [4], replicated, may hold values from -6 to 6
Outputs:
- image: float32 [4, 128, 256], P(None, 'row')
The draws below stay inside these ranges and needn't reach their ends.
All inputs are finite; a program needn't handle non-finite values.
Results may differ from the reference program's by a relative error of at most 0.00035.
Values may be sent and summed in bfloat16 or wider, within the bound.
No kernel may reach another device: no remote copies, remote signals or barrier semaphores. Data moves between devices by JAX's collectives and lax.ppermute only.
A program may use at most 64 MiB of HBM per device.

```python
import jax
import jax.numpy as jnp
from jax import lax

FIELDS = 4
FEAT = 12
HID = 32
OUTC = 4
DZ = 8
CX = 256
NZ = 64
NY = 128
N_DEPTH = 8


def shard_levels(rng, dims, pieces, least, high):
    loudness, own = 1.0, jax.random.fold_in(rng, 6)
    for axis_at, parts in pieces:
        heights = jnp.exp(jax.random.uniform(jax.random.fold_in(own, axis_at), (parts,), jnp.float32, least / len(pieces), high / len(pieces)))
        loudness = loudness * jnp.repeat(heights, dims[axis_at] // parts).reshape([-1 if axis == axis_at else 1 for axis in range(len(dims))])
    return loudness


def noise(key, shape, deviation, limit, shards=(), kind=jnp.bfloat16):
    loudness = shard_levels(key, shape, shards, -0.22, 0.18) if shards else 1.0
    drawn = jax.random.normal(key, shape, jnp.float32) * deviation * loudness
    return jnp.minimum(jnp.maximum(drawn, -limit), limit).astype(kind)


def setup_inputs(seed: int = 0) -> dict:
    key_of = jax.random.split(jax.random.key(seed), 6)
    return {
        "fields": noise(key_of[0], (FIELDS, NZ, NY, CX), 8.0, 48.0, ((1, 8), (2, 4))),
        "w_in": noise(key_of[1], (HID, FEAT), FEAT ** -0.5, 1.75, (), jnp.float32),
        "b_in": noise(key_of[2], (HID,), 0.5, 3.0, (), jnp.float32),
        "w_out": noise(key_of[3], (OUTC, HID), HID ** -0.5, 1.0, (), jnp.float32),
        "b_out": noise(key_of[4], (OUTC,), 1.0, 6.0, (), jnp.float32),
    }


smooth_taps = (1.0 / 64, 6.0 / 64, 15.0 / 64, 20.0 / 64, 15.0 / 64, 6.0 / 64, 1.0 / 64)
slope_taps = (-1.0 / 60, 9.0 / 60, -45.0 / 60, 0.0, 45.0 / 60, -9.0 / 60, 1.0 / 60)
depth_scale = 2.0


def filter_axis(values, taps, axis):
    count = values.shape[axis] - 6
    total = taps[0] * lax.slice_in_dim(values, 0, count, axis=axis)
    for place in range(1, 7):
        total = total + taps[place] * lax.slice_in_dim(values, place, place + count, axis=axis)
    return total


def smooth_block(block):
    along_z = filter_axis(block, smooth_taps, 1)
    along_y = filter_axis(along_z, smooth_taps, 2)
    padded = jnp.pad(along_y, ((0, 0), (0, 0), (0, 0), (3, 3)))
    return filter_axis(padded, smooth_taps, 3)


def shade(center, slope_y, slope_z, w_in, b_in, w_out, b_out, total_depth):
    depth_n = center.shape[1]
    features = jnp.concatenate([center, slope_y, slope_z], 0).reshape(12, -1)
    hidden = jnp.tanh(jnp.dot(w_in, features, precision=lax.Precision.HIGHEST, preferred_element_type=jnp.float32) + b_in[:, None])
    out = jnp.dot(w_out, hidden, precision=lax.Precision.HIGHEST, preferred_element_type=jnp.float32) + b_out[:, None]
    rgb = jax.nn.sigmoid(out[0:3]).reshape(3, depth_n, -1)
    optical = (jax.nn.softplus(out[3]) * (depth_scale / total_depth)).reshape(depth_n, -1)
    alpha = 1.0 - jnp.exp(-optical)
    before = jnp.cumsum(optical, axis=0) - optical
    weight = jnp.exp(-before) * alpha
    color = jnp.sum(weight[None] * rgb, axis=1)
    through = jnp.exp(-jnp.sum(optical, axis=0))
    return jnp.concatenate([color, through[None]], 0)


def reference(fields, w_in, b_in, w_out, b_out):
    padded = jnp.pad(fields, ((0, 0), (6, 6), (6, 6), (0, 0)))

    def slab_image(start):
        block = lax.dynamic_slice_in_dim(padded, start, DZ + 12, 1).astype(jnp.float32)
        smoothed = smooth_block(block)
        zpos = start - 3 + lax.iota(jnp.int32, DZ + 6)
        ypos = lax.iota(jnp.int32, NY + 6) - 3
        inside = ((zpos >= 0) & (zpos < NZ))[:, None, None] & ((ypos >= 0) & (ypos < NY))[None, :, None]
        smoothed = jnp.where(inside[None], smoothed, 0.0)
        center = smoothed[:, 3:-3, 3:-3, :]
        slope_z = filter_axis(smoothed[:, :, 3:-3, :], slope_taps, 1)
        slope_y = filter_axis(smoothed[:, 3:-3, :, :], slope_taps, 2)
        return shade(center, slope_y, slope_z, w_in, b_in, w_out, b_out, NZ)

    starts = jnp.arange(N_DEPTH, dtype=jnp.int32) * DZ
    slabs = lax.map(slab_image, starts)

    def compose(carry, piece):
        color, through = carry
        return (color + through[None] * piece[0:3], through * piece[3]), None

    start_color = jnp.zeros((3, NY * CX), jnp.float32)
    start_through = jnp.ones((NY * CX,), jnp.float32)
    (color, through), unused = lax.scan(compose, (start_color, start_through), slabs)
    image = jnp.concatenate([color, (1.0 - through)[None]], 0)
    return image.reshape(4, NY, CX)
```

```python
import functools

import jax
import jax.numpy as jnp
from jax import lax
from jax.experimental import pallas as pl
from jax.experimental.pallas import tpu as pltpu
from jax.sharding import PartitionSpec as P

FIELDS = 4
HALO = 6
LANES = 128
HIGHEST = lax.Precision.HIGHEST
F32 = jnp.float32
BF16 = jnp.bfloat16
depth_scale = 2.0
smooth_counts = (20.0, 15.0, 6.0, 1.0)
slope_counts = ((1, 45.0), (2, -9.0), (3, 1.0))


def dot(a, b, precision=None):
    return jnp.dot(a, b, preferred_element_type=F32, precision=precision)


def iota(shape, dim):
    return lax.broadcasted_iota(jnp.int32, shape, dim)


def smooth_count(distance):
    d = jnp.abs(distance)
    out = jnp.where(d == 0, smooth_counts[0], 0.0)
    for place in (1, 2, 3):
        out = jnp.where(d == place, smooth_counts[place], out)
    return out.astype(F32)


def split(x):
    high = x.astype(BF16)
    return high, (x - high.astype(F32)).astype(BF16)


def pack_kernel(fields, mine, theirs, straight, diagonal, left, right):
    side = lax.axis_index("depth") & 1
    layers, rows = fields.shape[1], fields.shape[2]
    kw, kh = layers * FIELDS, HALO * FIELDS
    for layer in range(layers):
        for field in range(FIELDS):
            plane = fields[field, layer].astype(F32)
            place = pl.ds(layer * FIELDS + field, rows, stride=kw)
            left[place, :] = plane[:, :LANES]
            right[place, :] = plane[:, LANES:]
    lane = iota((kw, LANES), 1)
    shift = pl.multiple_of(side * (kw - kh), 8)

    def halves(row, start, count):
        a = left[pl.ds(row * kw + start, count), :]
        b = right[pl.ds(row * kw + start, count), :]
        return jnp.where(side == 0, a, b), jnp.where(side == 0, b, a)

    extra_low = jnp.zeros((kw, LANES), F32)
    extra_high = jnp.zeros((kw, LANES), F32)
    for row in range(0, rows, 2):
        pairs = []
        for r in (row, row + 1):
            a = left[pl.ds(r * kw, kw), :]
            b = right[pl.ds(r * kw, kw), :]
            inside = (lane >= 3 * r) & (lane < 3 * r + 3)
            extra_low = jnp.where(inside, pltpu.roll(b, (3 * r) % LANES, 1), extra_low)
            extra_high = jnp.where(inside, pltpu.roll(a, (3 * r + 3) % LANES, 1), extra_high)
            own = jnp.where(side == 0, a, b)
            other = jnp.where(side == 0, b, a)
            mine[pl.ds(r * kw, kw), :] = own.astype(BF16)
            theirs[pl.ds(r * kw, kw), :] = other.astype(BF16)
            pairs.append(halves(r, shift, kh))
        both = pl.ds(row * kh, 2 * kh)
        straight[both, :] = jnp.concatenate([pairs[0][0], pairs[1][0]], 0).astype(BF16)
        diagonal[both, :] = jnp.concatenate([pairs[0][1], pairs[1][1]], 0).astype(BF16)
    own = jnp.where(side == 0, extra_low, extra_high)
    other = jnp.where(side == 0, extra_high, extra_low)
    mine[rows * kw :, :] = own.astype(BF16)
    theirs[rows * kw :, :] = other.astype(BF16)
    empty = jnp.zeros((kw - kh, LANES), F32)
    for source, target in ((own, straight), (other, diagonal)):
        part = jnp.where(side == 0, source[:kh], source[kw - kh :])
        target[rows * kh :, :] = jnp.concatenate([part, empty], 0).astype(BF16)


def band_kernel(mine, swap, straight, diagonal, first, second):
    odd = lax.axis_index("row") & 1
    kw = 8 * FIELDS
    rows = mine.shape[0] // kw - 1
    for out, from_end in ((first, 1 - odd), (second, odd)):
        at, extra = 0, HALO * sum(r.shape[0] // (rows + 1) for r in (mine, swap)) + 2 * HALO * HALO * FIELDS
        for source in (mine, swap, straight, diagonal):
            width = kw if source.shape[0] == (rows + 1) * kw else HALO * FIELDS
            start = pl.multiple_of(from_end * (rows - HALO) * width, 16)
            out[at : at + HALO * width, :] = source[pl.ds(start, HALO * width), :]
            out[extra : extra + 32, :] = source[rows * width : rows * width + 32, :]
            at += HALO * width
            extra += 32


def weights_kernel(params, w1, w2a, w2b, bias2, *, layers, hidden, slabs):
    depth = lax.axis_index("depth")
    side = depth & 1
    base = (depth - side) * layers
    total = slabs * layers
    zs = 2 * layers
    kk = (2 * layers + 2 * HALO) * FIELDS
    width = w1.shape[1] // 3
    table = params[0:hidden, :]
    row, col = iota((LANES, width), 0), iota((LANES, width), 1)
    field = col & 3
    pick1 = jnp.where(col < kk, field, jnp.where(col < 2 * kk, field + 4, jnp.where(col == 2 * kk, 12, -1)))
    pick2 = jnp.where(col < kk, field + 8, -1)
    part1 = dot(table, (row == pick1).astype(F32), HIGHEST)
    part2 = dot(table, (row == pick2).astype(F32), HIGHEST)
    kappa = iota((hidden, width), 1)
    slot = jnp.where(kappa < kk, kappa, kappa - kk) >> 2
    low, high = slot - 4 * layers // 2 - HALO, slot - 2 * layers
    zk = jnp.where(slot < layers, side * layers + slot, (1 - side) * layers + slot - layers)
    below, above = 2 * layers, -HALO
    zk = jnp.where(slot >= 2 * layers, high + jnp.where(side == 0, below, above), zk)
    zk = jnp.where(slot >= 2 * layers + HALO, low + jnp.where(side == 0, above, below), zk)
    scale = 1.0 / 64.0**3
    for z in range(zs):
        distance = zk - z
        center = smooth_count(distance) * scale
        slope = jnp.zeros((hidden, width), F32)
        for offset, count in slope_counts:
            for sign in (1, -1):
                at = base + z + sign * offset
                inside = ((at >= 0) & (at < total)).astype(F32)
                slope = slope + (inside * (sign * count)) * smooth_count(distance - sign * offset)
        center = jnp.where(kappa < kk, center, jnp.where(kappa < 2 * kk, center * (1.0 / 60.0), 1.0))
        high_part, low_part = split(center * part1 + (slope * (scale / 60.0)) * part2)
        at = pl.ds(z * hidden, hidden)
        w1[at, 0:width] = high_part
        w1[at, width : 2 * width] = low_part
        w1[at, 2 * width :] = high_part
    outs = FIELDS * layers
    rr, cc = iota((outs, LANES), 0), iota((outs, LANES), 1)
    group = layers * hidden
    source = params[hidden : hidden + 8, :]
    rows8 = iota((outs, 8), 0) // layers == iota((outs, 8), 1)
    spread = dot(rows8.astype(F32), source, HIGHEST)
    across = iota((LANES, group), 0) == (iota((LANES, group), 1) & (hidden - 1))
    full = dot(spread, across.astype(F32), HIGHEST)
    diagonal = (iota((outs, group), 0) & (layers - 1)) == iota((outs, group), 1) // hidden
    high_part, low_part = split(jnp.where(diagonal, full, 0.0))
    w2a[0:outs, :] = high_part
    w2a[outs:, :] = low_part
    w2b[...] = high_part
    bias = jnp.sum(jnp.where(cc == hidden, spread, 0.0), axis=1, keepdims=True)
    bias2[...] = jnp.broadcast_to(bias, bias2.shape)


def shade_kernel(mine, swap, straight, diagonal, first, second, w1, w2a, w2b, bias2, out, grid, edge, xhi, xlo, *, layers, rows):
    side = lax.axis_index("depth") & 1
    band = lax.axis_index("row")
    bands = lax.axis_size("row")
    odd = band & 1
    kw, kh = layers * FIELDS, HALO * FIELDS
    kk = 2 * (kw + kh)
    offsets = ((mine, 0, kw), (swap, kw, kw), (straight, 2 * kw, kh), (diagonal, 2 * kw + kh, kh))
    i, j = iota((LANES, LANES), 0), iota((LANES, LANES), 1)
    taps = smooth_count(i - j).astype(BF16)
    ir, ic = i // 3, i % 3
    spot = jnp.where(side == 0, (j + 3) & (LANES - 1), j)
    jr, jc = spot // 3, spot % 3
    apart = jnp.where(side == 0, ic - jc + 3, jc - ic + 3)
    border = jnp.where((ir == jr) & (i < 3 * rows) & (spot < 3 * rows), smooth_count(apart), 0.0).astype(BF16)
    for source, at, width in offsets:
        filtered = dot(source[0 : rows * width, :], taps)
        grid[HALO : HALO + rows, at : at + width, :] = filtered.reshape(rows, width, LANES)
        edge[0, at : at + width, :] = dot(source[rows * width : rows * width + 32, :], border)[:width]
    far = HALO + rows
    for source, base, which in ((first, odd, 2 - odd), (second, 1 - odd, 1 + odd)):
        place = (1 - base) * far
        start, extra = 0, HALO * kk
        filtered = dot(source[0 : HALO * kk, :], taps)
        edges = dot(source[HALO * kk :, :], border)
        for index, (unused, at, width) in enumerate(offsets):
            piece = filtered[start : start + HALO * width].reshape(HALO, width, LANES)
            grid[pl.ds(place, HALO), at : at + width, :] = piece
            edge[which, at : at + width, :] = edges[index * 32 : index * 32 + width]
            start += HALO * width
    lane = iota((16, LANES), 1)
    near = ((lane + jnp.where(side == 0, 3, 0)) & (LANES - 1)) < 3
    above = (band > 0).astype(F32)
    below = (band < bands - 1).astype(F32)

    def filter_rows(group, carry):
        at = pl.ds(pl.multiple_of(group * 16, 16), 16)
        after = pl.ds(pl.multiple_of(group * 16 + kk, 16), 16)
        edges = [edge[k, at, :] for k in range(3)]
        chain = [None] * 6
        ring = []
        for r in range(rows + 2 * HALO):
            which = 1 if r < HALO else 0 if r < HALO + rows else 2
            own_row = (r - HALO) % rows
            turned = pltpu.roll(edges[which], (-3 * own_row) % LANES, 1)
            value = grid[r, at, :] + jnp.where(near, turned, 0.0)
            for level in range(6):
                previous, chain[level] = chain[level], value
                if previous is None:
                    value = None
                    break
                value = previous + value
            if value is None:
                continue
            y = r - HALO - 3
            if y < 0:
                value = value * above
            elif y >= rows:
                value = value * below
            ring.append(value)
            if len(ring) == 7:
                slope = (ring[6] - ring[0]) - 9.0 * (ring[5] - ring[1]) + 45.0 * (ring[4] - ring[2])
                y -= 3
                xhi[y, at, :], xlo[y, at, :] = split(ring[3])
                xhi[y, after, :], xlo[y, after, :] = split(slope)
                ring.pop(0)
        return carry

    lax.fori_loop(0, kk // 16, filter_rows, 0)
    rest = xhi.shape[1] - 2 * kk
    ones = jnp.where(iota((rest, LANES), 0) == 0, 1.0, 0.0).astype(BF16)
    for y in range(rows):
        xhi[y, 2 * kk :, :] = ones
        xlo[y, 2 * kk :, :] = jnp.zeros((rest, LANES), BF16)
    wide = 2 * LANES
    outs = FIELDS * layers
    group = w2a.shape[1]
    sub = iota((layers, wide), 0)
    scale = depth_scale / (lax.axis_size("depth") * layers)

    def shade(pair, carry):
        y = 2 * pair
        high = jnp.concatenate([xhi[y], xhi[y + 1]], 1)
        low = jnp.concatenate([xlo[y], xlo[y + 1]], 1)
        stacked = jnp.concatenate([high, high, low], 0)
        total = jnp.zeros((1, wide), F32)
        front = jnp.ones((1, wide), F32)
        color = [jnp.zeros((layers, wide), F32) for unused in range(3)]
        for half in range(2):
            hidden = jnp.tanh(dot(w1[half * group : (half + 1) * group, :], stacked))
            hidden_high, hidden_low = split(hidden)
            o = dot(w2a[...], hidden_high)
            o = o[:outs] + o[outs:] + dot(w2b[...], hidden_low) + bias2[...]
            x = o[3 * layers :]
            optical = (jnp.maximum(x, 0.0) + jnp.log1p(jnp.exp(-jnp.abs(x)))) * scale
            through = optical
            for step in (1, 2, 4):
                through = through + jnp.where(sub >= step, pltpu.roll(through, step, 0), 0.0)
            through = through + total
            total = through[layers - 1 :]
            after = jnp.exp(-through)
            before = jnp.where(sub == 0, front, pltpu.roll(after, 1, 0))
            front = after[layers - 1 :]
            weight = before - after
            for c in range(3):
                color[c] = color[c] + weight / (1.0 + jnp.exp(-o[c * layers : (c + 1) * layers]))
        for c in range(3):
            line = jnp.sum(color[c], axis=0, keepdims=True)
            out[c, pl.ds(y, 1), :] = line[:, :LANES]
            out[c, pl.ds(y + 1, 1), :] = line[:, LANES:]
        out[3, pl.ds(y, 1), :] = front[:, :LANES]
        out[3, pl.ds(y + 1, 1), :] = front[:, LANES:]
        return carry

    lax.fori_loop(0, rows // 2, shade, 0)


def call(kernel, out_shape, operands, scratch=(), flops=0, name=None):
    vmem = pl.BlockSpec(memory_space=pltpu.VMEM)
    return pl.pallas_call(
        kernel,
        out_shape=out_shape,
        in_specs=[vmem] * len(operands),
        out_specs=jax.tree.map(lambda unused: vmem, out_shape),
        scratch_shapes=list(scratch),
        compiler_params=pltpu.CompilerParams(vmem_limit_bytes=40 * 2**20),
        cost_estimate=pl.CostEstimate(flops=flops, bytes_accessed=2**20, transcendentals=0),
        name=name,
    )(*operands)


def combine(front, back):
    color = front[0:3] + front[3:4] * back[0:3]
    return jnp.concatenate([color, front[3:4] * back[3:4]], 0)


def local(fields, w_in, b_in, w_out, b_out):
    layers, rows, columns = fields.shape[1:]
    hidden = w_in.shape[0]
    slabs = lax.axis_size("depth")
    bands = lax.axis_size("row")
    me = lax.axis_index("depth")
    side = me & 1
    kw, kh = layers * FIELDS, HALO * FIELDS
    kk = 2 * (kw + kh)
    shape = jax.ShapeDtypeStruct
    mine, theirs, own_halo, other_halo = call(
        pack_kernel,
        [
            shape(((rows + 1) * kw, LANES), BF16),
            shape(((rows + 1) * kw, LANES), BF16),
            shape((rows * kh + kw, LANES), BF16),
            shape((rows * kh + kw, LANES), BF16),
        ],
        (fields,),
        [pltpu.VMEM((rows * kw, LANES), F32)] * 2,
        name="pack",
    )
    swap_pairs = [(i, i ^ 1) for i in range(slabs)]
    odd, even = range(1, slabs, 2), range(0, slabs, 2)
    diagonal_pairs = [(i, i + 1) for i in odd if i + 1 < slabs] + [(i, i - 1) for i in even if i]
    straight_pairs = [(i, i + 2) for i in odd if i + 2 < slabs] + [(i, i - 2) for i in even if i]
    swap = lax.ppermute(theirs, "depth", swap_pairs)
    diagonal = lax.ppermute(other_halo, "depth", diagonal_pairs)
    straight = lax.ppermute(own_halo, "depth", straight_pairs)

    table = jnp.zeros((hidden + 8, LANES), F32)
    table = table.at[:hidden, :12].set(w_in).at[:hidden, 12].set(b_in)
    table = table.at[hidden : hidden + 4, :hidden].set(w_out).at[hidden : hidden + 4, hidden].set(b_out)
    width = 256
    outs = FIELDS * layers
    w1, w2a, w2b, bias2 = call(
        functools.partial(weights_kernel, layers=layers, hidden=hidden, slabs=slabs),
        [
            shape((2 * layers * hidden, 3 * width), BF16),
            shape((2 * outs, layers * hidden), BF16),
            shape((outs, layers * hidden), BF16),
            shape((outs, 2 * LANES), F32),
        ],
        (table,),
        flops=10**8,
        name="weights",
    )
    message = shape((HALO * kk + 4 * 32, LANES), BF16)
    first, second = call(band_kernel, [message, message], (mine, swap, straight, diagonal), name="band")
    within = [(i, i ^ 1) for i in range(bands)]
    across = [(i, i + 1) for i in range(1, bands - 1, 2)] + [(i + 1, i) for i in range(1, bands - 1, 2)]
    second = lax.ppermute(second, "row", across)
    first = lax.ppermute(first, "row", within)
    current = call(
        functools.partial(shade_kernel, layers=layers, rows=rows),
        shape((4, rows, LANES), F32),
        (mine, swap, straight, diagonal, first, second, w1, w2a, w2b, bias2),
        [
            pltpu.VMEM((rows + 2 * HALO, kk, LANES), F32),
            pltpu.VMEM((3, kk, LANES), F32),
            pltpu.VMEM((rows, width, LANES), BF16),
            pltpu.VMEM((rows, width, LANES), BF16),
        ],
        flops=10**10,
        name="shade",
    )
    step = 2
    while step < slabs:
        received = lax.ppermute(current, "depth", [(i, i ^ step) for i in range(slabs)])
        behind = (me & step) != 0
        current = combine(jnp.where(behind, received, current), jnp.where(behind, current, received))
        step *= 2
    current = jnp.concatenate([current[0:3], 1.0 - current[3:4]], 0)
    other = lax.ppermute(current, "depth", swap_pairs)
    first_half = jnp.where(side == 0, current, other)
    second_half = jnp.where(side == 0, other, current)
    return jnp.concatenate([first_half, second_half], 2)


def solution(mesh):
    return jax.shard_map(
        local,
        mesh=mesh,
        in_specs=(P(None, "depth", "row", None), P(), P(), P(), P()),
        out_specs=P(None, "row", None),
        check_vma=False,
    )
```

```python
import functools

import jax
import jax.numpy as jnp
from jax import lax
from jax.experimental import pallas as pl
from jax.experimental.pallas import tpu as pltpu
from jax.sharding import PartitionSpec as P

FIELDS = 4
HALO = 6
LANES = 128
HIGHEST = lax.Precision.HIGHEST
F32 = jnp.float32
BF16 = jnp.bfloat16
depth_scale = 2.0
smooth_counts = (20.0, 15.0, 6.0, 1.0)
slope_counts = ((1, 45.0), (2, -9.0), (3, 1.0))


def dot(a, b, precision=None):
    return jnp.dot(a, b, preferred_element_type=F32, precision=precision)


def iota(shape, dim):
    return lax.broadcasted_iota(jnp.int32, shape, dim)


def smooth_count(distance):
    d = jnp.abs(distance)
    out = jnp.where(d == 0, smooth_counts[0], 0.0)
    for place in (1, 2, 3):
        out = jnp.where(d == place, smooth_counts[place], out)
    return out.astype(F32)


def split(x):
    high = x.astype(BF16)
    return high, (x - high.astype(F32)).astype(BF16)


def pack_kernel(fields, mine, theirs, straight, diagonal, left, right):
    side = lax.axis_index("depth") & 1
    layers, rows = fields.shape[1], fields.shape[2]
    kw, kh = layers * FIELDS, HALO * FIELDS
    for layer in range(layers):
        for field in range(FIELDS):
            plane = fields[field, layer].astype(F32)
            place = pl.ds(layer * FIELDS + field, rows, stride=kw)
            left[place, :] = plane[:, :LANES]
            right[place, :] = plane[:, LANES:]
    lane = iota((kw, LANES), 1)
    shift = pl.multiple_of(side * (kw - kh), 8)

    def halves(row, start, count):
        a = left[pl.ds(row * kw + start, count), :]
        b = right[pl.ds(row * kw + start, count), :]
        return jnp.where(side == 0, a, b), jnp.where(side == 0, b, a)

    extra_low = jnp.zeros((kw, LANES), F32)
    extra_high = jnp.zeros((kw, LANES), F32)
    for row in range(0, rows, 2):
        pairs = []
        for r in (row, row + 1):
            a = left[pl.ds(r * kw, kw), :]
            b = right[pl.ds(r * kw, kw), :]
            inside = (lane >= 3 * r) & (lane < 3 * r + 3)
            extra_low = jnp.where(inside, pltpu.roll(b, (3 * r) % LANES, 1), extra_low)
            extra_high = jnp.where(inside, pltpu.roll(a, (3 * r + 3) % LANES, 1), extra_high)
            own = jnp.where(side == 0, a, b)
            other = jnp.where(side == 0, b, a)
            mine[pl.ds(r * kw, kw), :] = own.astype(BF16)
            theirs[pl.ds(r * kw, kw), :] = other.astype(BF16)
            pairs.append(halves(r, shift, kh))
        both = pl.ds(row * kh, 2 * kh)
        straight[both, :] = jnp.concatenate([pairs[0][0], pairs[1][0]], 0).astype(BF16)
        diagonal[both, :] = jnp.concatenate([pairs[0][1], pairs[1][1]], 0).astype(BF16)
    own = jnp.where(side == 0, extra_low, extra_high)
    other = jnp.where(side == 0, extra_high, extra_low)
    mine[rows * kw :, :] = own.astype(BF16)
    theirs[rows * kw :, :] = other.astype(BF16)
    empty = jnp.zeros((kw - kh, LANES), F32)
    for source, target in ((own, straight), (other, diagonal)):
        part = jnp.where(side == 0, source[:kh], source[kw - kh :])
        target[rows * kh :, :] = jnp.concatenate([part, empty], 0).astype(BF16)


def band_kernel(mine, swap, straight, diagonal, first, second):
    odd = lax.axis_index("row") & 1
    kw = 8 * FIELDS
    rows = mine.shape[0] // kw - 1
    for out, from_end in ((first, 1 - odd), (second, odd)):
        at, extra = 0, HALO * sum(r.shape[0] // (rows + 1) for r in (mine, swap)) + 2 * HALO * HALO * FIELDS
        for source in (mine, swap, straight, diagonal):
            width = kw if source.shape[0] == (rows + 1) * kw else HALO * FIELDS
            start = pl.multiple_of(from_end * (rows - HALO) * width, 16)
            out[at : at + HALO * width, :] = source[pl.ds(start, HALO * width), :]
            out[extra : extra + 32, :] = source[rows * width : rows * width + 32, :]
            at += HALO * width
            extra += 32


def weights_kernel(w_in, b_in, w_out, b_out, w1, w2, *, layers, hidden, slabs):
    depth = lax.axis_index("depth")
    side = depth & 1
    base = (depth - side) * layers
    total = slabs * layers
    width = w1.shape[2]
    window = (layers + 2 * HALO) * FIELDS
    kinds = w_in.shape[1]
    row, col = iota((kinds, width), 0), iota((kinds, width), 1)
    within = col % (2 * window)
    field = col & 3
    ending = col >= 6 * window
    pick1 = jnp.where(ending, -1, jnp.where(within < window, field, field + 4))
    pick2 = jnp.where(ending | (within >= window), -1, field + 8)
    eye = iota((hidden, hidden), 0) == iota((hidden, hidden), 1)
    bias = jnp.sum(jnp.where(eye, b_in[...], 0.0), axis=1, keepdims=True)
    part1 = dot(w_in[...], (row == pick1).astype(F32), HIGHEST)
    part2 = dot(w_in[...], (row == pick2).astype(F32), HIGHEST)
    kappa = iota((hidden, width), 1)
    part1 = jnp.where(kappa == 6 * window, bias, jnp.where(kappa == 6 * window + 1, bias, part1))
    scale = 1.0 / 64.0**3
    z, place = iota((layers, width), 0), iota((layers, width), 1)
    inner = place % (2 * window)
    slope_kind = inner >= window
    last = place >= 6 * window
    slot = jnp.where(slope_kind, inner - window, inner) >> 2
    low_column = ((place >= 2 * window) & (place < 4 * window)) | (place == 6 * window + 1)
    for half in range(2):
        distance = slot - HALO - z
        center = smooth_count(distance) * scale
        slope = jnp.zeros((layers, width), F32)
        for offset, count in slope_counts:
            for sign in (1, -1):
                at = base + half * layers + z + sign * offset
                inside = ((at >= 0) & (at < total)).astype(F32)
                slope = slope + (inside * (sign * count)) * smooth_count(distance - sign * offset)
        center = jnp.where(last, 1.0, jnp.where(slope_kind, center * (1.0 / 60.0), center))
        product = center[None] * part1[:, None, :] + (slope * (scale / 60.0))[None] * part2[:, None, :]
        high = product.astype(BF16).astype(F32)
        chosen = jnp.where(low_column[None], product - high, high)
        w1[half] = chosen.reshape(hidden * layers, width).astype(BF16)
    outs = w_out.shape[0]
    for c in range(outs):
        values = jnp.sum(jnp.where(eye, w_out[c : c + 1, :], 0.0), axis=1, keepdims=True)
        w2[c * hidden : (c + 1) * hidden, :] = jnp.broadcast_to(values, (hidden, LANES))
    pick = iota((8, outs), 0) == iota((8, outs), 1)
    values = jnp.sum(jnp.where(pick, b_out[...], 0.0), axis=1, keepdims=True)
    w2[outs * hidden :, :] = jnp.broadcast_to(values, (8, LANES))


def shade_kernel(mine, swap, straight, diagonal, first, second, w1, w2, out, grid, edge, kept, *, layers, rows):
    side = lax.axis_index("depth") & 1
    band = lax.axis_index("row")
    bands = lax.axis_size("row")
    odd = band & 1
    kw, kh = layers * FIELDS, HALO * FIELDS
    kk = 2 * (kw + kh)
    offsets = (
        (mine, kh + side * kw, kw),
        (swap, kh + (1 - side) * kw, kw),
        (straight, (1 - side) * (kh + 2 * kw), kh),
        (diagonal, side * (kh + 2 * kw), kh),
    )
    i, j = iota((LANES, LANES), 0), iota((LANES, LANES), 1)
    taps = smooth_count(i - j).astype(BF16)
    ir, ic = i // 3, i % 3
    spot = jnp.where(side == 0, (j + 3) & (LANES - 1), j)
    jr, jc = spot // 3, spot % 3
    apart = jnp.where(side == 0, ic - jc + 3, jc - ic + 3)
    border = jnp.where((ir == jr) & (i < 3 * rows) & (spot < 3 * rows), smooth_count(apart), 0.0).astype(BF16)
    for source, at, width in offsets:
        at = pl.ds(pl.multiple_of(at, 8), width)
        filtered = dot(source[0 : rows * width, :], taps)
        grid[HALO : HALO + rows, at, :] = filtered.reshape(rows, width, LANES)
        edge[0, at, :] = dot(source[rows * width : rows * width + 32, :], border)[:width]
    far = HALO + rows
    for source, base, which in ((first, odd, 2 - odd), (second, 1 - odd, 1 + odd)):
        place = (1 - base) * far
        start = 0
        filtered = dot(source[0 : HALO * kk, :], taps)
        edges = dot(source[HALO * kk :, :], border)
        for index, (unused, at, width) in enumerate(offsets):
            at = pl.ds(pl.multiple_of(at, 8), width)
            piece = filtered[start : start + HALO * width].reshape(HALO, width, LANES)
            grid[pl.ds(place, HALO), at, :] = piece
            edge[which, at, :] = edges[index * 32 : index * 32 + width]
            start += HALO * width
    lane = iota((16, LANES), 1)
    near = ((lane + jnp.where(side == 0, 3, 0)) & (LANES - 1)) < 3
    above = (band > 0).astype(F32)
    below = (band < bands - 1).astype(F32)

    def filter_rows(group, carry):
        at = pl.ds(pl.multiple_of(group * 16, 16), 16)
        edges = [edge[k, at, :] for k in range(3)]
        chain = [None] * 6
        ring = []
        for r in range(rows + 2 * HALO):
            which = 1 if r < HALO else 0 if r < HALO + rows else 2
            own_row = (r - HALO) % rows
            turned = pltpu.roll(edges[which], (-3 * own_row) % LANES, 1)
            value = grid[r, at, :] + jnp.where(near, turned, 0.0)
            for level in range(6):
                previous, chain[level] = chain[level], value
                if previous is None:
                    value = None
                    break
                value = previous + value
            if value is None:
                continue
            y = r - HALO - 3
            if y < 0:
                value = value * above
            elif y >= rows:
                value = value * below
            ring.append(value)
            if len(ring) == 7:
                slope = (ring[6] - ring[0]) - 9.0 * (ring[5] - ring[1]) + 45.0 * (ring[4] - ring[2])
                y -= 3
                kept[0, y, at, :], kept[2, y, at, :] = split(ring[3])
                kept[1, y, at, :], kept[3, y, at, :] = split(slope)
                ring.pop(0)
        return carry

    lax.fori_loop(0, kk // 16, filter_rows, 0)
    wide = 2 * LANES
    window = kw + 2 * kh
    hidden = w1.shape[1] // layers
    rest = w1.shape[2] - 6 * window
    ones = jnp.where(iota((rest, wide), 0) < 2, 1.0, 0.0).astype(BF16)
    sub = iota((layers, wide), 0)
    scale = depth_scale / (lax.axis_size("depth") * layers)

    def splat(index):
        line = w2[index : index + 1, :]
        return jnp.broadcast_to(jnp.concatenate([line, line], 1), (layers, wide))

    def shade(pair, carry):
        y = 2 * pair
        total = jnp.zeros((1, wide), F32)
        front = jnp.ones((1, wide), F32)
        color = [jnp.zeros((layers, wide), F32) for unused in range(3)]
        for half in range(2):
            at = pl.ds(half * kw, window)
            c_high, s_high, c_low, s_low = [
                jnp.concatenate([kept[k, y, at, :], kept[k, y + 1, at, :]], 1) for k in range(4)
            ]
            stacked = jnp.concatenate([c_high, s_high, c_high, s_high, c_low, s_low, ones], 0)
            units = jnp.tanh(dot(w1[half], stacked))
            o = [splat(4 * hidden + c) for c in range(4)]
            for h in range(hidden):
                unit = units[h * layers : (h + 1) * layers]
                for c in range(4):
                    o[c] = o[c] + splat(c * hidden + h) * unit
            x = o[3]
            optical = (jnp.maximum(x, 0.0) + jnp.log1p(jnp.exp(-jnp.abs(x)))) * scale
            through = optical
            for step in (1, 2, 4):
                through = through + jnp.where(sub >= step, pltpu.roll(through, step, 0), 0.0)
            through = through + total
            total = through[layers - 1 :]
            after = jnp.exp(-through)
            before = jnp.where(sub == 0, front, pltpu.roll(after, 1, 0))
            front = after[layers - 1 :]
            weight = before - after
            for c in range(3):
                color[c] = color[c] + weight / (1.0 + jnp.exp(-o[c]))
        for c in range(3):
            line = jnp.sum(color[c], axis=0, keepdims=True)
            out[c, pl.ds(y, 1), :] = line[:, :LANES]
            out[c, pl.ds(y + 1, 1), :] = line[:, LANES:]
        out[3, pl.ds(y, 1), :] = front[:, :LANES]
        out[3, pl.ds(y + 1, 1), :] = front[:, LANES:]
        return carry

    lax.fori_loop(0, rows // 2, shade, 0)


def call(kernel, out_shape, operands, scratch=(), flops=0, name=None):
    vmem = pl.BlockSpec(memory_space=pltpu.VMEM)
    return pl.pallas_call(
        kernel,
        out_shape=out_shape,
        in_specs=[vmem] * len(operands),
        out_specs=jax.tree.map(lambda unused: vmem, out_shape),
        scratch_shapes=list(scratch),
        compiler_params=pltpu.CompilerParams(vmem_limit_bytes=40 * 2**20),
        cost_estimate=pl.CostEstimate(flops=flops, bytes_accessed=2**20, transcendentals=0),
        name=name,
    )(*operands)


def combine(front, back):
    color = front[0:3] + front[3:4] * back[0:3]
    return jnp.concatenate([color, front[3:4] * back[3:4]], 0)


def local(fields, w_in, b_in, w_out, b_out):
    layers, rows, columns = fields.shape[1:]
    hidden = w_in.shape[0]
    slabs = lax.axis_size("depth")
    bands = lax.axis_size("row")
    me = lax.axis_index("depth")
    side = me & 1
    kw, kh = layers * FIELDS, HALO * FIELDS
    kk = 2 * (kw + kh)
    shape = jax.ShapeDtypeStruct
    mine, theirs, own_halo, other_halo = call(
        pack_kernel,
        [
            shape(((rows + 1) * kw, LANES), BF16),
            shape(((rows + 1) * kw, LANES), BF16),
            shape((rows * kh + kw, LANES), BF16),
            shape((rows * kh + kw, LANES), BF16),
        ],
        (fields,),
        [pltpu.VMEM((rows * kw, LANES), F32)] * 2,
        name="pack",
    )
    swap_pairs = [(i, i ^ 1) for i in range(slabs)]
    odd, even = range(1, slabs, 2), range(0, slabs, 2)
    diagonal_pairs = [(i, i + 1) for i in odd if i + 1 < slabs] + [(i, i - 1) for i in even if i]
    straight_pairs = [(i, i + 2) for i in odd if i + 2 < slabs] + [(i, i - 2) for i in even if i]
    swap = lax.ppermute(theirs, "depth", swap_pairs)
    diagonal = lax.ppermute(other_halo, "depth", diagonal_pairs)
    straight = lax.ppermute(own_halo, "depth", straight_pairs)

    width = -(-(6 * (kw + 2 * kh) + 2) // 256) * 256
    w1, w2 = call(
        functools.partial(weights_kernel, layers=layers, hidden=hidden, slabs=slabs),
        [shape((2, layers * hidden, width), BF16), shape((4 * hidden + 8, LANES), F32)],
        (w_in, b_in[None], w_out, b_out[None]),
        flops=10**8,
        name="weights",
    )
    message = shape((HALO * kk + 4 * 32, LANES), BF16)
    first, second = call(band_kernel, [message, message], (mine, swap, straight, diagonal), name="band")
    within = [(i, i ^ 1) for i in range(bands)]
    across = [(i, i + 1) for i in range(1, bands - 1, 2)] + [(i + 1, i) for i in range(1, bands - 1, 2)]
    second = lax.ppermute(second, "row", across)
    first = lax.ppermute(first, "row", within)
    current = call(
        functools.partial(shade_kernel, layers=layers, rows=rows),
        shape((4, rows, LANES), F32),
        (mine, swap, straight, diagonal, first, second, w1, w2),
        [
            pltpu.VMEM((rows + 2 * HALO, kk, LANES), F32),
            pltpu.VMEM((3, kk, LANES), F32),
            pltpu.VMEM((4, rows, kk, LANES), BF16),
        ],
        flops=10**10,
        name="shade",
    )
    step = 2
    while step < slabs:
        received = lax.ppermute(current, "depth", [(i, i ^ step) for i in range(slabs)])
        behind = (me & step) != 0
        current = combine(jnp.where(behind, received, current), jnp.where(behind, current, received))
        step *= 2
    current = jnp.concatenate([current[0:3], 1.0 - current[3:4]], 0)
    other = lax.ppermute(current, "depth", swap_pairs)
    first_half = jnp.where(side == 0, current, other)
    second_half = jnp.where(side == 0, other, current)
    return jnp.concatenate([first_half, second_half], 2)


def solution(mesh):
    return jax.shard_map(
        local,
        mesh=mesh,
        in_specs=(P(None, "depth", "row", None), P(), P(), P(), P()),
        out_specs=P(None, "row", None),
        check_vma=False,
    )
```

```python
import functools

import jax
import jax.numpy as jnp
from jax import lax
from jax.experimental import pallas as pl
from jax.experimental.pallas import tpu as pltpu
from jax.sharding import PartitionSpec as P

FIELDS = 4
HALO = 6
LANES = 128
HIGHEST = lax.Precision.HIGHEST
F32 = jnp.float32
BF16 = jnp.bfloat16
depth_scale = 2.0
smooth_counts = (20.0, 15.0, 6.0, 1.0)
slope_counts = ((1, 45.0), (2, -9.0), (3, 1.0))


def dot(a, b, precision=None):
    return jnp.dot(a, b, preferred_element_type=F32, precision=precision)


def iota(shape, dim):
    return lax.broadcasted_iota(jnp.int32, shape, dim)


def smooth_count(distance):
    d = jnp.abs(distance)
    out = jnp.where(d == 0, smooth_counts[0], 0.0)
    for place in (1, 2, 3):
        out = jnp.where(d == place, smooth_counts[place], out)
    return out.astype(F32)


def split(x):
    high = x.astype(BF16)
    return high, (x - high.astype(F32)).astype(BF16)


def pack_kernel(fields, mine, theirs, straight, diagonal, left, right):
    side = lax.axis_index("depth") & 1
    layers, rows = fields.shape[1], fields.shape[2]
    kw, kh = layers * FIELDS, HALO * FIELDS
    for layer in range(layers):
        for field in range(FIELDS):
            plane = fields[field, layer].astype(F32)
            place = pl.ds(layer * FIELDS + field, rows, stride=kw)
            left[place, :] = plane[:, :LANES]
            right[place, :] = plane[:, LANES:]
    lane = iota((kw, LANES), 1)
    shift = pl.multiple_of(side * (kw - kh), 8)

    def halves(row, start, count):
        a = left[pl.ds(row * kw + start, count), :]
        b = right[pl.ds(row * kw + start, count), :]
        return jnp.where(side == 0, a, b), jnp.where(side == 0, b, a)

    extra_low = jnp.zeros((kw, LANES), F32)
    extra_high = jnp.zeros((kw, LANES), F32)
    for row in range(0, rows, 2):
        pairs = []
        for r in (row, row + 1):
            a = left[pl.ds(r * kw, kw), :]
            b = right[pl.ds(r * kw, kw), :]
            inside = (lane >= 3 * r) & (lane < 3 * r + 3)
            extra_low = jnp.where(inside, pltpu.roll(b, (3 * r) % LANES, 1), extra_low)
            extra_high = jnp.where(inside, pltpu.roll(a, (3 * r + 3) % LANES, 1), extra_high)
            own = jnp.where(side == 0, a, b)
            other = jnp.where(side == 0, b, a)
            mine[pl.ds(r * kw, kw), :] = own.astype(BF16)
            theirs[pl.ds(r * kw, kw), :] = other.astype(BF16)
            pairs.append(halves(r, shift, kh))
        both = pl.ds(row * kh, 2 * kh)
        straight[both, :] = jnp.concatenate([pairs[0][0], pairs[1][0]], 0).astype(BF16)
        diagonal[both, :] = jnp.concatenate([pairs[0][1], pairs[1][1]], 0).astype(BF16)
    own = jnp.where(side == 0, extra_low, extra_high)
    other = jnp.where(side == 0, extra_high, extra_low)
    mine[rows * kw :, :] = own.astype(BF16)
    theirs[rows * kw :, :] = other.astype(BF16)
    empty = jnp.zeros((kw - kh, LANES), F32)
    for source, target in ((own, straight), (other, diagonal)):
        part = jnp.where(side == 0, source[:kh], source[kw - kh :])
        target[rows * kh :, :] = jnp.concatenate([part, empty], 0).astype(BF16)


def band_kernel(mine, swap, straight, diagonal, first, second):
    odd = lax.axis_index("row") & 1
    kw = 8 * FIELDS
    rows = mine.shape[0] // kw - 1
    for out, from_end in ((first, 1 - odd), (second, odd)):
        at, extra = 0, HALO * sum(r.shape[0] // (rows + 1) for r in (mine, swap)) + 2 * HALO * HALO * FIELDS
        for source in (mine, swap, straight, diagonal):
            width = kw if source.shape[0] == (rows + 1) * kw else HALO * FIELDS
            start = pl.multiple_of(from_end * (rows - HALO) * width, 16)
            out[at : at + HALO * width, :] = source[pl.ds(start, HALO * width), :]
            out[extra : extra + 32, :] = source[rows * width : rows * width + 32, :]
            at += HALO * width
            extra += 32


def weights_kernel(w_in, b_in, w_out, b_out, w1, w2, *, layers, hidden, slabs):
    depth = lax.axis_index("depth")
    side = depth & 1
    base = (depth - side) * layers
    total = slabs * layers
    width = w1.shape[2]
    window = (layers + 2 * HALO) * FIELDS
    kinds = w_in.shape[1]
    row, col = iota((kinds, width), 0), iota((kinds, width), 1)
    within = col % (2 * window)
    field = col & 3
    ending = col >= 6 * window
    pick1 = jnp.where(ending, -1, jnp.where(within < window, field, field + 4))
    pick2 = jnp.where(ending | (within >= window), -1, field + 8)
    eye = iota((hidden, hidden), 0) == iota((hidden, hidden), 1)
    bias = jnp.sum(jnp.where(eye, b_in[...], 0.0), axis=1, keepdims=True)
    part1 = dot(w_in[...], (row == pick1).astype(F32), HIGHEST)
    part2 = dot(w_in[...], (row == pick2).astype(F32), HIGHEST)
    kappa = iota((hidden, width), 1)
    part1 = jnp.where(kappa == 6 * window, bias, jnp.where(kappa == 6 * window + 1, bias, part1))
    scale = 1.0 / 64.0**3
    z, place = iota((layers, width), 0), iota((layers, width), 1)
    inner = place % (2 * window)
    slope_kind = inner >= window
    last = place >= 6 * window
    slot = jnp.where(slope_kind, inner - window, inner) >> 2
    low_column = ((place >= 2 * window) & (place < 4 * window)) | (place == 6 * window + 1)
    for half in range(2):
        distance = slot - HALO - z
        center = smooth_count(distance) * scale
        slope = jnp.zeros((layers, width), F32)
        for offset, count in slope_counts:
            for sign in (1, -1):
                at = base + half * layers + z + sign * offset
                inside = ((at >= 0) & (at < total)).astype(F32)
                slope = slope + (inside * (sign * count)) * smooth_count(distance - sign * offset)
        center = jnp.where(last, 1.0, jnp.where(slope_kind, center * (1.0 / 60.0), center))
        product = center[None] * part1[:, None, :] + (slope * (scale / 60.0))[None] * part2[:, None, :]
        high = product.astype(BF16).astype(F32)
        chosen = jnp.where(low_column[None], product - high, high)
        w1[half] = chosen.reshape(hidden * layers, width).astype(BF16)
    outs = w_out.shape[0]
    for c in range(outs):
        values = jnp.sum(jnp.where(eye, w_out[c : c + 1, :], 0.0), axis=1, keepdims=True)
        w2[c * hidden : (c + 1) * hidden, :] = jnp.broadcast_to(values, (hidden, LANES))
    pick = iota((8, outs), 0) == iota((8, outs), 1)
    values = jnp.sum(jnp.where(pick, b_out[...], 0.0), axis=1, keepdims=True)
    w2[outs * hidden :, :] = jnp.broadcast_to(values, (8, LANES))


def shade_kernel(mine, swap, straight, diagonal, first, second, w1, w2, out, grid, edge, kept, *, layers, rows):
    side = lax.axis_index("depth") & 1
    band = lax.axis_index("row")
    bands = lax.axis_size("row")
    odd = band & 1
    kw, kh = layers * FIELDS, HALO * FIELDS
    kk = 2 * (kw + kh)
    offsets = (
        (mine, kh + side * kw, kw),
        (swap, kh + (1 - side) * kw, kw),
        (straight, (1 - side) * (kh + 2 * kw), kh),
        (diagonal, side * (kh + 2 * kw), kh),
    )
    i, j = iota((LANES, LANES), 0), iota((LANES, LANES), 1)
    taps = smooth_count(i - j).astype(BF16)
    ir, ic = i // 3, i % 3
    spot = jnp.where(side == 0, (j + 3) & (LANES - 1), j)
    jr, jc = spot // 3, spot % 3
    apart = jnp.where(side == 0, ic - jc + 3, jc - ic + 3)
    border = jnp.where((ir == jr) & (i < 3 * rows) & (spot < 3 * rows), smooth_count(apart), 0.0).astype(BF16)
    for source, at, width in offsets:
        at = pl.ds(pl.multiple_of(at, 8), width)
        filtered = dot(source[0 : rows * width, :], taps)
        grid[HALO : HALO + rows, at, :] = filtered.reshape(rows, width, LANES)
        edge[0, at, :] = dot(source[rows * width : rows * width + 32, :], border)[:width]
    far = HALO + rows
    for source, base, which in ((first, odd, 2 - odd), (second, 1 - odd, 1 + odd)):
        place = (1 - base) * far
        start = 0
        filtered = dot(source[0 : HALO * kk, :], taps)
        edges = dot(source[HALO * kk :, :], border)
        for index, (unused, at, width) in enumerate(offsets):
            at = pl.ds(pl.multiple_of(at, 8), width)
            piece = filtered[start : start + HALO * width].reshape(HALO, width, LANES)
            grid[pl.ds(place, HALO), at, :] = piece
            edge[which, at, :] = edges[index * 32 : index * 32 + width]
            start += HALO * width
    lane = iota((16, LANES), 1)
    near = ((lane + jnp.where(side == 0, 3, 0)) & (LANES - 1)) < 3
    above = (band > 0).astype(F32)
    below = (band < bands - 1).astype(F32)

    def filter_rows(group, carry):
        at = pl.ds(pl.multiple_of(group * 16, 16), 16)
        edges = [edge[k, at, :] for k in range(3)]
        chain = [None] * 6
        ring = []
        for r in range(rows + 2 * HALO):
            which = 1 if r < HALO else 0 if r < HALO + rows else 2
            own_row = (r - HALO) % rows
            turned = pltpu.roll(edges[which], (-3 * own_row) % LANES, 1)
            value = grid[r, at, :] + jnp.where(near, turned, 0.0)
            for level in range(6):
                previous, chain[level] = chain[level], value
                if previous is None:
                    value = None
                    break
                value = previous + value
            if value is None:
                continue
            y = r - HALO - 3
            if y < 0:
                value = value * above
            elif y >= rows:
                value = value * below
            ring.append(value)
            if len(ring) == 7:
                slope = (ring[6] - ring[0]) - 9.0 * (ring[5] - ring[1]) + 45.0 * (ring[4] - ring[2])
                y -= 3
                kept[0, y, at, :], kept[2, y, at, :] = split(ring[3])
                kept[1, y, at, :], kept[3, y, at, :] = split(slope)
                ring.pop(0)
        return carry

    lax.fori_loop(0, kk // 16, filter_rows, 0, unroll=kk // 16)
    wide = 2 * LANES
    window = kw + 2 * kh
    hidden = w1.shape[1] // layers
    rest = w1.shape[2] - 6 * window
    ones = jnp.where(iota((rest, wide), 0) < 2, 1.0, 0.0).astype(BF16)
    sub = iota((layers, wide), 0)
    scale = depth_scale / (lax.axis_size("depth") * layers)

    def splat(index):
        line = w2[index : index + 1, :]
        return jnp.broadcast_to(jnp.concatenate([line, line], 1), (layers, wide))

    def shade(pair, carry):
        y = 2 * pair
        total = jnp.zeros((1, wide), F32)
        front = jnp.ones((1, wide), F32)
        color = [jnp.zeros((layers, wide), F32) for unused in range(3)]
        for half in range(2):
            at = pl.ds(half * kw, window)
            c_high, s_high, c_low, s_low = [
                jnp.concatenate([kept[k, y, at, :], kept[k, y + 1, at, :]], 1) for k in range(4)
            ]
            stacked = jnp.concatenate([c_high, s_high, c_high, s_high, c_low, s_low, ones], 0)
            units = jnp.tanh(dot(w1[half], stacked))
            o = [splat(4 * hidden + c) for c in range(4)]
            for h in range(hidden):
                unit = units[h * layers : (h + 1) * layers]
                for c in range(4):
                    o[c] = o[c] + splat(c * hidden + h) * unit
            x = o[3]
            optical = (jnp.maximum(x, 0.0) + jnp.log1p(jnp.exp(-jnp.abs(x)))) * scale
            through = optical
            for step in (1, 2, 4):
                through = through + jnp.where(sub >= step, pltpu.roll(through, step, 0), 0.0)
            through = through + total
            total = through[layers - 1 :]
            after = jnp.exp(-through)
            before = jnp.where(sub == 0, front, pltpu.roll(after, 1, 0))
            front = after[layers - 1 :]
            weight = before - after
            for c in range(3):
                color[c] = color[c] + weight / (1.0 + jnp.exp(-o[c]))
        for c in range(3):
            line = jnp.sum(color[c], axis=0, keepdims=True)
            out[c, pl.ds(y, 1), :] = line[:, :LANES]
            out[c, pl.ds(y + 1, 1), :] = line[:, LANES:]
        out[3, pl.ds(y, 1), :] = front[:, :LANES]
        out[3, pl.ds(y + 1, 1), :] = front[:, LANES:]
        return carry

    lax.fori_loop(0, rows // 2, shade, 0, unroll=8)


def call(kernel, out_shape, operands, scratch=(), flops=0, name=None):
    vmem = pl.BlockSpec(memory_space=pltpu.VMEM)
    return pl.pallas_call(
        kernel,
        out_shape=out_shape,
        in_specs=[vmem] * len(operands),
        out_specs=jax.tree.map(lambda unused: vmem, out_shape),
        scratch_shapes=list(scratch),
        compiler_params=pltpu.CompilerParams(vmem_limit_bytes=40 * 2**20),
        cost_estimate=pl.CostEstimate(flops=flops, bytes_accessed=2**20, transcendentals=0),
        name=name,
    )(*operands)


def combine(front, back):
    color = front[0:3] + front[3:4] * back[0:3]
    return jnp.concatenate([color, front[3:4] * back[3:4]], 0)


def local(fields, w_in, b_in, w_out, b_out):
    layers, rows, columns = fields.shape[1:]
    hidden = w_in.shape[0]
    slabs = lax.axis_size("depth")
    bands = lax.axis_size("row")
    me = lax.axis_index("depth")
    side = me & 1
    kw, kh = layers * FIELDS, HALO * FIELDS
    kk = 2 * (kw + kh)
    shape = jax.ShapeDtypeStruct
    mine, theirs, own_halo, other_halo = call(
        pack_kernel,
        [
            shape(((rows + 1) * kw, LANES), BF16),
            shape(((rows + 1) * kw, LANES), BF16),
            shape((rows * kh + kw, LANES), BF16),
            shape((rows * kh + kw, LANES), BF16),
        ],
        (fields,),
        [pltpu.VMEM((rows * kw, LANES), F32)] * 2,
        name="pack",
    )
    swap_pairs = [(i, i ^ 1) for i in range(slabs)]
    odd, even = range(1, slabs, 2), range(0, slabs, 2)
    diagonal_pairs = [(i, i + 1) for i in odd if i + 1 < slabs] + [(i, i - 1) for i in even if i]
    straight_pairs = [(i, i + 2) for i in odd if i + 2 < slabs] + [(i, i - 2) for i in even if i]
    swap = lax.ppermute(theirs, "depth", swap_pairs)
    diagonal = lax.ppermute(other_halo, "depth", diagonal_pairs)
    straight = lax.ppermute(own_halo, "depth", straight_pairs)

    width = -(-(6 * (kw + 2 * kh) + 2) // 256) * 256
    w1, w2 = call(
        functools.partial(weights_kernel, layers=layers, hidden=hidden, slabs=slabs),
        [shape((2, layers * hidden, width), BF16), shape((4 * hidden + 8, LANES), F32)],
        (w_in, b_in[None], w_out, b_out[None]),
        flops=10**8,
        name="weights",
    )
    message = shape((HALO * kk + 4 * 32, LANES), BF16)
    first, second = call(band_kernel, [message, message], (mine, swap, straight, diagonal), name="band")
    within = [(i, i ^ 1) for i in range(bands)]
    across = [(i, i + 1) for i in range(1, bands - 1, 2)] + [(i + 1, i) for i in range(1, bands - 1, 2)]
    second = lax.ppermute(second, "row", across)
    first = lax.ppermute(first, "row", within)
    current = call(
        functools.partial(shade_kernel, layers=layers, rows=rows),
        shape((4, rows, LANES), F32),
        (mine, swap, straight, diagonal, first, second, w1, w2),
        [
            pltpu.VMEM((rows + 2 * HALO, kk, LANES), F32),
            pltpu.VMEM((3, kk, LANES), F32),
            pltpu.VMEM((4, rows, kk, LANES), BF16),
        ],
        flops=10**10,
        name="shade",
    )
    step = 2
    while step < slabs:
        received = lax.ppermute(current, "depth", [(i, i ^ step) for i in range(slabs)])
        behind = (me & step) != 0
        current = combine(jnp.where(behind, received, current), jnp.where(behind, current, received))
        step *= 2
    current = jnp.concatenate([current[0:3], 1.0 - current[3:4]], 0)
    other = lax.ppermute(current, "depth", swap_pairs)
    first_half = jnp.where(side == 0, current, other)
    second_half = jnp.where(side == 0, other, current)
    return jnp.concatenate([first_half, second_half], 2)


def solution(mesh):
    return jax.shard_map(
        local,
        mesh=mesh,
        in_specs=(P(None, "depth", "row", None), P(), P(), P(), P()),
        out_specs=P(None, "row", None),
        check_vma=False,
    )
```

```python
import functools

import jax
import jax.numpy as jnp
from jax import lax
from jax.experimental import pallas as pl
from jax.experimental.pallas import tpu as pltpu
from jax.sharding import PartitionSpec as P

FIELDS = 4
HALO = 6
LANES = 128
HIGHEST = lax.Precision.HIGHEST
F32 = jnp.float32
BF16 = jnp.bfloat16
depth_scale = 2.0
smooth_counts = (20.0, 15.0, 6.0, 1.0)
slope_counts = ((1, 45.0), (2, -9.0), (3, 1.0))


def dot(a, b, precision=None):
    return jnp.dot(a, b, preferred_element_type=F32, precision=precision)


def iota(shape, dim):
    return lax.broadcasted_iota(jnp.int32, shape, dim)


def smooth_count(distance):
    d = jnp.abs(distance)
    out = jnp.where(d == 0, smooth_counts[0], 0.0)
    for place in (1, 2, 3):
        out = jnp.where(d == place, smooth_counts[place], out)
    return out.astype(F32)


def split(x):
    high = x.astype(BF16)
    return high, (x - high.astype(F32)).astype(BF16)


def pack_kernel(fields, mine, theirs, straight, diagonal, left, right):
    side = lax.axis_index("depth") & 1
    layers, rows = fields.shape[1], fields.shape[2]
    kw, kh = layers * FIELDS, HALO * FIELDS
    for layer in range(layers):
        for field in range(FIELDS):
            plane = fields[field, layer].astype(F32)
            place = pl.ds(layer * FIELDS + field, rows, stride=kw)
            left[place, :] = plane[:, :LANES]
            right[place, :] = plane[:, LANES:]
    lane = iota((kw, LANES), 1)
    shift = pl.multiple_of(side * (kw - kh), 8)

    def halves(row, start, count):
        a = left[pl.ds(row * kw + start, count), :]
        b = right[pl.ds(row * kw + start, count), :]
        return jnp.where(side == 0, a, b), jnp.where(side == 0, b, a)

    extra_low = jnp.zeros((kw, LANES), F32)
    extra_high = jnp.zeros((kw, LANES), F32)
    for row in range(0, rows, 2):
        pairs = []
        for r in (row, row + 1):
            a = left[pl.ds(r * kw, kw), :]
            b = right[pl.ds(r * kw, kw), :]
            inside = (lane >= 3 * r) & (lane < 3 * r + 3)
            extra_low = jnp.where(inside, pltpu.roll(b, (3 * r) % LANES, 1), extra_low)
            extra_high = jnp.where(inside, pltpu.roll(a, (3 * r + 3) % LANES, 1), extra_high)
            own = jnp.where(side == 0, a, b)
            other = jnp.where(side == 0, b, a)
            mine[pl.ds(r * kw, kw), :] = own.astype(BF16)
            theirs[pl.ds(r * kw, kw), :] = other.astype(BF16)
            pairs.append(halves(r, shift, kh))
        both = pl.ds(row * kh, 2 * kh)
        straight[both, :] = jnp.concatenate([pairs[0][0], pairs[1][0]], 0).astype(BF16)
        diagonal[both, :] = jnp.concatenate([pairs[0][1], pairs[1][1]], 0).astype(BF16)
    own = jnp.where(side == 0, extra_low, extra_high)
    other = jnp.where(side == 0, extra_high, extra_low)
    mine[rows * kw :, :] = own.astype(BF16)
    theirs[rows * kw :, :] = other.astype(BF16)
    empty = jnp.zeros((kw - kh, LANES), F32)
    for source, target in ((own, straight), (other, diagonal)):
        part = jnp.where(side == 0, source[:kh], source[kw - kh :])
        target[rows * kh :, :] = jnp.concatenate([part, empty], 0).astype(BF16)


def band_kernel(mine, swap, straight, diagonal, first, second):
    odd = lax.axis_index("row") & 1
    kw = 8 * FIELDS
    rows = mine.shape[0] // kw - 1
    for out, from_end in ((first, 1 - odd), (second, odd)):
        at, extra = 0, HALO * sum(r.shape[0] // (rows + 1) for r in (mine, swap)) + 2 * HALO * HALO * FIELDS
        for source in (mine, swap, straight, diagonal):
            width = kw if source.shape[0] == (rows + 1) * kw else HALO * FIELDS
            start = pl.multiple_of(from_end * (rows - HALO) * width, 16)
            out[at : at + HALO * width, :] = source[pl.ds(start, HALO * width), :]
            out[extra : extra + 32, :] = source[rows * width : rows * width + 32, :]
            at += HALO * width
            extra += 32


def weights_kernel(w_in, b_in, w_out, b_out, w1, w2, *, layers, hidden, slabs):
    depth = lax.axis_index("depth")
    side = depth & 1
    base = (depth - side) * layers
    total = slabs * layers
    width = w1.shape[2]
    window = (layers + 2 * HALO) * FIELDS
    kinds = w_in.shape[1]
    row, col = iota((kinds, width), 0), iota((kinds, width), 1)
    within = col % (2 * window)
    field = col & 3
    ending = col >= 6 * window
    pick1 = jnp.where(ending, -1, jnp.where(within < window, field, field + 4))
    pick2 = jnp.where(ending | (within >= window), -1, field + 8)
    eye = iota((hidden, hidden), 0) == iota((hidden, hidden), 1)
    bias = jnp.sum(jnp.where(eye, b_in[...], 0.0), axis=1, keepdims=True)
    part1 = dot(w_in[...], (row == pick1).astype(F32), HIGHEST)
    part2 = dot(w_in[...], (row == pick2).astype(F32), HIGHEST)
    kappa = iota((hidden, width), 1)
    part1 = jnp.where(kappa == 6 * window, bias, jnp.where(kappa == 6 * window + 1, bias, part1))
    scale = 1.0 / 64.0**3
    z, place = iota((layers, width), 0), iota((layers, width), 1)
    inner = place % (2 * window)
    slope_kind = inner >= window
    last = place >= 6 * window
    slot = jnp.where(slope_kind, inner - window, inner) >> 2
    low_column = ((place >= 2 * window) & (place < 4 * window)) | (place == 6 * window + 1)
    for half in range(2):
        distance = slot - HALO - z
        center = smooth_count(distance) * scale
        slope = jnp.zeros((layers, width), F32)
        for offset, count in slope_counts:
            for sign in (1, -1):
                at = base + half * layers + z + sign * offset
                inside = ((at >= 0) & (at < total)).astype(F32)
                slope = slope + (inside * (sign * count)) * smooth_count(distance - sign * offset)
        center = jnp.where(last, 1.0, jnp.where(slope_kind, center * (1.0 / 60.0), center))
        product = center[None] * part1[:, None, :] + (slope * (scale / 60.0))[None] * part2[:, None, :]
        high = product.astype(BF16).astype(F32)
        chosen = jnp.where(low_column[None], product - high, high)
        w1[half] = chosen.reshape(hidden * layers, width).astype(BF16)
    outs = w_out.shape[0]
    for c in range(outs):
        values = jnp.sum(jnp.where(eye, w_out[c : c + 1, :], 0.0), axis=1, keepdims=True)
        w2[c * hidden : (c + 1) * hidden, :] = jnp.broadcast_to(values, (hidden, LANES))
    pick = iota((8, outs), 0) == iota((8, outs), 1)
    values = jnp.sum(jnp.where(pick, b_out[...], 0.0), axis=1, keepdims=True)
    w2[outs * hidden :, :] = jnp.broadcast_to(values, (8, LANES))


def shade_kernel(*refs, layers, rows, own_rows, flip, masked):
    if masked:
        mine, swap, straight, diagonal, halo, w1, w2, done, out, grid, edge, kept = refs
        out[...] = done[...]
    else:
        mine, swap, straight, diagonal, halo, w1, w2, out, grid, edge, kept = refs
    side = lax.axis_index("depth") & 1
    band = lax.axis_index("row")
    top = 1 - (band & 1) if flip else band & 1
    kw, kh = layers * FIELDS, HALO * FIELDS
    kk = 2 * (kw + kh)
    offsets = (
        (mine, kh + side * kw, kw),
        (swap, kh + (1 - side) * kw, kw),
        (straight, (1 - side) * (kh + 2 * kw), kh),
        (diagonal, side * (kh + 2 * kw), kh),
    )
    own_place, halo_place = HALO * top, own_rows * (1 - top)
    own_start, halo_start = (rows - own_rows) * (1 - top), (rows - HALO) * top
    i, j = iota((LANES, LANES), 0), iota((LANES, LANES), 1)
    taps = smooth_count(i - j).astype(BF16)

    def border(shift):
        spot = (j + jnp.where(side == 0, 3, 0) - 3 * shift) & (LANES - 1)
        ir, ic, jr, jc = i // 3, i % 3, spot // 3, spot % 3
        apart = jnp.where(side == 0, ic - jc + 3, jc - ic + 3)
        return jnp.where((ir == jr) & (i < 3 * rows) & (spot < 3 * rows), smooth_count(apart), 0.0).astype(BF16)

    own_border, halo_border = border(own_place - own_start), border(halo_place - halo_start)
    start = 0
    filtered_halo = dot(halo[0 : HALO * kk, :], taps)
    edges = dot(halo[HALO * kk :, :], halo_border)
    for index, (source, at, width) in enumerate(offsets):
        at = pl.ds(pl.multiple_of(at, 8), width)
        span = pl.ds(pl.multiple_of(own_start * width, 16), own_rows * width)
        filtered = dot(source[span, :], taps)
        grid[pl.ds(own_place, own_rows), at, :] = filtered.reshape(own_rows, width, LANES)
        edge[0, at, :] = dot(source[rows * width : rows * width + 32, :], own_border)[:width]
        piece = filtered_halo[start : start + HALO * width].reshape(HALO, width, LANES)
        grid[pl.ds(halo_place, HALO), at, :] = piece
        edge[1, at, :] = edges[index * 32 : index * 32 + width]
        start += HALO * width
    total_rows = own_rows + HALO
    out_rows = own_rows - HALO
    lane = iota((16, LANES), 1)
    near = ((lane + jnp.where(side == 0, 3, 0)) & (LANES - 1)) < 3
    before_in = jnp.where((top == 1) & (band == 0), 0.0, 1.0)
    after_in = jnp.where((top == 0) & (band == lax.axis_size("row") - 1), 0.0, 1.0)

    def filter_rows(group, carry):
        at = pl.ds(pl.multiple_of(group * 16, 16), 16)
        own_edge, halo_edge = edge[0, at, :], edge[1, at, :]
        low_edge = jnp.where(top == 1, halo_edge, own_edge)
        high_edge = jnp.where(top == 1, own_edge, halo_edge)
        chain = [None] * 6
        ring = []
        for r in range(total_rows):
            turned = low_edge if r < HALO else own_edge if r < own_rows else high_edge
            turned = pltpu.roll(turned, (-3 * r) % LANES, 1)
            value = grid[r, at, :] + jnp.where(near, turned, 0.0)
            for level in range(6):
                previous, chain[level] = chain[level], value
                if previous is None:
                    value = None
                    break
                value = previous + value
            if value is None:
                continue
            center = r - 3
            if masked and center < HALO:
                value = value * before_in
            elif masked and center >= own_rows:
                value = value * after_in
            ring.append(value)
            if len(ring) == 7:
                slope = (ring[6] - ring[0]) - 9.0 * (ring[5] - ring[1]) + 45.0 * (ring[4] - ring[2])
                y = center - 3 - HALO
                kept[0, y, at, :], kept[2, y, at, :] = split(ring[3])
                kept[1, y, at, :], kept[3, y, at, :] = split(slope)
                ring.pop(0)
        return carry

    lax.fori_loop(0, kk // 16, filter_rows, 0, unroll=kk // 16)
    first_row = HALO - own_place + own_start
    wide = 2 * LANES
    window = kw + 2 * kh
    hidden = w1.shape[1] // layers
    rest = w1.shape[2] - 6 * window
    ones = jnp.where(iota((rest, wide), 0) < 2, 1.0, 0.0).astype(BF16)
    sub = iota((layers, wide), 0)
    scale = depth_scale / (lax.axis_size("depth") * layers)

    def splat(index):
        line = w2[index : index + 1, :]
        return jnp.broadcast_to(jnp.concatenate([line, line], 1), (layers, wide))

    def shade(pair, carry):
        y = 2 * pair
        total = jnp.zeros((1, wide), F32)
        front = jnp.ones((1, wide), F32)
        color = [jnp.zeros((layers, wide), F32) for unused in range(3)]
        for half in range(2):
            at = pl.ds(half * kw, window)
            c_high, s_high, c_low, s_low = [
                jnp.concatenate([kept[k, y, at, :], kept[k, y + 1, at, :]], 1) for k in range(4)
            ]
            stacked = jnp.concatenate([c_high, s_high, c_high, s_high, c_low, s_low, ones], 0)
            units = jnp.tanh(dot(w1[half], stacked))
            o = [splat(4 * hidden + c) for c in range(4)]
            for h in range(hidden):
                unit = units[h * layers : (h + 1) * layers]
                for c in range(4):
                    o[c] = o[c] + splat(c * hidden + h) * unit
            x = o[3]
            optical = (jnp.maximum(x, 0.0) + jnp.log1p(jnp.exp(-jnp.abs(x)))) * scale
            through = optical
            for step in (1, 2, 4):
                through = through + jnp.where(sub >= step, pltpu.roll(through, step, 0), 0.0)
            through = through + total
            total = through[layers - 1 :]
            after = jnp.exp(-through)
            before = jnp.where(sub == 0, front, pltpu.roll(after, 1, 0))
            front = after[layers - 1 :]
            weight = before - after
            for c in range(3):
                color[c] = color[c] + weight / (1.0 + jnp.exp(-o[c]))
        for c in range(3):
            line = jnp.sum(color[c], axis=0, keepdims=True)
            out[c, pl.ds(first_row + y, 1), :] = line[:, :LANES]
            out[c, pl.ds(first_row + y + 1, 1), :] = line[:, LANES:]
        out[3, pl.ds(first_row + y, 1), :] = front[:, :LANES]
        out[3, pl.ds(first_row + y + 1, 1), :] = front[:, LANES:]
        return carry

    lax.fori_loop(0, out_rows // 2, shade, 0, unroll=out_rows // 2)


def call(kernel, out_shape, operands, scratch=(), flops=0, name=None):
    vmem = pl.BlockSpec(memory_space=pltpu.VMEM)
    return pl.pallas_call(
        kernel,
        out_shape=out_shape,
        in_specs=[vmem] * len(operands),
        out_specs=jax.tree.map(lambda unused: vmem, out_shape),
        scratch_shapes=list(scratch),
        compiler_params=pltpu.CompilerParams(vmem_limit_bytes=40 * 2**20),
        cost_estimate=pl.CostEstimate(flops=flops, bytes_accessed=2**20, transcendentals=0),
        name=name,
    )(*operands)


def combine(front, back):
    color = front[0:3] + front[3:4] * back[0:3]
    return jnp.concatenate([color, front[3:4] * back[3:4]], 0)


def local(fields, w_in, b_in, w_out, b_out):
    layers, rows, columns = fields.shape[1:]
    hidden = w_in.shape[0]
    slabs = lax.axis_size("depth")
    bands = lax.axis_size("row")
    me = lax.axis_index("depth")
    side = me & 1
    kw, kh = layers * FIELDS, HALO * FIELDS
    kk = 2 * (kw + kh)
    shape = jax.ShapeDtypeStruct
    mine, theirs, own_halo, other_halo = call(
        pack_kernel,
        [
            shape(((rows + 1) * kw, LANES), BF16),
            shape(((rows + 1) * kw, LANES), BF16),
            shape((rows * kh + kw, LANES), BF16),
            shape((rows * kh + kw, LANES), BF16),
        ],
        (fields,),
        [pltpu.VMEM((rows * kw, LANES), F32)] * 2,
        name="pack",
    )
    swap_pairs = [(i, i ^ 1) for i in range(slabs)]
    odd, even = range(1, slabs, 2), range(0, slabs, 2)
    diagonal_pairs = [(i, i + 1) for i in odd if i + 1 < slabs] + [(i, i - 1) for i in even if i]
    straight_pairs = [(i, i + 2) for i in odd if i + 2 < slabs] + [(i, i - 2) for i in even if i]
    swap = lax.ppermute(theirs, "depth", swap_pairs)
    diagonal = lax.ppermute(other_halo, "depth", diagonal_pairs)
    straight = lax.ppermute(own_halo, "depth", straight_pairs)

    width = -(-(6 * (kw + 2 * kh) + 2) // 256) * 256
    w1, w2 = call(
        functools.partial(weights_kernel, layers=layers, hidden=hidden, slabs=slabs),
        [shape((2, layers * hidden, width), BF16), shape((4 * hidden + 8, LANES), F32)],
        (w_in, b_in[None], w_out, b_out[None]),
        flops=10**8,
        name="weights",
    )
    mine, w1, w2 = lax.optimization_barrier((mine, w1, w2))
    message = shape((HALO * kk + 4 * 32, LANES), BF16)
    first, second = call(band_kernel, [message, message], (mine, swap, straight, diagonal), name="band")
    within = [(i, i ^ 1) for i in range(bands)]
    across = [(i, i + 1) for i in range(1, bands - 1, 2)] + [(i + 1, i) for i in range(1, bands - 1, 2)]
    second = lax.ppermute(second, "row", across)
    first = lax.ppermute(first, "row", within)

    def shaded(own_rows, flip, halo, previous, name):
        return call(
            functools.partial(
                shade_kernel, layers=layers, rows=rows, own_rows=own_rows, flip=flip, masked=bool(previous)
            ),
            shape((4, rows, LANES), F32),
            (mine, swap, straight, diagonal, halo, w1, w2, *previous),
            [
                pltpu.VMEM((own_rows + HALO, kk, LANES), F32),
                pltpu.VMEM((2, kk, LANES), F32),
                pltpu.VMEM((4, own_rows - HALO, kk, LANES), BF16),
            ],
            flops=10**10,
            name=name,
        )

    current = shaded(rows, False, first, (), "shade_most")
    current = shaded(2 * HALO, True, second, (current,), "shade_rest")
    step = 2
    while step < slabs:
        received = lax.ppermute(current, "depth", [(i, i ^ step) for i in range(slabs)])
        behind = (me & step) != 0
        current = combine(jnp.where(behind, received, current), jnp.where(behind, current, received))
        step *= 2
    current = jnp.concatenate([current[0:3], 1.0 - current[3:4]], 0)
    other = lax.ppermute(current, "depth", swap_pairs)
    first_half = jnp.where(side == 0, current, other)
    second_half = jnp.where(side == 0, other, current)
    return jnp.concatenate([first_half, second_half], 2)


def solution(mesh):
    return jax.shard_map(
        local,
        mesh=mesh,
        in_specs=(P(None, "depth", "row", None), P(), P(), P(), P()),
        out_specs=P(None, "row", None),
        check_vma=False,
    )
```

```python
import functools

import jax
import jax.numpy as jnp
from jax import lax
from jax.experimental import pallas as pl
from jax.experimental.pallas import tpu as pltpu
from jax.sharding import PartitionSpec as P

FIELDS = 4
HALO = 6
LANES = 128
HIGHEST = lax.Precision.HIGHEST
F32 = jnp.float32
BF16 = jnp.bfloat16
depth_scale = 2.0
smooth_counts = (20.0, 15.0, 6.0, 1.0)
slope_counts = ((1, 45.0), (2, -9.0), (3, 1.0))


def dot(a, b, precision=None):
    return jnp.dot(a, b, preferred_element_type=F32, precision=precision)


def iota(shape, dim):
    return lax.broadcasted_iota(jnp.int32, shape, dim)


def smooth_count(distance):
    d = jnp.abs(distance)
    out = jnp.where(d == 0, smooth_counts[0], 0.0)
    for place in (1, 2, 3):
        out = jnp.where(d == place, smooth_counts[place], out)
    return out.astype(F32)


def split(x):
    high = x.astype(BF16)
    return high, (x - high.astype(F32)).astype(BF16)


def pack_kernel(fields, mine, theirs, straight, diagonal, left, right):
    side = lax.axis_index("depth") & 1
    layers, rows = fields.shape[1], fields.shape[2]
    kw, kh = layers * FIELDS, HALO * FIELDS
    for layer in range(layers):
        for field in range(FIELDS):
            plane = fields[field, layer].astype(F32)
            place = pl.ds(layer * FIELDS + field, rows, stride=kw)
            left[place, :] = plane[:, :LANES]
            right[place, :] = plane[:, LANES:]
    lane = iota((kw, LANES), 1)
    shift = pl.multiple_of(side * (kw - kh), 8)

    def halves(row, start, count):
        a = left[pl.ds(row * kw + start, count), :]
        b = right[pl.ds(row * kw + start, count), :]
        return jnp.where(side == 0, a, b), jnp.where(side == 0, b, a)

    extra_low = jnp.zeros((kw, LANES), F32)
    extra_high = jnp.zeros((kw, LANES), F32)
    for row in range(0, rows, 2):
        pairs = []
        for r in (row, row + 1):
            a = left[pl.ds(r * kw, kw), :]
            b = right[pl.ds(r * kw, kw), :]
            inside = (lane >= 3 * r) & (lane < 3 * r + 3)
            extra_low = jnp.where(inside, pltpu.roll(b, (3 * r) % LANES, 1), extra_low)
            extra_high = jnp.where(inside, pltpu.roll(a, (3 * r + 3) % LANES, 1), extra_high)
            own = jnp.where(side == 0, a, b)
            other = jnp.where(side == 0, b, a)
            mine[pl.ds(r * kw, kw), :] = own.astype(BF16)
            theirs[pl.ds(r * kw, kw), :] = other.astype(BF16)
            pairs.append(halves(r, shift, kh))
        both = pl.ds(row * kh, 2 * kh)
        straight[both, :] = jnp.concatenate([pairs[0][0], pairs[1][0]], 0).astype(BF16)
        diagonal[both, :] = jnp.concatenate([pairs[0][1], pairs[1][1]], 0).astype(BF16)
    own = jnp.where(side == 0, extra_low, extra_high)
    other = jnp.where(side == 0, extra_high, extra_low)
    mine[rows * kw :, :] = own.astype(BF16)
    theirs[rows * kw :, :] = other.astype(BF16)
    empty = jnp.zeros((kw - kh, LANES), F32)
    for source, target in ((own, straight), (other, diagonal)):
        part = jnp.where(side == 0, source[:kh], source[kw - kh :])
        target[rows * kh :, :] = jnp.concatenate([part, empty], 0).astype(BF16)


def band_kernel(mine, swap, straight, diagonal, first, second):
    odd = lax.axis_index("row") & 1
    kw = 8 * FIELDS
    rows = mine.shape[0] // kw - 1
    for out, from_end in ((first, 1 - odd), (second, odd)):
        at, extra = 0, HALO * sum(r.shape[0] // (rows + 1) for r in (mine, swap)) + 2 * HALO * HALO * FIELDS
        for source in (mine, swap, straight, diagonal):
            width = kw if source.shape[0] == (rows + 1) * kw else HALO * FIELDS
            start = pl.multiple_of(from_end * (rows - HALO) * width, 16)
            out[at : at + HALO * width, :] = source[pl.ds(start, HALO * width), :]
            out[extra : extra + 32, :] = source[rows * width : rows * width + 32, :]
            at += HALO * width
            extra += 32


def weights_kernel(w_in, b_in, w_out, b_out, w1, w2, *, layers, hidden, slabs):
    depth = lax.axis_index("depth")
    side = depth & 1
    base = (depth - side) * layers
    total = slabs * layers
    width = w1.shape[2]
    window = (layers + 2 * HALO) * FIELDS
    kinds = w_in.shape[1]
    row, col = iota((kinds, width), 0), iota((kinds, width), 1)
    within = col % (2 * window)
    field = col & 3
    ending = col >= 6 * window
    pick1 = jnp.where(ending, -1, jnp.where(within < window, field, field + 4))
    pick2 = jnp.where(ending | (within >= window), -1, field + 8)
    eye = iota((hidden, hidden), 0) == iota((hidden, hidden), 1)
    bias = jnp.sum(jnp.where(eye, b_in[...], 0.0), axis=1, keepdims=True)
    part1 = dot(w_in[...], (row == pick1).astype(F32), HIGHEST)
    part2 = dot(w_in[...], (row == pick2).astype(F32), HIGHEST)
    kappa = iota((hidden, width), 1)
    part1 = jnp.where(kappa == 6 * window, bias, jnp.where(kappa == 6 * window + 1, bias, part1))
    scale = 1.0 / 64.0**3
    row_sign = jnp.where((lax.axis_index("row") & 1) == 0, -1.0 / 60.0, 1.0 / 60.0)
    z, place = iota((layers, width), 0), iota((layers, width), 1)
    inner = place % (2 * window)
    slope_kind = inner >= window
    last = place >= 6 * window
    slot = jnp.where(slope_kind, inner - window, inner) >> 2
    low_column = ((place >= 2 * window) & (place < 4 * window)) | (place == 6 * window + 1)
    for half in range(2):
        distance = slot - HALO - z
        center = smooth_count(distance) * scale
        slope = jnp.zeros((layers, width), F32)
        for offset, count in slope_counts:
            for sign in (1, -1):
                at = base + half * layers + z + sign * offset
                inside = ((at >= 0) & (at < total)).astype(F32)
                slope = slope + (inside * (sign * count)) * smooth_count(distance - sign * offset)
        center = jnp.where(last, 1.0, jnp.where(slope_kind, center * row_sign, center))
        product = center[None] * part1[:, None, :] + (slope * (scale / 60.0))[None] * part2[:, None, :]
        high = product.astype(BF16).astype(F32)
        chosen = jnp.where(low_column[None], product - high, high)
        w1[half] = chosen.reshape(hidden * layers, width).astype(BF16)
    outs = w_out.shape[0]
    for c in range(outs):
        values = jnp.sum(jnp.where(eye, w_out[c : c + 1, :], 0.0), axis=1, keepdims=True)
        factor = 0.5 if c < 3 else 1.0
        w2[c * hidden : (c + 1) * hidden, :] = jnp.broadcast_to(factor * values, (hidden, LANES))
    pick = iota((8, outs), 0) == iota((8, outs), 1)
    values = jnp.sum(jnp.where(pick, b_out[...], 0.0), axis=1, keepdims=True)
    values = jnp.where(iota((8, 1), 0) < 3, 0.5 * values, values)
    w2[outs * hidden :, :] = jnp.broadcast_to(values, (8, LANES))


def places(side, layers):
    kw, kh = layers * FIELDS, HALO * FIELDS
    far = kh + 2 * kw
    return ((kh + side * kw, kw), (kh + (1 - side) * kw, kw), ((1 - side) * far, kh), (side * far, kh))


def tap_matrix():
    return smooth_count(iota((LANES, LANES), 0) - iota((LANES, LANES), 1)).astype(BF16)


def border(side, first, sign, low, high):
    i, j = iota((LANES, LANES), 0), iota((LANES, LANES), 1)
    spot = (j + jnp.where(side == 0, 3, 0)) & (LANES - 1)
    ir, ic, jr, jc = i // 3, i % 3, spot // 3, spot % 3
    apart = jnp.where(side == 0, ic - jc + 3, jc - ic + 3)
    here = (ir == first + sign * jr) & (jr >= low) & (jr < high)
    return jnp.where(here, smooth_count(apart), 0.0).astype(BF16)


def place_halo(halo, grid, edge, layers, side, flipped, edges):
    kk = 2 * (layers + HALO) * FIELDS
    filtered = dot(halo[0 : HALO * kk, :], tap_matrix())
    added = dot(halo[HALO * kk :, :], edges)
    start = 0
    for index, (at, width) in enumerate(places(side, layers)):
        at = pl.ds(pl.multiple_of(at, 8), width)
        for row in range(HALO):
            grid[jnp.where(flipped, HALO - 1 - row, row), at, :] = filtered[start : start + width]
            start += width
        edge[at, :] = added[index * 32 : index * 32 + width]


def near_cut(side):
    return ((iota((16, LANES), 1) + jnp.where(side == 0, 3, 0)) & (LANES - 1)) < 3


def next_row(value, chain, ring, scale=None):
    for level in range(6):
        previous, chain[level] = chain[level], value
        if previous is None:
            return None
        value = previous + value
    if scale is not None:
        value = value * scale
    ring.append(value)
    if len(ring) < 7:
        return None
    slope = (ring[6] - ring[0]) - 9.0 * (ring[5] - ring[1]) + 45.0 * (ring[4] - ring[2])
    center = ring[3]
    ring.pop(0)
    return center, slope


def keep(kept, y, at, center, slope):
    kept[0, y, at, :], kept[2, y, at, :] = split(center)
    kept[1, y, at, :], kept[3, y, at, :] = split(slope)


def shade_rows(kept, w1, w2, out, layers, first, flipped, last):
    kw, kh = layers * FIELDS, HALO * FIELDS
    wide = 2 * LANES
    window = kw + 2 * kh
    hidden = w1.shape[1] // layers
    rest = w1.shape[2] - 6 * window
    ones = jnp.where(iota((rest, wide), 0) < 2, 1.0, 0.0).astype(BF16)
    sub = iota((layers, wide), 0)
    scale = depth_scale / (lax.axis_size("depth") * layers)

    def splat(index):
        line = w2[index : index + 1, :]
        return jnp.broadcast_to(jnp.concatenate([line, line], 1), (layers, wide))

    def target(k):
        return pl.ds(jnp.where(flipped, last - first - k, first + k), 1)

    for y in range(0, kept.shape[1], 2):
        total = jnp.zeros((1, wide), F32)
        front = jnp.ones((1, wide), F32)
        color = [jnp.zeros((layers, wide), F32) for unused in range(3)]
        for half in range(2):
            at = pl.ds(half * kw, window)
            c_high, s_high, c_low, s_low = [
                jnp.concatenate([kept[k, y, at, :], kept[k, y + 1, at, :]], 1) for k in range(4)
            ]
            stacked = jnp.concatenate([c_high, s_high, c_high, s_high, c_low, s_low, ones], 0)
            units = jnp.tanh(dot(w1[half], stacked))
            o = [splat(4 * hidden + c) for c in range(4)]
            for h in range(hidden):
                unit = units[h * layers : (h + 1) * layers]
                for c in range(4):
                    o[c] = o[c] + splat(c * hidden + h) * unit
            x = o[3]
            optical = (jnp.maximum(x, 0.0) + jnp.log(1.0 + jnp.exp(-jnp.abs(x)))) * scale
            through = optical
            for step in (1, 2, 4):
                through = through + jnp.where(sub >= step, pltpu.roll(through, step, 0), 0.0)
            through = through + total
            total = through[layers - 1 :]
            after = jnp.exp(-through)
            before = jnp.where(sub == 0, front, pltpu.roll(after, 1, 0))
            front = after[layers - 1 :]
            weight = before - after
            for c in range(3):
                color[c] = color[c] + weight * jnp.tanh(o[c])
        lines = [0.5 * (1.0 - front + jnp.sum(color[c], axis=0, keepdims=True)) for c in range(3)]
        for c, line in enumerate(lines + [front]):
            out[c, target(y), :] = line[:, :LANES]
            out[c, target(y + 1), :] = line[:, LANES:]


def most_kernel(mine, swap, straight, diagonal, halo, w1, w2, out, state, grid, edge, kept, *, layers, rows):
    side = lax.axis_index("depth") & 1
    flipped = (lax.axis_index("row") & 1) == 0
    kk = 2 * (layers + HALO) * FIELDS
    first, sign = jnp.where(flipped, rows + HALO - 1, -HALO), jnp.where(flipped, -1, 1)
    own_border = border(side, first, sign, HALO, rows + HALO)
    halo_border = border(side, jnp.where(flipped, HALO - 1, rows - HALO), sign, 0, HALO)
    place_halo(halo, grid, edge.at[1], layers, side, flipped, halo_border)
    taps = tap_matrix()
    for source, (at, width) in zip((mine, swap, straight, diagonal), places(side, layers)):
        at = pl.ds(pl.multiple_of(at, 8), width)
        filtered = dot(source[0 : rows * width, :], taps)
        for row in range(rows):
            place = jnp.where(flipped, rows + HALO - 1 - row, row + HALO)
            grid[place, at, :] = filtered[row * width : (row + 1) * width]
        edge[0, at, :] = dot(source[rows * width : rows * width + 32, :], own_border)[:width]
    near = near_cut(side)

    def filter_rows(group, carry):
        at = pl.ds(pl.multiple_of(group * 16, 16), 16)
        edges = edge[1, at, :], edge[0, at, :]
        chain, ring = [None] * 6, []
        for r in range(rows + HALO):
            turned = pltpu.roll(edges[r >= HALO], (-3 * r) % LANES, 1)
            given = next_row(grid[r, at, :] + jnp.where(near, turned, 0.0), chain, ring)
            if given is not None:
                keep(kept, r - 2 * HALO, at, *given)
        for index, value in enumerate(chain + ring):
            state[index, at, :] = value
        return carry

    lax.fori_loop(0, kk // 16, filter_rows, 0, unroll=kk // 16)
    shade_rows(kept, w1, w2, out, layers, 0, flipped, rows - 1)


def rest_kernel(halo, w1, w2, state, done, out, grid, edge, kept, *, layers, rows):
    out[...] = done[...]
    side = lax.axis_index("depth") & 1
    band = lax.axis_index("row")
    flipped = (band & 1) == 0
    kk = 2 * (layers + HALO) * FIELDS
    halo_border = border(side, jnp.where(flipped, rows - 1, 0), jnp.where(flipped, -1, 1), 0, HALO)
    place_halo(halo, grid, edge, layers, side, flipped, halo_border)
    near = near_cut(side)
    outside = jnp.where(flipped, band == 0, band == lax.axis_size("row") - 1)
    inside = jnp.where(outside, 0.0, 1.0)

    def filter_rows(group, carry):
        at = pl.ds(pl.multiple_of(group * 16, 16), 16)
        edges = edge[at, :]
        values = [state[index, at, :] for index in range(12)]
        chain, ring = values[:6], values[6:]
        for r in range(HALO):
            turned = pltpu.roll(edges, (-3 * r) % LANES, 1)
            value = grid[r, at, :] + jnp.where(near, turned, 0.0)
            keep(kept, r, at, *next_row(value, chain, ring, inside if r >= 3 else None))
        return carry

    lax.fori_loop(0, kk // 16, filter_rows, 0, unroll=kk // 16)
    shade_rows(kept, w1, w2, out, layers, rows - HALO, flipped, rows - 1)


def call(kernel, out_shape, operands, scratch=(), flops=0, name=None):
    vmem = pl.BlockSpec(memory_space=pltpu.VMEM)
    return pl.pallas_call(
        kernel,
        out_shape=out_shape,
        in_specs=[vmem] * len(operands),
        out_specs=jax.tree.map(lambda unused: vmem, out_shape),
        scratch_shapes=list(scratch),
        compiler_params=pltpu.CompilerParams(vmem_limit_bytes=40 * 2**20),
        cost_estimate=pl.CostEstimate(flops=flops, bytes_accessed=2**20, transcendentals=0),
        name=name,
    )(*operands)


def combine(front, back):
    color = front[0:3] + front[3:4] * back[0:3]
    return jnp.concatenate([color, front[3:4] * back[3:4]], 0)


def local(fields, w_in, b_in, w_out, b_out):
    layers, rows, columns = fields.shape[1:]
    hidden = w_in.shape[0]
    slabs = lax.axis_size("depth")
    bands = lax.axis_size("row")
    me = lax.axis_index("depth")
    side = me & 1
    kw, kh = layers * FIELDS, HALO * FIELDS
    kk = 2 * (kw + kh)
    shape = jax.ShapeDtypeStruct
    mine, theirs, own_halo, other_halo = call(
        pack_kernel,
        [
            shape(((rows + 1) * kw, LANES), BF16),
            shape(((rows + 1) * kw, LANES), BF16),
            shape((rows * kh + kw, LANES), BF16),
            shape((rows * kh + kw, LANES), BF16),
        ],
        (fields,),
        [pltpu.VMEM((rows * kw, LANES), F32)] * 2,
        name="pack",
    )
    swap_pairs = [(i, i ^ 1) for i in range(slabs)]
    odd, even = range(1, slabs, 2), range(0, slabs, 2)
    diagonal_pairs = [(i, i + 1) for i in odd if i + 1 < slabs] + [(i, i - 1) for i in even if i]
    straight_pairs = [(i, i + 2) for i in odd if i + 2 < slabs] + [(i, i - 2) for i in even if i]
    swap = lax.ppermute(theirs, "depth", swap_pairs)
    diagonal = lax.ppermute(other_halo, "depth", diagonal_pairs)
    straight = lax.ppermute(own_halo, "depth", straight_pairs)

    width = -(-(6 * (kw + 2 * kh) + 2) // 256) * 256
    w1, w2 = call(
        functools.partial(weights_kernel, layers=layers, hidden=hidden, slabs=slabs),
        [shape((2, layers * hidden, width), BF16), shape((4 * hidden + 8, LANES), F32)],
        (w_in, b_in[None], w_out, b_out[None]),
        flops=10**8,
        name="weights",
    )
    mine, w1, w2 = lax.optimization_barrier((mine, w1, w2))
    message = shape((HALO * kk + 4 * 32, LANES), BF16)
    first, second = call(band_kernel, [message, message], (mine, swap, straight, diagonal), name="band")
    within = [(i, i ^ 1) for i in range(bands)]
    across = [(i, i + 1) for i in range(1, bands - 1, 2)] + [(i + 1, i) for i in range(1, bands - 1, 2)]
    second = lax.ppermute(second, "row", across)
    first = lax.ppermute(first, "row", within)

    image = shape((4, rows, LANES), F32)
    current, state = call(
        functools.partial(most_kernel, layers=layers, rows=rows),
        [image, shape((12, kk, LANES), F32)],
        (mine, swap, straight, diagonal, first, w1, w2),
        [
            pltpu.VMEM((rows + HALO, kk, LANES), F32),
            pltpu.VMEM((2, kk, LANES), F32),
            pltpu.VMEM((4, rows - HALO, kk, LANES), BF16),
        ],
        flops=10**10,
        name="shade_most",
    )
    current = call(
        functools.partial(rest_kernel, layers=layers, rows=rows),
        image,
        (second, w1, w2, state, current),
        [
            pltpu.VMEM((HALO, kk, LANES), F32),
            pltpu.VMEM((kk, LANES), F32),
            pltpu.VMEM((4, HALO, kk, LANES), BF16),
        ],
        flops=10**9,
        name="shade_rest",
    )
    step = 2
    while step < slabs:
        received = lax.ppermute(current, "depth", [(i, i ^ step) for i in range(slabs)])
        behind = (me & step) != 0
        current = combine(jnp.where(behind, received, current), jnp.where(behind, current, received))
        step *= 2
    current = jnp.concatenate([current[0:3], 1.0 - current[3:4]], 0)
    other = lax.ppermute(current, "depth", swap_pairs)
    first_half = jnp.where(side == 0, current, other)
    second_half = jnp.where(side == 0, other, current)
    return jnp.concatenate([first_half, second_half], 2)


def solution(mesh):
    return jax.shard_map(
        local,
        mesh=mesh,
        in_specs=(P(None, "depth", "row", None), P(), P(), P(), P()),
        out_specs=P(None, "row", None),
        check_vma=False,
    )
```

```python
import functools

import jax
import jax.numpy as jnp
from jax import lax
from jax.experimental import pallas as pl
from jax.experimental.pallas import tpu as pltpu
from jax.sharding import PartitionSpec as P

FIELDS = 4
HALO = 6
LANES = 128
HIGHEST = lax.Precision.HIGHEST
F32 = jnp.float32
BF16 = jnp.bfloat16
depth_scale = 2.0
smooth_counts = (20.0, 15.0, 6.0, 1.0)
slope_counts = ((1, 45.0), (2, -9.0), (3, 1.0))


def dot(a, b, precision=None):
    return jnp.dot(a, b, preferred_element_type=F32, precision=precision)


def iota(shape, dim):
    return lax.broadcasted_iota(jnp.int32, shape, dim)


def smooth_count(distance):
    d = jnp.abs(distance)
    out = jnp.where(d == 0, smooth_counts[0], 0.0)
    for place in (1, 2, 3):
        out = jnp.where(d == place, smooth_counts[place], out)
    return out.astype(F32)


def split(x):
    high = x.astype(BF16)
    return high, (x - high.astype(F32)).astype(BF16)


def pack_kernel(fields, mine, theirs, straight, diagonal, left, right):
    side = lax.axis_index("depth") & 1
    layers, rows = fields.shape[1], fields.shape[2]
    kw, kh = layers * FIELDS, HALO * FIELDS
    for layer in range(layers):
        for field in range(FIELDS):
            plane = fields[field, layer].astype(F32)
            place = pl.ds(layer * FIELDS + field, rows, stride=kw)
            left[place, :] = plane[:, :LANES]
            right[place, :] = plane[:, LANES:]
    lane = iota((kw, LANES), 1)
    shift = pl.multiple_of(side * (kw - kh), 8)

    def halves(row, start, count):
        a = left[pl.ds(row * kw + start, count), :]
        b = right[pl.ds(row * kw + start, count), :]
        return jnp.where(side == 0, a, b), jnp.where(side == 0, b, a)

    extra_low = jnp.zeros((kw, LANES), F32)
    extra_high = jnp.zeros((kw, LANES), F32)
    for row in range(0, rows, 2):
        pairs = []
        for r in (row, row + 1):
            a = left[pl.ds(r * kw, kw), :]
            b = right[pl.ds(r * kw, kw), :]
            inside = (lane >= 3 * r) & (lane < 3 * r + 3)
            extra_low = jnp.where(inside, pltpu.roll(b, (3 * r) % LANES, 1), extra_low)
            extra_high = jnp.where(inside, pltpu.roll(a, (3 * r + 3) % LANES, 1), extra_high)
            own = jnp.where(side == 0, a, b)
            other = jnp.where(side == 0, b, a)
            mine[pl.ds(r * kw, kw), :] = own.astype(BF16)
            theirs[pl.ds(r * kw, kw), :] = other.astype(BF16)
            pairs.append(halves(r, shift, kh))
        both = pl.ds(row * kh, 2 * kh)
        straight[both, :] = jnp.concatenate([pairs[0][0], pairs[1][0]], 0).astype(BF16)
        diagonal[both, :] = jnp.concatenate([pairs[0][1], pairs[1][1]], 0).astype(BF16)
    own = jnp.where(side == 0, extra_low, extra_high)
    other = jnp.where(side == 0, extra_high, extra_low)
    mine[rows * kw :, :] = own.astype(BF16)
    theirs[rows * kw :, :] = other.astype(BF16)
    empty = jnp.zeros((kw - kh, LANES), F32)
    for source, target in ((own, straight), (other, diagonal)):
        part = jnp.where(side == 0, source[:kh], source[kw - kh :])
        target[rows * kh :, :] = jnp.concatenate([part, empty], 0).astype(BF16)


def band_kernel(mine, swap, straight, diagonal, first, second):
    odd = lax.axis_index("row") & 1
    kw = 8 * FIELDS
    rows = mine.shape[0] // kw - 1
    for out, from_end in ((first, 1 - odd), (second, odd)):
        at, extra = 0, HALO * sum(r.shape[0] // (rows + 1) for r in (mine, swap)) + 2 * HALO * HALO * FIELDS
        for source in (mine, swap, straight, diagonal):
            width = kw if source.shape[0] == (rows + 1) * kw else HALO * FIELDS
            start = pl.multiple_of(from_end * (rows - HALO) * width, 16)
            out[at : at + HALO * width, :] = source[pl.ds(start, HALO * width), :]
            out[extra : extra + 32, :] = source[rows * width : rows * width + 32, :]
            at += HALO * width
            extra += 32


def weights_kernel(w_in, b_in, w_out, b_out, w1, w2, *, layers, hidden, slabs):
    depth = lax.axis_index("depth")
    side = depth & 1
    base = (depth - side) * layers
    total = slabs * layers
    width = w1.shape[2]
    window = (layers + 2 * HALO) * FIELDS
    kinds = w_in.shape[1]
    row, col = iota((kinds, width), 0), iota((kinds, width), 1)
    within = col % (2 * window)
    field = col & 3
    ending = col >= 6 * window
    pick1 = jnp.where(ending, -1, jnp.where(within < window, field, field + 4))
    pick2 = jnp.where(ending | (within >= window), -1, field + 8)
    eye = iota((hidden, hidden), 0) == iota((hidden, hidden), 1)
    bias = jnp.sum(jnp.where(eye, b_in[...], 0.0), axis=1, keepdims=True)
    part1 = dot(w_in[...], (row == pick1).astype(F32), HIGHEST)
    part2 = dot(w_in[...], (row == pick2).astype(F32), HIGHEST)
    kappa = iota((hidden, width), 1)
    part1 = jnp.where(kappa == 6 * window, bias, jnp.where(kappa == 6 * window + 1, bias, part1))
    scale = 1.0 / 64.0**3
    row_sign = jnp.where((lax.axis_index("row") & 1) == 0, -1.0 / 60.0, 1.0 / 60.0)
    z, place = iota((layers, width), 0), iota((layers, width), 1)
    inner = place % (2 * window)
    slope_kind = inner >= window
    last = place >= 6 * window
    slot = jnp.where(slope_kind, inner - window, inner) >> 2
    low_column = ((place >= 2 * window) & (place < 4 * window)) | (place == 6 * window + 1)
    for half in range(2):
        distance = slot - HALO - z
        center = smooth_count(distance) * scale
        slope = jnp.zeros((layers, width), F32)
        for offset, count in slope_counts:
            for sign in (1, -1):
                at = base + half * layers + z + sign * offset
                inside = ((at >= 0) & (at < total)).astype(F32)
                slope = slope + (inside * (sign * count)) * smooth_count(distance - sign * offset)
        center = jnp.where(last, 1.0, jnp.where(slope_kind, center * row_sign, center))
        product = center[None] * part1[:, None, :] + (slope * (scale / 60.0))[None] * part2[:, None, :]
        high = product.astype(BF16).astype(F32)
        chosen = jnp.where(low_column[None], product - high, high)
        w1[half] = chosen.reshape(hidden * layers, width).astype(BF16)
    outs = w_out.shape[0]
    for c in range(outs):
        values = jnp.sum(jnp.where(eye, w_out[c : c + 1, :], 0.0), axis=1, keepdims=True)
        factor = 0.5 if c < 3 else 1.0
        w2[c * hidden : (c + 1) * hidden, :] = jnp.broadcast_to(factor * values, (hidden, LANES))
    pick = iota((8, outs), 0) == iota((8, outs), 1)
    values = jnp.sum(jnp.where(pick, b_out[...], 0.0), axis=1, keepdims=True)
    values = jnp.where(iota((8, 1), 0) < 3, 0.5 * values, values)
    w2[outs * hidden :, :] = jnp.broadcast_to(values, (8, LANES))


def places(side, layers):
    kw, kh = layers * FIELDS, HALO * FIELDS
    far = kh + 2 * kw
    return ((kh + side * kw, kw), (kh + (1 - side) * kw, kw), ((1 - side) * far, kh), (side * far, kh))


def tap_matrix():
    return smooth_count(iota((LANES, LANES), 0) - iota((LANES, LANES), 1)).astype(BF16)


def border(side, first, sign, low, high):
    i, j = iota((LANES, LANES), 0), iota((LANES, LANES), 1)
    spot = (j + jnp.where(side == 0, 3, 0)) & (LANES - 1)
    ir, ic, jr, jc = i // 3, i % 3, spot // 3, spot % 3
    apart = jnp.where(side == 0, ic - jc + 3, jc - ic + 3)
    here = (ir == first + sign * jr) & (jr >= low) & (jr < high)
    return jnp.where(here, smooth_count(apart), 0.0).astype(BF16)


def place_halo(halo, grid, edge, layers, side, flipped, edges):
    kk = 2 * (layers + HALO) * FIELDS
    filtered = dot(halo[0 : HALO * kk, :], tap_matrix())
    added = dot(halo[HALO * kk :, :], edges)
    start = 0
    for index, (at, width) in enumerate(places(side, layers)):
        at = pl.ds(pl.multiple_of(at, 8), width)
        for row in range(HALO):
            grid[jnp.where(flipped, HALO - 1 - row, row), at, :] = filtered[start : start + width]
            start += width
        edge[at, :] = added[index * 32 : index * 32 + width]


def near_cut(side):
    return ((iota((16, LANES), 1) + jnp.where(side == 0, 3, 0)) & (LANES - 1)) < 3


def next_row(value, chain, ring, scale=None):
    for level in range(6):
        previous, chain[level] = chain[level], value
        if previous is None:
            return None
        value = previous + value
    if scale is not None:
        value = value * scale
    ring.append(value)
    if len(ring) < 7:
        return None
    slope = (ring[6] - ring[0]) - 9.0 * (ring[5] - ring[1]) + 45.0 * (ring[4] - ring[2])
    center = ring[3]
    ring.pop(0)
    return center, slope


def keep(kept, y, at, center, slope):
    kept[0, y, at, :], kept[2, y, at, :] = split(center)
    kept[1, y, at, :], kept[3, y, at, :] = split(slope)


def shade_rows(kept, w1, w2, out, layers, first, flipped, last):
    kw, kh = layers * FIELDS, HALO * FIELDS
    wide = 2 * LANES
    window = kw + 2 * kh
    hidden = w1.shape[1] // layers
    rest = w1.shape[2] - 6 * window
    ones = jnp.where(iota((rest, wide), 0) < 2, 1.0, 0.0).astype(BF16)
    sub = iota((layers, wide), 0)
    scale = depth_scale / (lax.axis_size("depth") * layers)

    def splat(index):
        line = w2[index : index + 1, :]
        return jnp.broadcast_to(jnp.concatenate([line, line], 1), (layers, wide))

    def target(k):
        return pl.ds(jnp.where(flipped, last - first - k, first + k), 1)

    for y in range(0, kept.shape[1], 2):
        total = jnp.zeros((1, wide), F32)
        front = jnp.ones((1, wide), F32)
        color = [jnp.zeros((layers, wide), F32) for unused in range(3)]
        for half in range(2):
            at = pl.ds(half * kw, window)
            c_high, s_high, c_low, s_low = [
                jnp.concatenate([kept[k, y, at, :], kept[k, y + 1, at, :]], 1) for k in range(4)
            ]
            stacked = jnp.concatenate([c_high, s_high, c_high, s_high, c_low, s_low, ones], 0)
            units = jnp.tanh(dot(w1[half], stacked))
            o = [splat(4 * hidden + c) for c in range(4)]
            for h in range(hidden):
                unit = units[h * layers : (h + 1) * layers]
                for c in range(4):
                    o[c] = o[c] + splat(c * hidden + h) * unit
            x = o[3]
            optical = (jnp.maximum(x, 0.0) + jnp.log(1.0 + jnp.exp(-jnp.abs(x)))) * scale
            through = optical
            for step in (1, 2, 4):
                through = through + jnp.where(sub >= step, pltpu.roll(through, step, 0), 0.0)
            through = through + total
            total = through[layers - 1 :]
            after = jnp.exp(-through)
            before = jnp.where(sub == 0, front, pltpu.roll(after, 1, 0))
            front = after[layers - 1 :]
            weight = before - after
            for c in range(3):
                color[c] = color[c] + weight * jnp.tanh(o[c])
        lines = [0.5 * (1.0 - front + jnp.sum(color[c], axis=0, keepdims=True)) for c in range(3)]
        for c, line in enumerate(lines + [front]):
            out[c, target(y), :] = line[:, :LANES]
            out[c, target(y + 1), :] = line[:, LANES:]


def most_kernel(mine, swap, straight, diagonal, halo, w1, w2, out, state, grid, edge, kept, *, layers, rows):
    side = lax.axis_index("depth") & 1
    flipped = (lax.axis_index("row") & 1) == 0
    kk = 2 * (layers + HALO) * FIELDS
    first, sign = jnp.where(flipped, rows + HALO - 1, -HALO), jnp.where(flipped, -1, 1)
    own_border = border(side, first, sign, HALO, rows + HALO)
    halo_border = border(side, jnp.where(flipped, HALO - 1, rows - HALO), sign, 0, HALO)
    place_halo(halo, grid, edge.at[1], layers, side, flipped, halo_border)
    taps = tap_matrix()
    for source, (at, width) in zip((mine, swap, straight, diagonal), places(side, layers)):
        at = pl.ds(pl.multiple_of(at, 8), width)
        filtered = dot(source[0 : rows * width, :], taps)
        for row in range(rows):
            place = jnp.where(flipped, rows + HALO - 1 - row, row + HALO)
            grid[place, at, :] = filtered[row * width : (row + 1) * width]
        edge[0, at, :] = dot(source[rows * width : rows * width + 32, :], own_border)[:width]
    near = near_cut(side)

    def filter_rows(group, carry):
        at = pl.ds(pl.multiple_of(group * 16, 16), 16)
        edges = edge[1, at, :], edge[0, at, :]
        chain, ring = [None] * 6, []
        for r in range(rows + HALO):
            turned = pltpu.roll(edges[r >= HALO], (-3 * r) % LANES, 1)
            given = next_row(grid[r, at, :] + jnp.where(near, turned, 0.0), chain, ring)
            if given is not None:
                keep(kept, r - 2 * HALO, at, *given)
        for index, value in enumerate(chain + ring):
            state[index, at, :] = value
        return carry

    lax.fori_loop(0, kk // 16, filter_rows, 0, unroll=kk // 16)
    shade_rows(kept, w1, w2, out, layers, 0, flipped, rows - 1)


def rest_kernel(halo, w1, w2, state, done, out, grid, edge, kept, *, layers, rows):
    out[...] = done[...]
    side = lax.axis_index("depth") & 1
    band = lax.axis_index("row")
    flipped = (band & 1) == 0
    kk = 2 * (layers + HALO) * FIELDS
    halo_border = border(side, jnp.where(flipped, rows - 1, 0), jnp.where(flipped, -1, 1), 0, HALO)
    place_halo(halo, grid, edge, layers, side, flipped, halo_border)
    near = near_cut(side)
    outside = jnp.where(flipped, band == 0, band == lax.axis_size("row") - 1)
    inside = jnp.where(outside, 0.0, 1.0)

    def filter_rows(group, carry):
        at = pl.ds(pl.multiple_of(group * 16, 16), 16)
        edges = edge[at, :]
        values = [state[index, at, :] for index in range(12)]
        chain, ring = values[:6], values[6:]
        for r in range(HALO):
            turned = pltpu.roll(edges, (-3 * r) % LANES, 1)
            value = grid[r, at, :] + jnp.where(near, turned, 0.0)
            keep(kept, r, at, *next_row(value, chain, ring, inside if r >= 3 else None))
        return carry

    lax.fori_loop(0, kk // 16, filter_rows, 0, unroll=kk // 16)
    shade_rows(kept, w1, w2, out, layers, rows - HALO, flipped, rows - 1)


def call(kernel, out_shape, operands, scratch=(), flops=0, name=None):
    vmem = pl.BlockSpec(memory_space=pltpu.VMEM)
    return pl.pallas_call(
        kernel,
        out_shape=out_shape,
        in_specs=[vmem] * len(operands),
        out_specs=jax.tree.map(lambda unused: vmem, out_shape),
        scratch_shapes=list(scratch),
        compiler_params=pltpu.CompilerParams(vmem_limit_bytes=40 * 2**20),
        cost_estimate=pl.CostEstimate(flops=flops, bytes_accessed=2**20, transcendentals=0),
        name=name,
    )(*operands)


def combine(front, back):
    color = front[0:3] + front[3:4] * back[0:3]
    return jnp.concatenate([color, front[3:4] * back[3:4]], 0)


def local(fields, w_in, b_in, w_out, b_out):
    layers, rows, columns = fields.shape[1:]
    hidden = w_in.shape[0]
    slabs = lax.axis_size("depth")
    bands = lax.axis_size("row")
    me = lax.axis_index("depth")
    side = me & 1
    kw, kh = layers * FIELDS, HALO * FIELDS
    kk = 2 * (kw + kh)
    shape = jax.ShapeDtypeStruct
    mine, theirs, own_halo, other_halo = call(
        pack_kernel,
        [
            shape(((rows + 1) * kw, LANES), BF16),
            shape(((rows + 1) * kw, LANES), BF16),
            shape((rows * kh + kw, LANES), BF16),
            shape((rows * kh + kw, LANES), BF16),
        ],
        (fields,),
        [pltpu.VMEM((rows * kw, LANES), F32)] * 2,
        name="pack",
    )
    swap_pairs = [(i, i ^ 1) for i in range(slabs)]
    odd, even = range(1, slabs, 2), range(0, slabs, 2)
    diagonal_pairs = [(i, i + 1) for i in odd if i + 1 < slabs] + [(i, i - 1) for i in even if i]
    straight_pairs = [(i, i + 2) for i in odd if i + 2 < slabs] + [(i, i - 2) for i in even if i]
    swap = lax.ppermute(theirs, "depth", swap_pairs)
    diagonal = lax.ppermute(other_halo, "depth", diagonal_pairs)
    straight = lax.ppermute(own_halo, "depth", straight_pairs)
    swap, diagonal, straight = lax.optimization_barrier((swap, diagonal, straight))

    width = -(-(6 * (kw + 2 * kh) + 2) // 256) * 256
    w1, w2 = call(
        functools.partial(weights_kernel, layers=layers, hidden=hidden, slabs=slabs),
        [shape((2, layers * hidden, width), BF16), shape((4 * hidden + 8, LANES), F32)],
        (w_in, b_in[None], w_out, b_out[None]),
        flops=10**8,
        name="weights",
    )
    mine, w1, w2 = lax.optimization_barrier((mine, w1, w2))
    message = shape((HALO * kk + 4 * 32, LANES), BF16)
    first, second = call(band_kernel, [message, message], (mine, swap, straight, diagonal), name="band")
    within = [(i, i ^ 1) for i in range(bands)]
    across = [(i, i + 1) for i in range(1, bands - 1, 2)] + [(i + 1, i) for i in range(1, bands - 1, 2)]
    second = lax.ppermute(second, "row", across)
    first = lax.ppermute(first, "row", within)

    image = shape((4, rows, LANES), F32)
    current, state = call(
        functools.partial(most_kernel, layers=layers, rows=rows),
        [image, shape((12, kk, LANES), F32)],
        (mine, swap, straight, diagonal, first, w1, w2),
        [
            pltpu.VMEM((rows + HALO, kk, LANES), F32),
            pltpu.VMEM((2, kk, LANES), F32),
            pltpu.VMEM((4, rows - HALO, kk, LANES), BF16),
        ],
        flops=10**10,
        name="shade_most",
    )
    current = call(
        functools.partial(rest_kernel, layers=layers, rows=rows),
        image,
        (second, w1, w2, state, current),
        [
            pltpu.VMEM((HALO, kk, LANES), F32),
            pltpu.VMEM((kk, LANES), F32),
            pltpu.VMEM((4, HALO, kk, LANES), BF16),
        ],
        flops=10**9,
        name="shade_rest",
    )
    def exchanged(distance):
        return lax.ppermute(current, "depth", [(i, i ^ distance) for i in range(slabs)])

    def composed(own, received, step):
        behind = (me & step) != 0
        return combine(jnp.where(behind, received, own), jnp.where(behind, own, received))

    step = 2
    while 2 * step < slabs:
        current = composed(current, exchanged(step), step)
        step *= 2
    across_x, across_z, across_both = exchanged(1), exchanged(step), exchanged(1 ^ step)
    own, other = composed(current, across_z, step), composed(across_x, across_both, step)
    whole = jnp.concatenate([jnp.where(side == 0, own, other), jnp.where(side == 0, other, own)], 2)
    return jnp.concatenate([whole[0:3], 1.0 - whole[3:4]], 0)


def solution(mesh):
    return jax.shard_map(
        local,
        mesh=mesh,
        in_specs=(P(None, "depth", "row", None), P(), P(), P(), P()),
        out_specs=P(None, "row", None),
        check_vma=False,
    )
```

```python
import functools

import jax
import jax.numpy as jnp
from jax import lax
from jax.experimental import pallas as pl
from jax.experimental.pallas import tpu as pltpu
from jax.sharding import PartitionSpec as P

FIELDS = 4
HALO = 6
LANES = 128
HIGHEST = lax.Precision.HIGHEST
F32 = jnp.float32
BF16 = jnp.bfloat16
depth_scale = 2.0
smooth_counts = (20.0, 15.0, 6.0, 1.0)
slope_counts = ((1, 45.0), (2, -9.0), (3, 1.0))


def dot(a, b, precision=None):
    return jnp.dot(a, b, preferred_element_type=F32, precision=precision)


def iota(shape, dim):
    return lax.broadcasted_iota(jnp.int32, shape, dim)


def smooth_count(distance):
    d = jnp.abs(distance)
    out = jnp.where(d == 0, smooth_counts[0], 0.0)
    for place in (1, 2, 3):
        out = jnp.where(d == place, smooth_counts[place], out)
    return out.astype(F32)


def split(x):
    high = x.astype(BF16)
    return high, (x - high.astype(F32)).astype(BF16)


def pack_kernel(fields, mine, theirs, straight, diagonal, left, right):
    side = lax.axis_index("depth") & 1
    layers, rows = fields.shape[1], fields.shape[2]
    kw, kh = layers * FIELDS, HALO * FIELDS
    pitch = left.shape[0] // rows
    for layer in range(layers):
        for field in range(FIELDS):
            plane = fields[field, layer].astype(F32)
            place = pl.ds(layer * FIELDS + field, rows, stride=pitch)
            left[place, :] = plane[:, :LANES]
            right[place, :] = plane[:, LANES:]
    lane = iota((kw, LANES), 1)
    shift = pl.multiple_of(side * (kw - kh), 8)

    def halves(row, start, count):
        a = left[pl.ds(row * pitch + start, count), :]
        b = right[pl.ds(row * pitch + start, count), :]
        return jnp.where(side == 0, a, b), jnp.where(side == 0, b, a)

    extra_low = jnp.zeros((kw, LANES), F32)
    extra_high = jnp.zeros((kw, LANES), F32)
    for row in range(0, rows, 2):
        pairs = []
        for r in (row, row + 1):
            a = left[pl.ds(r * pitch, kw), :]
            b = right[pl.ds(r * pitch, kw), :]
            inside = (lane >= 3 * r) & (lane < 3 * r + 3)
            extra_low = jnp.where(inside, pltpu.roll(b, (3 * r) % LANES, 1), extra_low)
            extra_high = jnp.where(inside, pltpu.roll(a, (3 * r + 3) % LANES, 1), extra_high)
            own = jnp.where(side == 0, a, b)
            other = jnp.where(side == 0, b, a)
            mine[pl.ds(r * kw, kw), :] = own.astype(BF16)
            theirs[pl.ds(r * kw, kw), :] = other.astype(BF16)
            pairs.append(halves(r, shift, kh))
        both = pl.ds(row * kh, 2 * kh)
        straight[both, :] = jnp.concatenate([pairs[0][0], pairs[1][0]], 0).astype(BF16)
        diagonal[both, :] = jnp.concatenate([pairs[0][1], pairs[1][1]], 0).astype(BF16)
    own = jnp.where(side == 0, extra_low, extra_high)
    other = jnp.where(side == 0, extra_high, extra_low)
    mine[rows * kw :, :] = own.astype(BF16)
    theirs[rows * kw :, :] = other.astype(BF16)
    empty = jnp.zeros((kw - kh, LANES), F32)
    for source, target in ((own, straight), (other, diagonal)):
        part = jnp.where(side == 0, source[:kh], source[kw - kh :])
        target[rows * kh :, :] = jnp.concatenate([part, empty], 0).astype(BF16)


def band_kernel(mine, swap, straight, diagonal, first, second):
    odd = lax.axis_index("row") & 1
    kw = 8 * FIELDS
    rows = mine.shape[0] // kw - 1
    for out, from_end in ((first, 1 - odd), (second, odd)):
        at, extra = 0, HALO * sum(r.shape[0] // (rows + 1) for r in (mine, swap)) + 2 * HALO * HALO * FIELDS
        for source in (mine, swap, straight, diagonal):
            width = kw if source.shape[0] == (rows + 1) * kw else HALO * FIELDS
            start = pl.multiple_of(from_end * (rows - HALO) * width, 16)
            out[at : at + HALO * width, :] = source[pl.ds(start, HALO * width), :]
            out[extra : extra + 32, :] = source[rows * width : rows * width + 32, :]
            at += HALO * width
            extra += 32


def tap_matrix():
    return smooth_count(iota((LANES, LANES), 0) - iota((LANES, LANES), 1)).astype(BF16)


def border(side, first, sign, low, high):
    i, j = iota((LANES, LANES), 0), iota((LANES, LANES), 1)
    spot = (j + jnp.where(side == 0, 3, 0)) & (LANES - 1)
    ir, ic, jr, jc = i // 3, i % 3, spot // 3, spot % 3
    apart = jnp.where(side == 0, ic - jc + 3, jc - ic + 3)
    here = (ir == first + sign * jr) & (jr >= low) & (jr < high)
    return jnp.where(here, smooth_count(apart), 0.0).astype(BF16)


def weights_kernel(w_in, b_in, w_out, b_out, w1, w2, filters, *, layers, rows, hidden, slabs):
    depth = lax.axis_index("depth")
    side = depth & 1
    flipped = (lax.axis_index("row") & 1) == 0
    sign = jnp.where(flipped, -1, 1)
    filters[0] = tap_matrix()
    filters[1] = border(side, jnp.where(flipped, rows + HALO - 1, -HALO), sign, HALO, rows + HALO)
    filters[2] = border(side, jnp.where(flipped, HALO - 1, rows - HALO), sign, 0, HALO)
    filters[3] = border(side, jnp.where(flipped, rows - 1, 0), sign, 0, HALO)
    base = (depth - side) * layers
    total = slabs * layers
    width = w1.shape[2]
    window = (layers + 2 * HALO) * FIELDS
    kinds = w_in.shape[1]
    row, col = iota((kinds, width), 0), iota((kinds, width), 1)
    within = col % (2 * window)
    field = col & 3
    ending = col >= 6 * window
    pick1 = jnp.where(ending, -1, jnp.where(within < window, field, field + 4))
    pick2 = jnp.where(ending | (within >= window), -1, field + 8)
    eye = iota((hidden, hidden), 0) == iota((hidden, hidden), 1)
    bias = jnp.sum(jnp.where(eye, b_in[...], 0.0), axis=1, keepdims=True)
    part1 = dot(w_in[...], (row == pick1).astype(F32), HIGHEST)
    part2 = dot(w_in[...], (row == pick2).astype(F32), HIGHEST)
    kappa = iota((hidden, width), 1)
    part1 = jnp.where(kappa == 6 * window, bias, jnp.where(kappa == 6 * window + 1, bias, part1))
    scale = 1.0 / 64.0**3
    row_sign = jnp.where(flipped, -1.0 / 60.0, 1.0 / 60.0)
    z, place = iota((layers, width), 0), iota((layers, width), 1)
    inner = place % (2 * window)
    slope_kind = inner >= window
    last = place >= 6 * window
    slot = jnp.where(slope_kind, inner - window, inner) >> 2
    low_column = ((place >= 2 * window) & (place < 4 * window)) | (place == 6 * window + 1)
    for half in range(2):
        distance = slot - HALO - z
        center = smooth_count(distance) * scale
        slope = jnp.zeros((layers, width), F32)
        for offset, count in slope_counts:
            for sign in (1, -1):
                at = base + half * layers + z + sign * offset
                inside = ((at >= 0) & (at < total)).astype(F32)
                slope = slope + (inside * (sign * count)) * smooth_count(distance - sign * offset)
        center = jnp.where(last, 1.0, jnp.where(slope_kind, center * row_sign, center))
        product = center[None] * part1[:, None, :] + (slope * (scale / 60.0))[None] * part2[:, None, :]
        high = product.astype(BF16).astype(F32)
        chosen = jnp.where(low_column[None], product - high, high)
        w1[half] = chosen.reshape(hidden * layers, width).astype(BF16)
    outs = w_out.shape[0]
    for c in range(outs):
        values = jnp.sum(jnp.where(eye, w_out[c : c + 1, :], 0.0), axis=1, keepdims=True)
        factor = 0.5 if c < 3 else 1.0
        w2[c * hidden : (c + 1) * hidden, :] = jnp.broadcast_to(factor * values, (hidden, LANES))
    pick = iota((8, outs), 0) == iota((8, outs), 1)
    values = jnp.sum(jnp.where(pick, b_out[...], 0.0), axis=1, keepdims=True)
    values = jnp.where(iota((8, 1), 0) < 3, 0.5 * values, values)
    w2[outs * hidden :, :] = jnp.broadcast_to(values, (8, LANES))


def places(side, layers):
    kw, kh = layers * FIELDS, HALO * FIELDS
    far = kh + 2 * kw
    return ((kh + side * kw, kw), (kh + (1 - side) * kw, kw), ((1 - side) * far, kh), (side * far, kh))


def place_halo(halo, grid, edge, layers, side, flipped, taps, edges):
    kk = 2 * (layers + HALO) * FIELDS
    filtered = dot(halo[0 : HALO * kk, :], taps)
    added = dot(halo[HALO * kk :, :], edges)
    start = 0
    for index, (at, width) in enumerate(places(side, layers)):
        at = pl.ds(pl.multiple_of(at, 8), width)
        for row in range(HALO):
            grid[jnp.where(flipped, HALO - 1 - row, row), at, :] = filtered[start : start + width]
            start += width
        edge[at, :] = added[index * 32 : index * 32 + width]


def near_cut(side):
    return ((iota((16, LANES), 1) + jnp.where(side == 0, 3, 0)) & (LANES - 1)) < 3


def next_row(value, chain, ring, scale=None):
    for level in range(6):
        previous, chain[level] = chain[level], value
        if previous is None:
            return None
        value = previous + value
    if scale is not None:
        value = value * scale
    ring.append(value)
    if len(ring) < 7:
        return None
    slope = (ring[6] - ring[0]) - 9.0 * (ring[5] - ring[1]) + 45.0 * (ring[4] - ring[2])
    center = ring[3]
    ring.pop(0)
    return center, slope


def keep(kept, y, at, center, slope):
    kept[0, y, at, :], kept[2, y, at, :] = split(center)
    kept[1, y, at, :], kept[3, y, at, :] = split(slope)


def shade_rows(kept, w1, w2, out, layers, first, flipped, last):
    kw, kh = layers * FIELDS, HALO * FIELDS
    wide = 2 * LANES
    window = kw + 2 * kh
    hidden = w1.shape[1] // layers
    rest = w1.shape[2] - 6 * window
    ones = jnp.where(iota((rest, wide), 0) < 2, 1.0, 0.0).astype(BF16)
    sub = iota((layers, wide), 0)
    scale = depth_scale / (lax.axis_size("depth") * layers)

    def splat(index):
        line = w2[index : index + 1, :]
        return jnp.broadcast_to(jnp.concatenate([line, line], 1), (layers, wide))

    def target(k):
        return pl.ds(jnp.where(flipped, last - first - k, first + k), 1)

    for y in range(0, kept.shape[1], 2):
        total = jnp.zeros((1, wide), F32)
        front = jnp.ones((1, wide), F32)
        color = [jnp.zeros((layers, wide), F32) for unused in range(3)]
        for half in range(2):
            at = pl.ds(half * kw, window)
            c_high, s_high, c_low, s_low = [
                jnp.concatenate([kept[k, y, at, :], kept[k, y + 1, at, :]], 1) for k in range(4)
            ]
            stacked = jnp.concatenate([c_high, s_high, c_high, s_high, c_low, s_low, ones], 0)
            units = jnp.tanh(dot(w1[half], stacked))
            o = [splat(4 * hidden + c) for c in range(4)]
            for h in range(hidden):
                unit = units[h * layers : (h + 1) * layers]
                for c in range(4):
                    o[c] = o[c] + splat(c * hidden + h) * unit
            x = o[3]
            optical = (jnp.maximum(x, 0.0) + jnp.log(1.0 + jnp.exp(-jnp.abs(x)))) * scale
            through = optical
            for step in (1, 2, 4):
                through = through + jnp.where(sub >= step, pltpu.roll(through, step, 0), 0.0)
            through = through + total
            total = through[layers - 1 :]
            after = jnp.exp(-through)
            before = jnp.where(sub == 0, front, pltpu.roll(after, 1, 0))
            front = after[layers - 1 :]
            weight = before - after
            for c in range(3):
                color[c] = color[c] + weight * jnp.tanh(o[c])
        lines = [0.5 * (1.0 - front + jnp.sum(color[c], axis=0, keepdims=True)) for c in range(3)]
        for c, line in enumerate(lines + [front]):
            out[c, target(y), :] = line[:, :LANES]
            out[c, target(y + 1), :] = line[:, LANES:]


def most_kernel(mine, swap, straight, diagonal, halo, w1, w2, filters, out, state, grid, edge, kept, *, layers, rows):
    side = lax.axis_index("depth") & 1
    flipped = (lax.axis_index("row") & 1) == 0
    kk = 2 * (layers + HALO) * FIELDS
    taps, own_border = filters[0], filters[1]
    place_halo(halo, grid, edge.at[1], layers, side, flipped, taps, filters[2])
    for source, (at, width) in zip((mine, swap, straight, diagonal), places(side, layers)):
        at = pl.ds(pl.multiple_of(at, 8), width)
        filtered = dot(source[0 : rows * width, :], taps)
        for row in range(rows):
            place = jnp.where(flipped, rows + HALO - 1 - row, row + HALO)
            grid[place, at, :] = filtered[row * width : (row + 1) * width]
        edge[0, at, :] = dot(source[rows * width : rows * width + 32, :], own_border)[:width]
    near = near_cut(side)

    def filter_rows(group, carry):
        at = pl.ds(pl.multiple_of(group * 16, 16), 16)
        edges = edge[1, at, :], edge[0, at, :]
        chain, ring = [None] * 6, []
        for r in range(rows + HALO):
            turned = pltpu.roll(edges[r >= HALO], (-3 * r) % LANES, 1)
            given = next_row(grid[r, at, :] + jnp.where(near, turned, 0.0), chain, ring)
            if given is not None:
                keep(kept, r - 2 * HALO, at, *given)
        for index, value in enumerate(chain + ring):
            state[index, at, :] = value
        return carry

    lax.fori_loop(0, kk // 16, filter_rows, 0, unroll=kk // 16)
    shade_rows(kept, w1, w2, out, layers, 0, flipped, rows - 1)


def rest_kernel(halo, w1, w2, filters, state, done, out, grid, edge, kept, *, layers, rows):
    out[...] = done[...]
    side = lax.axis_index("depth") & 1
    band = lax.axis_index("row")
    flipped = (band & 1) == 0
    kk = 2 * (layers + HALO) * FIELDS
    place_halo(halo, grid, edge, layers, side, flipped, filters[0], filters[3])
    near = near_cut(side)
    outside = jnp.where(flipped, band == 0, band == lax.axis_size("row") - 1)
    inside = jnp.where(outside, 0.0, 1.0)

    def filter_rows(group, carry):
        at = pl.ds(pl.multiple_of(group * 16, 16), 16)
        edges = edge[at, :]
        values = [state[index, at, :] for index in range(12)]
        chain, ring = values[:6], values[6:]
        for r in range(HALO):
            turned = pltpu.roll(edges, (-3 * r) % LANES, 1)
            value = grid[r, at, :] + jnp.where(near, turned, 0.0)
            keep(kept, r, at, *next_row(value, chain, ring, inside if r >= 3 else None))
        return carry

    lax.fori_loop(0, kk // 16, filter_rows, 0, unroll=kk // 16)
    shade_rows(kept, w1, w2, out, layers, rows - HALO, flipped, rows - 1)


def call(kernel, out_shape, operands, scratch=(), flops=0, name=None):
    vmem = pl.BlockSpec(memory_space=pltpu.VMEM)
    return pl.pallas_call(
        kernel,
        out_shape=out_shape,
        in_specs=[vmem] * len(operands),
        out_specs=jax.tree.map(lambda unused: vmem, out_shape),
        scratch_shapes=list(scratch),
        compiler_params=pltpu.CompilerParams(vmem_limit_bytes=40 * 2**20),
        cost_estimate=pl.CostEstimate(flops=flops, bytes_accessed=2**20, transcendentals=0),
        name=name,
    )(*operands)


def combine(front, back):
    color = front[0:3] + front[3:4] * back[0:3]
    return jnp.concatenate([color, front[3:4] * back[3:4]], 0)


def local(fields, w_in, b_in, w_out, b_out):
    layers, rows, columns = fields.shape[1:]
    hidden = w_in.shape[0]
    slabs = lax.axis_size("depth")
    bands = lax.axis_size("row")
    me = lax.axis_index("depth")
    side = me & 1
    kw, kh = layers * FIELDS, HALO * FIELDS
    kk = 2 * (kw + kh)
    shape = jax.ShapeDtypeStruct
    mine, theirs, own_halo, other_halo = call(
        pack_kernel,
        [
            shape(((rows + 1) * kw, LANES), BF16),
            shape(((rows + 1) * kw, LANES), BF16),
            shape((rows * kh + kw, LANES), BF16),
            shape((rows * kh + kw, LANES), BF16),
        ],
        (fields,),
        [pltpu.VMEM((rows * (kw + 4), LANES), F32)] * 2,
        name="pack",
    )
    swap_pairs = [(i, i ^ 1) for i in range(slabs)]
    odd, even = range(1, slabs, 2), range(0, slabs, 2)
    diagonal_pairs = [(i, i + 1) for i in odd if i + 1 < slabs] + [(i, i - 1) for i in even if i]
    straight_pairs = [(i, i + 2) for i in odd if i + 2 < slabs] + [(i, i - 2) for i in even if i]
    swap = lax.ppermute(theirs, "depth", swap_pairs)
    diagonal = lax.ppermute(other_halo, "depth", diagonal_pairs)
    straight = lax.ppermute(own_halo, "depth", straight_pairs)
    swap, diagonal, straight = lax.optimization_barrier((swap, diagonal, straight))

    width = -(-(6 * (kw + 2 * kh) + 2) // 256) * 256
    w1, w2, filters = call(
        functools.partial(weights_kernel, layers=layers, rows=rows, hidden=hidden, slabs=slabs),
        [
            shape((2, layers * hidden, width), BF16),
            shape((4 * hidden + 8, LANES), F32),
            shape((4, LANES, LANES), BF16),
        ],
        (w_in, b_in[None], w_out, b_out[None]),
        flops=10**8,
        name="weights",
    )
    mine, w1, w2, filters = lax.optimization_barrier((mine, w1, w2, filters))
    message = shape((HALO * kk + 4 * 32, LANES), BF16)
    first, second = call(band_kernel, [message, message], (mine, swap, straight, diagonal), name="band")
    within = [(i, i ^ 1) for i in range(bands)]
    across = [(i, i + 1) for i in range(1, bands - 1, 2)] + [(i + 1, i) for i in range(1, bands - 1, 2)]
    second = lax.ppermute(second, "row", across)
    first = lax.ppermute(first, "row", within)

    image = shape((4, rows, LANES), F32)
    current, state = call(
        functools.partial(most_kernel, layers=layers, rows=rows),
        [image, shape((12, kk, LANES), F32)],
        (mine, swap, straight, diagonal, first, w1, w2, filters),
        [
            pltpu.VMEM((rows + HALO, kk, LANES), F32),
            pltpu.VMEM((2, kk, LANES), F32),
            pltpu.VMEM((4, rows - HALO, kk, LANES), BF16),
        ],
        flops=10**10,
        name="shade_most",
    )
    current = call(
        functools.partial(rest_kernel, layers=layers, rows=rows),
        image,
        (second, w1, w2, filters, state, current),
        [
            pltpu.VMEM((HALO, kk, LANES), F32),
            pltpu.VMEM((kk, LANES), F32),
            pltpu.VMEM((4, HALO, kk, LANES), BF16),
        ],
        flops=10**9,
        name="shade_rest",
    )
    def exchanged(distance):
        return lax.ppermute(current, "depth", [(i, i ^ distance) for i in range(slabs)])

    def composed(own, received, step):
        behind = (me & step) != 0
        return combine(jnp.where(behind, received, own), jnp.where(behind, own, received))

    step = 2
    while 2 * step < slabs:
        current = composed(current, exchanged(step), step)
        step *= 2
    across_x, across_z, across_both = exchanged(1), exchanged(step), exchanged(1 ^ step)
    own, other = composed(current, across_z, step), composed(across_x, across_both, step)
    whole = jnp.concatenate([jnp.where(side == 0, own, other), jnp.where(side == 0, other, own)], 2)
    return jnp.concatenate([whole[0:3], 1.0 - whole[3:4]], 0)


def solution(mesh):
    return jax.shard_map(
        local,
        mesh=mesh,
        in_specs=(P(None, "depth", "row", None), P(), P(), P(), P()),
        out_specs=P(None, "row", None),
        check_vma=False,
    )
```

```python
import functools

import jax
import jax.numpy as jnp
from jax import lax
from jax.experimental import pallas as pl
from jax.experimental.pallas import tpu as pltpu
from jax.sharding import PartitionSpec as P

FIELDS = 4
HALO = 6
LANES = 128
HIGHEST = lax.Precision.HIGHEST
F32 = jnp.float32
BF16 = jnp.bfloat16
depth_scale = 2.0
smooth_counts = (20.0, 15.0, 6.0, 1.0)
slope_counts = ((1, 45.0), (2, -9.0), (3, 1.0))


def dot(a, b, precision=None):
    return jnp.dot(a, b, preferred_element_type=F32, precision=precision)


def iota(shape, dim):
    return lax.broadcasted_iota(jnp.int32, shape, dim)


def smooth_count(distance):
    d = jnp.abs(distance)
    out = jnp.where(d == 0, smooth_counts[0], 0.0)
    for place in (1, 2, 3):
        out = jnp.where(d == place, smooth_counts[place], out)
    return out.astype(F32)


def split(x):
    high = x.astype(BF16)
    return high, (x - high.astype(F32)).astype(BF16)


def pack_kernel(fields, mine, theirs, straight, diagonal, left, right):
    side = lax.axis_index("depth") & 1
    layers, rows = fields.shape[1], fields.shape[2]
    kw, kh = layers * FIELDS, HALO * FIELDS
    pitch = left.shape[0] // rows
    for layer in range(layers):
        for field in range(FIELDS):
            plane = fields[field, layer].astype(F32)
            place = pl.ds(layer * FIELDS + field, rows, stride=pitch)
            left[place, :] = plane[:, :LANES]
            right[place, :] = plane[:, LANES:]
    lane = iota((kw, LANES), 1)
    shift = pl.multiple_of(side * (kw - kh), 8)

    def halves(row, start, count):
        a = left[pl.ds(row * pitch + start, count), :]
        b = right[pl.ds(row * pitch + start, count), :]
        return jnp.where(side == 0, a, b), jnp.where(side == 0, b, a)

    extra_low = jnp.zeros((kw, LANES), F32)
    extra_high = jnp.zeros((kw, LANES), F32)
    for row in range(0, rows, 2):
        pairs = []
        for r in (row, row + 1):
            a = left[pl.ds(r * pitch, kw), :]
            b = right[pl.ds(r * pitch, kw), :]
            inside = (lane >= 3 * r) & (lane < 3 * r + 3)
            extra_low = jnp.where(inside, pltpu.roll(b, (3 * r) % LANES, 1), extra_low)
            extra_high = jnp.where(inside, pltpu.roll(a, (3 * r + 3) % LANES, 1), extra_high)
            own = jnp.where(side == 0, a, b)
            other = jnp.where(side == 0, b, a)
            mine[pl.ds(r * kw, kw), :] = own.astype(BF16)
            theirs[pl.ds(r * kw, kw), :] = other.astype(BF16)
            pairs.append(halves(r, shift, kh))
        both = pl.ds(row * kh, 2 * kh)
        straight[both, :] = jnp.concatenate([pairs[0][0], pairs[1][0]], 0).astype(BF16)
        diagonal[both, :] = jnp.concatenate([pairs[0][1], pairs[1][1]], 0).astype(BF16)
    own = jnp.where(side == 0, extra_low, extra_high)
    other = jnp.where(side == 0, extra_high, extra_low)
    mine[rows * kw :, :] = own.astype(BF16)
    theirs[rows * kw :, :] = other.astype(BF16)
    empty = jnp.zeros((kw - kh, LANES), F32)
    for source, target in ((own, straight), (other, diagonal)):
        part = jnp.where(side == 0, source[:kh], source[kw - kh :])
        target[rows * kh :, :] = jnp.concatenate([part, empty], 0).astype(BF16)


def band_kernel(mine, swap, straight, diagonal, first, second):
    odd = lax.axis_index("row") & 1
    kw = 8 * FIELDS
    rows = mine.shape[0] // kw - 1
    for out, from_end in ((first, 1 - odd), (second, odd)):
        at, extra = 0, HALO * sum(r.shape[0] // (rows + 1) for r in (mine, swap)) + 2 * HALO * HALO * FIELDS
        for source in (mine, swap, straight, diagonal):
            width = kw if source.shape[0] == (rows + 1) * kw else HALO * FIELDS
            start = pl.multiple_of(from_end * (rows - HALO) * width, 16)
            out[at : at + HALO * width, :] = source[pl.ds(start, HALO * width), :]
            out[extra : extra + 32, :] = source[rows * width : rows * width + 32, :]
            at += HALO * width
            extra += 32


def tap_matrix():
    return smooth_count(iota((LANES, LANES), 0) - iota((LANES, LANES), 1)).astype(BF16)


def border(side, first, sign, low, high):
    i, j = iota((LANES, LANES), 0), iota((LANES, LANES), 1)
    spot = (j + jnp.where(side == 0, 3, 0)) & (LANES - 1)
    ir, ic, jr, jc = i // 3, i % 3, spot // 3, spot % 3
    apart = jnp.where(side == 0, ic - jc + 3, jc - ic + 3)
    here = (ir == first + sign * jr) & (jr >= low) & (jr < high)
    return jnp.where(here, smooth_count(apart), 0.0).astype(BF16)


def weights_kernel(w_in, b_in, w_out, b_out, w1, w2, filters, *, layers, rows, hidden, slabs):
    depth = lax.axis_index("depth")
    side = depth & 1
    flipped = (lax.axis_index("row") & 1) == 0
    sign = jnp.where(flipped, -1, 1)
    filters[0] = tap_matrix()
    filters[1] = border(side, jnp.where(flipped, rows + HALO - 1, -HALO), sign, HALO, rows + HALO)
    filters[2] = border(side, jnp.where(flipped, HALO - 1, rows - HALO), sign, 0, HALO)
    filters[3] = border(side, jnp.where(flipped, rows - 1, 0), sign, 0, HALO)
    base = (depth - side) * layers
    total = slabs * layers
    width = w1.shape[2]
    window = (layers + 2 * HALO) * FIELDS
    kinds = w_in.shape[1]
    row, col = iota((kinds, width), 0), iota((kinds, width), 1)
    within = col % (2 * window)
    field = col & 3
    ending = col >= 6 * window
    pick1 = jnp.where(ending, -1, jnp.where(within < window, field, field + 4))
    pick2 = jnp.where(ending | (within >= window), -1, field + 8)
    eye = iota((hidden, hidden), 0) == iota((hidden, hidden), 1)
    bias = jnp.sum(jnp.where(eye, b_in[...], 0.0), axis=1, keepdims=True)
    part1 = dot(w_in[...], (row == pick1).astype(F32), HIGHEST)
    part2 = dot(w_in[...], (row == pick2).astype(F32), HIGHEST)
    kappa = iota((hidden, width), 1)
    part1 = jnp.where(kappa == 6 * window, bias, jnp.where(kappa == 6 * window + 1, bias, part1))
    scale = 1.0 / 64.0**3
    row_sign = jnp.where(flipped, -1.0 / 60.0, 1.0 / 60.0)
    z, place = iota((layers, width), 0), iota((layers, width), 1)
    inner = place % (2 * window)
    slope_kind = inner >= window
    last = place >= 6 * window
    slot = jnp.where(slope_kind, inner - window, inner) >> 2
    low_column = ((place >= 2 * window) & (place < 4 * window)) | (place == 6 * window + 1)
    for half in range(2):
        distance = slot - HALO - z
        center = smooth_count(distance) * scale
        slope = jnp.zeros((layers, width), F32)
        for offset, count in slope_counts:
            for sign in (1, -1):
                at = base + half * layers + z + sign * offset
                inside = ((at >= 0) & (at < total)).astype(F32)
                slope = slope + (inside * (sign * count)) * smooth_count(distance - sign * offset)
        center = jnp.where(last, 1.0, jnp.where(slope_kind, center * row_sign, center))
        product = center[None] * part1[:, None, :] + (slope * (scale / 60.0))[None] * part2[:, None, :]
        high = product.astype(BF16).astype(F32)
        chosen = jnp.where(low_column[None], product - high, high)
        w1[half] = chosen.reshape(hidden * layers, width).astype(BF16)
    outs = w_out.shape[0]
    for c in range(outs):
        values = jnp.sum(jnp.where(eye, w_out[c : c + 1, :], 0.0), axis=1, keepdims=True)
        factor = 0.5 if c < 3 else 1.0
        w2[c * hidden : (c + 1) * hidden, :] = jnp.broadcast_to(factor * values, (hidden, LANES))
    pick = iota((8, outs), 0) == iota((8, outs), 1)
    values = jnp.sum(jnp.where(pick, b_out[...], 0.0), axis=1, keepdims=True)
    values = jnp.where(iota((8, 1), 0) < 3, 0.5 * values, values)
    w2[outs * hidden :, :] = jnp.broadcast_to(values, (8, LANES))


def places(side, layers):
    kw, kh = layers * FIELDS, HALO * FIELDS
    far = kh + 2 * kw
    return ((kh + side * kw, kw), (kh + (1 - side) * kw, kw), ((1 - side) * far, kh), (side * far, kh))


def place_halo(halo, grid, edge, layers, side, flipped, taps, edges):
    kk = 2 * (layers + HALO) * FIELDS
    filtered = dot(halo[0 : HALO * kk, :], taps)
    added = dot(halo[HALO * kk :, :], edges)
    start = 0
    for index, (at, width) in enumerate(places(side, layers)):
        at = pl.ds(pl.multiple_of(at, 8), width)
        for row in range(HALO):
            grid[jnp.where(flipped, HALO - 1 - row, row), at, :] = filtered[start : start + width]
            start += width
        edge[at, :] = added[index * 32 : index * 32 + width]


def near_cut(side):
    return ((iota((16, LANES), 1) + jnp.where(side == 0, 3, 0)) & (LANES - 1)) < 3


def next_row(value, chain, ring, scale=None):
    for level in range(6):
        previous, chain[level] = chain[level], value
        if previous is None:
            return None
        value = previous + value
    if scale is not None:
        value = value * scale
    ring.append(value)
    if len(ring) < 7:
        return None
    slope = (ring[6] - ring[0]) - 9.0 * (ring[5] - ring[1]) + 45.0 * (ring[4] - ring[2])
    center = ring[3]
    ring.pop(0)
    return center, slope


def keep(kept, y, at, center, slope):
    kept[0, y, at, :], kept[2, y, at, :] = split(center)
    kept[1, y, at, :], kept[3, y, at, :] = split(slope)


def shade_rows(kept, w1, w2, out, layers, first, flipped, last):
    kw, kh = layers * FIELDS, HALO * FIELDS
    wide = 2 * LANES
    window = kw + 2 * kh
    hidden = w1.shape[1] // layers
    rest = w1.shape[2] - 6 * window
    ones = jnp.where(iota((rest, wide), 0) < 2, 1.0, 0.0).astype(BF16)
    sub = iota((layers, wide), 0)
    scale = depth_scale / (lax.axis_size("depth") * layers)

    def splat(index):
        line = w2[index : index + 1, :]
        return jnp.broadcast_to(jnp.concatenate([line, line], 1), (layers, wide))

    def target(k):
        return pl.ds(jnp.where(flipped, last - first - k, first + k), 1)

    for y in range(0, kept.shape[1], 2):
        total = jnp.zeros((1, wide), F32)
        front = jnp.ones((1, wide), F32)
        color = [jnp.zeros((layers, wide), F32) for unused in range(3)]
        for half in range(2):
            at = pl.ds(half * kw, window)
            c_high, s_high, c_low, s_low = [
                jnp.concatenate([kept[k, y, at, :], kept[k, y + 1, at, :]], 1) for k in range(4)
            ]
            stacked = jnp.concatenate([c_high, s_high, c_high, s_high, c_low, s_low, ones], 0)
            units = jnp.tanh(dot(w1[half], stacked))
            o = [splat(4 * hidden + c) for c in range(4)]
            for h in range(hidden):
                unit = units[h * layers : (h + 1) * layers]
                for c in range(4):
                    o[c] = o[c] + splat(c * hidden + h) * unit
            x = o[3]
            optical = (jnp.maximum(x, 0.0) + jnp.log(1.0 + jnp.exp(-jnp.abs(x)))) * scale
            through = optical
            for step in (1, 2, 4):
                through = through + jnp.where(sub >= step, pltpu.roll(through, step, 0), 0.0)
            through = through + total
            total = through[layers - 1 :]
            after = jnp.exp(-through)
            before = jnp.where(sub == 0, front, pltpu.roll(after, 1, 0))
            front = after[layers - 1 :]
            weight = before - after
            for c in range(3):
                color[c] = color[c] + weight * jnp.tanh(o[c])
        lines = [0.5 * (1.0 - front + jnp.sum(color[c], axis=0, keepdims=True)) for c in range(3)]
        for c, line in enumerate(lines + [front]):
            out[c, target(y), :] = line[:, :LANES]
            out[c, target(y + 1), :] = line[:, LANES:]


def filter_kernel(mine, swap, straight, diagonal, filters, grid, edge, *, layers, rows):
    side = lax.axis_index("depth") & 1
    flipped = (lax.axis_index("row") & 1) == 0
    for source, (at, width) in zip((mine, swap, straight, diagonal), places(side, layers)):
        at = pl.ds(pl.multiple_of(at, 8), width)
        filtered = dot(source[0 : rows * width, :], filters[0])
        for row in range(rows):
            grid[jnp.where(flipped, rows - 1 - row, row), at, :] = filtered[row * width : (row + 1) * width]
        edge[at, :] = dot(source[rows * width : rows * width + 32, :], filters[1])[:width]


def most_kernel(own_grid, own_edge, halo, w1, w2, filters, out, state, grid, edge, kept, *, layers, rows):
    side = lax.axis_index("depth") & 1
    flipped = (lax.axis_index("row") & 1) == 0
    kk = 2 * (layers + HALO) * FIELDS
    place_halo(halo, grid, edge, layers, side, flipped, filters[0], filters[2])
    near = near_cut(side)

    def filter_rows(group, carry):
        at = pl.ds(pl.multiple_of(group * 16, 16), 16)
        halo_edge, edges = edge[at, :], own_edge[at, :]
        chain, ring = [None] * 6, []
        for r in range(rows + HALO):
            turned = pltpu.roll(halo_edge if r < HALO else edges, (-3 * r) % LANES, 1)
            value = grid[r, at, :] if r < HALO else own_grid[r - HALO, at, :]
            given = next_row(value + jnp.where(near, turned, 0.0), chain, ring)
            if given is not None:
                keep(kept, r - 2 * HALO, at, *given)
        for index, value in enumerate(chain + ring):
            state[index, at, :] = value
        return carry

    lax.fori_loop(0, kk // 16, filter_rows, 0, unroll=kk // 16)
    shade_rows(kept, w1, w2, out, layers, 0, flipped, rows - 1)


def rest_kernel(halo, w1, w2, filters, state, done, out, grid, edge, kept, *, layers, rows):
    out[...] = done[...]
    side = lax.axis_index("depth") & 1
    band = lax.axis_index("row")
    flipped = (band & 1) == 0
    kk = 2 * (layers + HALO) * FIELDS
    place_halo(halo, grid, edge, layers, side, flipped, filters[0], filters[3])
    near = near_cut(side)
    outside = jnp.where(flipped, band == 0, band == lax.axis_size("row") - 1)
    inside = jnp.where(outside, 0.0, 1.0)

    def filter_rows(group, carry):
        at = pl.ds(pl.multiple_of(group * 16, 16), 16)
        edges = edge[at, :]
        values = [state[index, at, :] for index in range(12)]
        chain, ring = values[:6], values[6:]
        for r in range(HALO):
            turned = pltpu.roll(edges, (-3 * r) % LANES, 1)
            value = grid[r, at, :] + jnp.where(near, turned, 0.0)
            keep(kept, r, at, *next_row(value, chain, ring, inside if r >= 3 else None))
        return carry

    lax.fori_loop(0, kk // 16, filter_rows, 0, unroll=kk // 16)
    shade_rows(kept, w1, w2, out, layers, rows - HALO, flipped, rows - 1)


def call(kernel, out_shape, operands, scratch=(), flops=0, name=None):
    vmem = pl.BlockSpec(memory_space=pltpu.VMEM)
    return pl.pallas_call(
        kernel,
        out_shape=out_shape,
        in_specs=[vmem] * len(operands),
        out_specs=jax.tree.map(lambda unused: vmem, out_shape),
        scratch_shapes=list(scratch),
        compiler_params=pltpu.CompilerParams(vmem_limit_bytes=40 * 2**20),
        cost_estimate=pl.CostEstimate(flops=flops, bytes_accessed=2**20, transcendentals=0),
        name=name,
    )(*operands)


def combine(front, back):
    color = front[0:3] + front[3:4] * back[0:3]
    return jnp.concatenate([color, front[3:4] * back[3:4]], 0)


def local(fields, w_in, b_in, w_out, b_out):
    layers, rows, columns = fields.shape[1:]
    hidden = w_in.shape[0]
    slabs = lax.axis_size("depth")
    bands = lax.axis_size("row")
    me = lax.axis_index("depth")
    side = me & 1
    kw, kh = layers * FIELDS, HALO * FIELDS
    kk = 2 * (kw + kh)
    shape = jax.ShapeDtypeStruct
    mine, theirs, own_halo, other_halo = call(
        pack_kernel,
        [
            shape(((rows + 1) * kw, LANES), BF16),
            shape(((rows + 1) * kw, LANES), BF16),
            shape((rows * kh + kw, LANES), BF16),
            shape((rows * kh + kw, LANES), BF16),
        ],
        (fields,),
        [pltpu.VMEM((rows * (kw + 4), LANES), F32)] * 2,
        name="pack",
    )
    swap_pairs = [(i, i ^ 1) for i in range(slabs)]
    odd, even = range(1, slabs, 2), range(0, slabs, 2)
    diagonal_pairs = [(i, i + 1) for i in odd if i + 1 < slabs] + [(i, i - 1) for i in even if i]
    straight_pairs = [(i, i + 2) for i in odd if i + 2 < slabs] + [(i, i - 2) for i in even if i]
    swap = lax.ppermute(theirs, "depth", swap_pairs)
    diagonal = lax.ppermute(other_halo, "depth", diagonal_pairs)
    straight = lax.ppermute(own_halo, "depth", straight_pairs)
    swap, diagonal, straight = lax.optimization_barrier((swap, diagonal, straight))

    width = -(-(6 * (kw + 2 * kh) + 2) // 256) * 256
    w1, w2, filters = call(
        functools.partial(weights_kernel, layers=layers, rows=rows, hidden=hidden, slabs=slabs),
        [
            shape((2, layers * hidden, width), BF16),
            shape((4 * hidden + 8, LANES), F32),
            shape((4, LANES, LANES), BF16),
        ],
        (w_in, b_in[None], w_out, b_out[None]),
        flops=10**8,
        name="weights",
    )
    mine, w1, w2, filters = lax.optimization_barrier((mine, w1, w2, filters))
    message = shape((HALO * kk + 4 * 32, LANES), BF16)
    first, second = call(band_kernel, [message, message], (mine, swap, straight, diagonal), name="band")
    within = [(i, i ^ 1) for i in range(bands)]
    across = [(i, i + 1) for i in range(1, bands - 1, 2)] + [(i + 1, i) for i in range(1, bands - 1, 2)]
    second = lax.ppermute(second, "row", across)
    first = lax.ppermute(first, "row", within)

    own_grid, own_edge = call(
        functools.partial(filter_kernel, layers=layers, rows=rows),
        [shape((rows, kk, LANES), F32), shape((kk, LANES), F32)],
        (mine, swap, straight, diagonal, filters),
        flops=10**9,
        name="filter",
    )
    image = shape((4, rows, LANES), F32)
    current, state = call(
        functools.partial(most_kernel, layers=layers, rows=rows),
        [image, shape((12, kk, LANES), F32)],
        (own_grid, own_edge, first, w1, w2, filters),
        [
            pltpu.VMEM((HALO, kk, LANES), F32),
            pltpu.VMEM((kk, LANES), F32),
            pltpu.VMEM((4, rows - HALO, kk, LANES), BF16),
        ],
        flops=10**10,
        name="shade_most",
    )
    current = call(
        functools.partial(rest_kernel, layers=layers, rows=rows),
        image,
        (second, w1, w2, filters, state, current),
        [
            pltpu.VMEM((HALO, kk, LANES), F32),
            pltpu.VMEM((kk, LANES), F32),
            pltpu.VMEM((4, HALO, kk, LANES), BF16),
        ],
        flops=10**9,
        name="shade_rest",
    )
    def exchanged(distance):
        return lax.ppermute(current, "depth", [(i, i ^ distance) for i in range(slabs)])

    def composed(own, received, step):
        behind = (me & step) != 0
        return combine(jnp.where(behind, received, own), jnp.where(behind, own, received))

    step = 2
    while 2 * step < slabs:
        current = composed(current, exchanged(step), step)
        step *= 2
    across_x, across_z, across_both = exchanged(1), exchanged(step), exchanged(1 ^ step)
    own, other = composed(current, across_z, step), composed(across_x, across_both, step)
    whole = jnp.concatenate([jnp.where(side == 0, own, other), jnp.where(side == 0, other, own)], 2)
    return jnp.concatenate([whole[0:3], 1.0 - whole[3:4]], 0)


def solution(mesh):
    return jax.shard_map(
        local,
        mesh=mesh,
        in_specs=(P(None, "depth", "row", None), P(), P(), P(), P()),
        out_specs=P(None, "row", None),
        check_vma=False,
    )
```

```python
import functools

import jax
import jax.numpy as jnp
from jax import lax
from jax.experimental import pallas as pl
from jax.experimental.pallas import tpu as pltpu
from jax.sharding import PartitionSpec as P

FIELDS = 4
HALO = 6
LANES = 128
HIGHEST = lax.Precision.HIGHEST
F32 = jnp.float32
BF16 = jnp.bfloat16
depth_scale = 2.0
smooth_counts = (20.0, 15.0, 6.0, 1.0)
slope_counts = ((1, 45.0), (2, -9.0), (3, 1.0))


def dot(a, b, precision=None):
    return jnp.dot(a, b, preferred_element_type=F32, precision=precision)


def iota(shape, dim):
    return lax.broadcasted_iota(jnp.int32, shape, dim)


def smooth_count(distance):
    d = jnp.abs(distance)
    out = jnp.where(d == 0, smooth_counts[0], 0.0)
    for place in (1, 2, 3):
        out = jnp.where(d == place, smooth_counts[place], out)
    return out.astype(F32)


def split(x):
    high = x.astype(BF16)
    return high, (x - high.astype(F32)).astype(BF16)


def pack_kernel(fields, mine, theirs, straight, diagonal, left, right):
    side = lax.axis_index("depth") & 1
    layers, rows = fields.shape[1], fields.shape[2]
    kw, kh = layers * FIELDS, HALO * FIELDS
    pitch = left.shape[0] // rows
    for layer in range(layers):
        for field in range(FIELDS):
            plane = fields[field, layer].astype(F32)
            place = pl.ds(layer * FIELDS + field, rows, stride=pitch)
            left[place, :] = plane[:, :LANES]
            right[place, :] = plane[:, LANES:]
    lane = iota((kw, LANES), 1)
    shift = pl.multiple_of(side * (kw - kh), 8)

    def halves(row, start, count):
        a = left[pl.ds(row * pitch + start, count), :]
        b = right[pl.ds(row * pitch + start, count), :]
        return jnp.where(side == 0, a, b), jnp.where(side == 0, b, a)

    extra_low = jnp.zeros((kw, LANES), F32)
    extra_high = jnp.zeros((kw, LANES), F32)
    for row in range(0, rows, 2):
        pairs = []
        for r in (row, row + 1):
            a = left[pl.ds(r * pitch, kw), :]
            b = right[pl.ds(r * pitch, kw), :]
            inside = (lane >= 3 * r) & (lane < 3 * r + 3)
            extra_low = jnp.where(inside, pltpu.roll(b, (3 * r) % LANES, 1), extra_low)
            extra_high = jnp.where(inside, pltpu.roll(a, (3 * r + 3) % LANES, 1), extra_high)
            own = jnp.where(side == 0, a, b)
            other = jnp.where(side == 0, b, a)
            mine[pl.ds(r * kw, kw), :] = own.astype(BF16)
            theirs[pl.ds(r * kw, kw), :] = other.astype(BF16)
            pairs.append(halves(r, shift, kh))
        both = pl.ds(row * kh, 2 * kh)
        straight[both, :] = jnp.concatenate([pairs[0][0], pairs[1][0]], 0).astype(BF16)
        diagonal[both, :] = jnp.concatenate([pairs[0][1], pairs[1][1]], 0).astype(BF16)
    own = jnp.where(side == 0, extra_low, extra_high)
    other = jnp.where(side == 0, extra_high, extra_low)
    mine[rows * kw :, :] = own.astype(BF16)
    theirs[rows * kw :, :] = other.astype(BF16)
    empty = jnp.zeros((kw - kh, LANES), F32)
    for source, target in ((own, straight), (other, diagonal)):
        part = jnp.where(side == 0, source[:kh], source[kw - kh :])
        target[rows * kh :, :] = jnp.concatenate([part, empty], 0).astype(BF16)


def band_kernel(mine, swap, straight, diagonal, first, second):
    odd = lax.axis_index("row") & 1
    kw = 8 * FIELDS
    rows = mine.shape[0] // kw - 1
    for out, from_end in ((first, 1 - odd), (second, odd)):
        at, extra = 0, HALO * sum(r.shape[0] // (rows + 1) for r in (mine, swap)) + 2 * HALO * HALO * FIELDS
        for source in (mine, swap, straight, diagonal):
            width = kw if source.shape[0] == (rows + 1) * kw else HALO * FIELDS
            start = pl.multiple_of(from_end * (rows - HALO) * width, 16)
            out[at : at + HALO * width, :] = source[pl.ds(start, HALO * width), :]
            out[extra : extra + 32, :] = source[rows * width : rows * width + 32, :]
            at += HALO * width
            extra += 32


def tap_matrix():
    return smooth_count(iota((LANES, LANES), 0) - iota((LANES, LANES), 1)).astype(BF16)


def border(side, first, sign, low, high):
    i, j = iota((LANES, LANES), 0), iota((LANES, LANES), 1)
    spot = (j + jnp.where(side == 0, 3, 0)) & (LANES - 1)
    ir, ic, jr, jc = i // 3, i % 3, spot // 3, spot % 3
    apart = jnp.where(side == 0, ic - jc + 3, jc - ic + 3)
    here = (ir == first + sign * jr) & (jr >= low) & (jr < high)
    return jnp.where(here, smooth_count(apart), 0.0).astype(BF16)


def weights_kernel(w_in, b_in, w_out, b_out, w1, w2, filters, *, layers, rows, hidden, slabs):
    depth = lax.axis_index("depth")
    side = depth & 1
    flipped = (lax.axis_index("row") & 1) == 0
    sign = jnp.where(flipped, -1, 1)
    filters[0] = tap_matrix()
    filters[1] = border(side, jnp.where(flipped, rows + HALO - 1, -HALO), sign, HALO, rows + HALO)
    filters[2] = border(side, jnp.where(flipped, HALO - 1, rows - HALO), sign, 0, HALO)
    filters[3] = border(side, jnp.where(flipped, rows - 1, 0), sign, 0, HALO)
    base = (depth - side) * layers
    total = slabs * layers
    width = w1.shape[2]
    window = (layers + 2 * HALO) * FIELDS
    kinds = w_in.shape[1]
    row, col = iota((kinds, width), 0), iota((kinds, width), 1)
    within = col % (2 * window)
    field = col & 3
    ending = col >= 6 * window
    pick1 = jnp.where(ending, -1, jnp.where(within < window, field, field + 4))
    pick2 = jnp.where(ending | (within >= window), -1, field + 8)
    eye = iota((hidden, hidden), 0) == iota((hidden, hidden), 1)
    bias = jnp.sum(jnp.where(eye, b_in[...], 0.0), axis=1, keepdims=True)
    part1 = dot(w_in[...], (row == pick1).astype(F32), HIGHEST)
    part2 = dot(w_in[...], (row == pick2).astype(F32), HIGHEST)
    kappa = iota((hidden, width), 1)
    part1 = jnp.where(kappa == 6 * window, bias, jnp.where(kappa == 6 * window + 1, bias, part1))
    scale = 1.0 / 64.0**3
    row_sign = jnp.where(flipped, -1.0 / 60.0, 1.0 / 60.0)
    z, place = iota((layers, width), 0), iota((layers, width), 1)
    inner = place % (2 * window)
    slope_kind = inner >= window
    last = place >= 6 * window
    slot = jnp.where(slope_kind, inner - window, inner) >> 2
    low_column = ((place >= 2 * window) & (place < 4 * window)) | (place == 6 * window + 1)
    for half in range(2):
        distance = slot - HALO - z
        center = smooth_count(distance) * scale
        slope = jnp.zeros((layers, width), F32)
        for offset, count in slope_counts:
            for sign in (1, -1):
                at = base + half * layers + z + sign * offset
                inside = ((at >= 0) & (at < total)).astype(F32)
                slope = slope + (inside * (sign * count)) * smooth_count(distance - sign * offset)
        center = jnp.where(last, 1.0, jnp.where(slope_kind, center * row_sign, center))
        product = center[None] * part1[:, None, :] + (slope * (scale / 60.0))[None] * part2[:, None, :]
        high = product.astype(BF16).astype(F32)
        chosen = jnp.where(low_column[None], product - high, high)
        w1[half] = chosen.reshape(hidden * layers, width).astype(BF16)
    outs = w_out.shape[0]
    for c in range(outs):
        values = jnp.sum(jnp.where(eye, w_out[c : c + 1, :], 0.0), axis=1, keepdims=True)
        factor = 0.5 if c < 3 else 1.0
        w2[c * hidden : (c + 1) * hidden, :] = jnp.broadcast_to(factor * values, (hidden, LANES))
    pick = iota((8, outs), 0) == iota((8, outs), 1)
    values = jnp.sum(jnp.where(pick, b_out[...], 0.0), axis=1, keepdims=True)
    values = jnp.where(iota((8, 1), 0) < 3, 0.5 * values, values)
    w2[outs * hidden :, :] = jnp.broadcast_to(values, (8, LANES))


def places(side, layers):
    kw, kh = layers * FIELDS, HALO * FIELDS
    far = kh + 2 * kw
    return ((kh + side * kw, kw), (kh + (1 - side) * kw, kw), ((1 - side) * far, kh), (side * far, kh))


def place_halo(halo, grid, edge, layers, side, flipped, taps, edges):
    kk = 2 * (layers + HALO) * FIELDS
    filtered = dot(halo[0 : HALO * kk, :], taps)
    added = dot(halo[HALO * kk :, :], edges)
    start = 0
    for index, (at, width) in enumerate(places(side, layers)):
        at = pl.ds(pl.multiple_of(at, 8), width)
        for row in range(HALO):
            grid[jnp.where(flipped, HALO - 1 - row, row), at, :] = filtered[start : start + width]
            start += width
        edge[at, :] = added[index * 32 : index * 32 + width]


def near_cut(side):
    return ((iota((16, LANES), 1) + jnp.where(side == 0, 3, 0)) & (LANES - 1)) < 3


def next_row(value, chain, ring, scale=None):
    for level in range(6):
        previous, chain[level] = chain[level], value
        if previous is None:
            return None
        value = previous + value
    if scale is not None:
        value = value * scale
    ring.append(value)
    if len(ring) < 7:
        return None
    slope = (ring[6] - ring[0]) - 9.0 * (ring[5] - ring[1]) + 45.0 * (ring[4] - ring[2])
    center = ring[3]
    ring.pop(0)
    return center, slope


def keep(kept, y, at, center, slope):
    kept[0, y, at, :], kept[2, y, at, :] = split(center)
    kept[1, y, at, :], kept[3, y, at, :] = split(slope)


def shade_rows(kept, w1, w2, out, layers, first, flipped, last):
    kw, kh = layers * FIELDS, HALO * FIELDS
    wide = 2 * LANES
    window = kw + 2 * kh
    hidden = w1.shape[1] // layers
    rest = w1.shape[2] - 6 * window
    ones = jnp.where(iota((rest, wide), 0) < 2, 1.0, 0.0).astype(BF16)
    sub = iota((layers, wide), 0)
    scale = depth_scale / (lax.axis_size("depth") * layers)

    def splat(index):
        line = w2[index : index + 1, :]
        return jnp.broadcast_to(jnp.concatenate([line, line], 1), (layers, wide))

    def target(k):
        return pl.ds(jnp.where(flipped, last - first - k, first + k), 1)

    for y in range(0, kept.shape[1], 2):
        total = jnp.zeros((1, wide), F32)
        front = jnp.ones((1, wide), F32)
        color = [jnp.zeros((layers, wide), F32) for unused in range(3)]
        for half in range(2):
            at = pl.ds(half * kw, window)
            c_high, s_high, c_low, s_low = [
                jnp.concatenate([kept[k, y, at, :], kept[k, y + 1, at, :]], 1) for k in range(4)
            ]
            stacked = jnp.concatenate([c_high, s_high, c_high, s_high, c_low, s_low, ones], 0)
            units = jnp.tanh(dot(w1[half], stacked))
            o = [splat(4 * hidden + c) for c in range(4)]
            for h in range(hidden):
                unit = units[h * layers : (h + 1) * layers]
                for c in range(4):
                    o[c] = o[c] + splat(c * hidden + h) * unit
            x = o[3]
            optical = (jnp.maximum(x, 0.0) + jnp.log(1.0 + jnp.exp(-jnp.abs(x)))) * scale
            through = optical
            for step in (1, 2, 4):
                through = through + jnp.where(sub >= step, pltpu.roll(through, step, 0), 0.0)
            through = through + total
            total = through[layers - 1 :]
            after = jnp.exp(-through)
            before = jnp.where(sub == 0, front, pltpu.roll(after, 1, 0))
            front = after[layers - 1 :]
            weight = before - after
            for c in range(3):
                color[c] = color[c] + weight * jnp.tanh(o[c])
        lines = [0.5 * (1.0 - front + jnp.sum(color[c], axis=0, keepdims=True)) for c in range(3)]
        for c, line in enumerate(lines + [front]):
            out[c, target(y), :] = line[:, :LANES]
            out[c, target(y + 1), :] = line[:, LANES:]


def filter_kernel(mine, swap, straight, diagonal, filters, grid, edge, *, layers, rows):
    side = lax.axis_index("depth") & 1
    flipped = (lax.axis_index("row") & 1) == 0
    for source, (at, width) in zip((mine, swap, straight, diagonal), places(side, layers)):
        at = pl.ds(pl.multiple_of(at, 8), width)
        filtered = dot(source[0 : rows * width, :], filters[0])
        for row in range(rows):
            grid[jnp.where(flipped, rows - 1 - row, row), at, :] = filtered[row * width : (row + 1) * width]
        edge[at, :] = dot(source[rows * width : rows * width + 32, :], filters[1])[:width]


def most_kernel(own_grid, own_edge, halo, w1, w2, filters, out, state, grid, edge, kept, *, layers, rows):
    side = lax.axis_index("depth") & 1
    flipped = (lax.axis_index("row") & 1) == 0
    kk = 2 * (layers + HALO) * FIELDS
    place_halo(halo, grid, edge, layers, side, flipped, filters[0], filters[2])
    near = near_cut(side)

    def filter_rows(group, carry):
        at = pl.ds(pl.multiple_of(group * 16, 16), 16)
        halo_edge, edges = edge[at, :], own_edge[at, :]
        chain, ring = [None] * 6, []
        for r in range(rows + HALO):
            turned = pltpu.roll(halo_edge if r < HALO else edges, (-3 * r) % LANES, 1)
            value = grid[r, at, :] if r < HALO else own_grid[r - HALO, at, :]
            given = next_row(value + jnp.where(near, turned, 0.0), chain, ring)
            if given is not None:
                keep(kept, r - 2 * HALO, at, *given)
        for index, value in enumerate(chain + ring):
            state[index, at, :] = value
        return carry

    lax.fori_loop(0, kk // 16, filter_rows, 0, unroll=kk // 16)
    shade_rows(kept, w1, w2, out, layers, 0, flipped, rows - 1)


def rest_kernel(halo, w1, w2, filters, state, done, out, grid, edge, kept, *, layers, rows):
    out[...] = done[...]
    side = lax.axis_index("depth") & 1
    band = lax.axis_index("row")
    flipped = (band & 1) == 0
    kk = 2 * (layers + HALO) * FIELDS
    place_halo(halo, grid, edge, layers, side, flipped, filters[0], filters[3])
    near = near_cut(side)
    outside = jnp.where(flipped, band == 0, band == lax.axis_size("row") - 1)
    inside = jnp.where(outside, 0.0, 1.0)

    def filter_rows(group, carry):
        at = pl.ds(pl.multiple_of(group * 16, 16), 16)
        edges = edge[at, :]
        values = [state[index, at, :] for index in range(12)]
        chain, ring = values[:6], values[6:]
        for r in range(HALO):
            turned = pltpu.roll(edges, (-3 * r) % LANES, 1)
            value = grid[r, at, :] + jnp.where(near, turned, 0.0)
            keep(kept, r, at, *next_row(value, chain, ring, inside if r >= 3 else None))
        return carry

    lax.fori_loop(0, kk // 16, filter_rows, 0, unroll=kk // 16)
    shade_rows(kept, w1, w2, out, layers, rows - HALO, flipped, rows - 1)


def call(kernel, out_shape, operands, scratch=(), flops=0, name=None):
    vmem = pl.BlockSpec(memory_space=pltpu.VMEM)
    return pl.pallas_call(
        kernel,
        out_shape=out_shape,
        in_specs=[vmem] * len(operands),
        out_specs=jax.tree.map(lambda unused: vmem, out_shape),
        scratch_shapes=list(scratch),
        compiler_params=pltpu.CompilerParams(vmem_limit_bytes=40 * 2**20),
        cost_estimate=pl.CostEstimate(flops=flops, bytes_accessed=2**20, transcendentals=0),
        name=name,
    )(*operands)


def combine(front, back):
    color = front[0:3] + front[3:4] * back[0:3]
    return jnp.concatenate([color, front[3:4] * back[3:4]], 0)


def local(fields, w_in, b_in, w_out, b_out):
    layers, rows, columns = fields.shape[1:]
    hidden = w_in.shape[0]
    slabs = lax.axis_size("depth")
    bands = lax.axis_size("row")
    me = lax.axis_index("depth")
    side = me & 1
    kw, kh = layers * FIELDS, HALO * FIELDS
    kk = 2 * (kw + kh)
    shape = jax.ShapeDtypeStruct
    mine, theirs, own_halo, other_halo = call(
        pack_kernel,
        [
            shape(((rows + 1) * kw, LANES), BF16),
            shape(((rows + 1) * kw, LANES), BF16),
            shape((rows * kh + kw, LANES), BF16),
            shape((rows * kh + kw, LANES), BF16),
        ],
        (fields,),
        [pltpu.VMEM((rows * (kw + 4), LANES), F32)] * 2,
        name="pack",
    )
    swap_pairs = [(i, i ^ 1) for i in range(slabs)]
    odd, even = range(1, slabs, 2), range(0, slabs, 2)
    diagonal_pairs = [(i, i + 1) for i in odd if i + 1 < slabs] + [(i, i - 1) for i in even if i]
    straight_pairs = [(i, i + 2) for i in odd if i + 2 < slabs] + [(i, i - 2) for i in even if i]
    swap = lax.ppermute(theirs, "depth", swap_pairs)
    diagonal = lax.ppermute(other_halo, "depth", diagonal_pairs)
    straight = lax.ppermute(own_halo, "depth", straight_pairs)
    swap, straight, diagonal = lax.optimization_barrier((swap, straight, diagonal))

    width = -(-(6 * (kw + 2 * kh) + 2) // 256) * 256
    w1, w2, filters = call(
        functools.partial(weights_kernel, layers=layers, rows=rows, hidden=hidden, slabs=slabs),
        [
            shape((2, layers * hidden, width), BF16),
            shape((4 * hidden + 8, LANES), F32),
            shape((4, LANES, LANES), BF16),
        ],
        (w_in, b_in[None], w_out, b_out[None]),
        flops=10**8,
        name="weights",
    )
    mine, w1, w2, filters = lax.optimization_barrier((mine, w1, w2, filters))
    message = shape((HALO * kk + 4 * 32, LANES), BF16)
    first, second = call(band_kernel, [message, message], (mine, swap, straight, diagonal), name="band")
    within = [(i, i ^ 1) for i in range(bands)]
    across = [(i, i + 1) for i in range(1, bands - 1, 2)] + [(i + 1, i) for i in range(1, bands - 1, 2)]
    second = lax.ppermute(second, "row", across)
    first = lax.ppermute(first, "row", within)

    own_grid, own_edge = call(
        functools.partial(filter_kernel, layers=layers, rows=rows),
        [shape((rows, kk, LANES), F32), shape((kk, LANES), F32)],
        (mine, swap, straight, diagonal, filters),
        flops=10**9,
        name="filter",
    )
    image = shape((4, rows, LANES), F32)
    current, state = call(
        functools.partial(most_kernel, layers=layers, rows=rows),
        [image, shape((12, kk, LANES), F32)],
        (own_grid, own_edge, first, w1, w2, filters),
        [
            pltpu.VMEM((HALO, kk, LANES), F32),
            pltpu.VMEM((kk, LANES), F32),
            pltpu.VMEM((4, rows - HALO, kk, LANES), BF16),
        ],
        flops=10**10,
        name="shade_most",
    )
    current = call(
        functools.partial(rest_kernel, layers=layers, rows=rows),
        image,
        (second, w1, w2, filters, state, current),
        [
            pltpu.VMEM((HALO, kk, LANES), F32),
            pltpu.VMEM((kk, LANES), F32),
            pltpu.VMEM((4, HALO, kk, LANES), BF16),
        ],
        flops=10**9,
        name="shade_rest",
    )
    step = 2
    while step < slabs:
        received = lax.ppermute(current, "depth", [(i, i ^ step) for i in range(slabs)])
        behind = (me & step) != 0
        current = combine(jnp.where(behind, received, current), jnp.where(behind, current, received))
        step *= 2
    current = jnp.concatenate([current[0:3], 1.0 - current[3:4]], 0)
    other = lax.ppermute(current, "depth", swap_pairs)
    first_half = jnp.where(side == 0, current, other)
    second_half = jnp.where(side == 0, other, current)
    return jnp.concatenate([first_half, second_half], 2)


def solution(mesh):
    return jax.shard_map(
        local,
        mesh=mesh,
        in_specs=(P(None, "depth", "row", None), P(), P(), P(), P()),
        out_specs=P(None, "row", None),
        check_vma=False,
    )
```

```python
import functools

import jax
import jax.numpy as jnp
from jax import lax
from jax.experimental import pallas as pl
from jax.experimental.pallas import tpu as pltpu
from jax.sharding import PartitionSpec as P

FIELDS = 4
HALO = 6
LANES = 128
HIGHEST = lax.Precision.HIGHEST
F32 = jnp.float32
BF16 = jnp.bfloat16
depth_scale = 2.0
smooth_counts = (20.0, 15.0, 6.0, 1.0)
slope_counts = ((1, 45.0), (2, -9.0), (3, 1.0))


def dot(a, b, precision=None):
    return jnp.dot(a, b, preferred_element_type=F32, precision=precision)


def iota(shape, dim):
    return lax.broadcasted_iota(jnp.int32, shape, dim)


def smooth_count(distance):
    d = jnp.abs(distance)
    out = jnp.where(d == 0, smooth_counts[0], 0.0)
    for place in (1, 2, 3):
        out = jnp.where(d == place, smooth_counts[place], out)
    return out.astype(F32)


def split(x):
    high = x.astype(BF16)
    return high, (x - high.astype(F32)).astype(BF16)


def pack_kernel(fields, mine, theirs, straight, diagonal, left, right):
    side = lax.axis_index("depth") & 1
    layers, rows = fields.shape[1], fields.shape[2]
    kw, kh = layers * FIELDS, HALO * FIELDS
    pitch = left.shape[0] // rows
    for layer in range(layers):
        for field in range(FIELDS):
            plane = fields[field, layer].astype(F32)
            place = pl.ds(layer * FIELDS + field, rows, stride=pitch)
            left[place, :] = plane[:, :LANES]
            right[place, :] = plane[:, LANES:]
    lane = iota((kw, LANES), 1)
    shift = pl.multiple_of(side * (kw - kh), 8)

    def halves(row, start, count):
        a = left[pl.ds(row * pitch + start, count), :]
        b = right[pl.ds(row * pitch + start, count), :]
        return jnp.where(side == 0, a, b), jnp.where(side == 0, b, a)

    extra_low = jnp.zeros((kw, LANES), F32)
    extra_high = jnp.zeros((kw, LANES), F32)
    for row in range(0, rows, 2):
        pairs = []
        for r in (row, row + 1):
            a = left[pl.ds(r * pitch, kw), :]
            b = right[pl.ds(r * pitch, kw), :]
            inside = (lane >= 3 * r) & (lane < 3 * r + 3)
            extra_low = jnp.where(inside, pltpu.roll(b, (3 * r) % LANES, 1), extra_low)
            extra_high = jnp.where(inside, pltpu.roll(a, (3 * r + 3) % LANES, 1), extra_high)
            own = jnp.where(side == 0, a, b)
            other = jnp.where(side == 0, b, a)
            mine[pl.ds(r * kw, kw), :] = own.astype(BF16)
            theirs[pl.ds(r * kw, kw), :] = other.astype(BF16)
            pairs.append(halves(r, shift, kh))
        both = pl.ds(row * kh, 2 * kh)
        straight[both, :] = jnp.concatenate([pairs[0][0], pairs[1][0]], 0).astype(BF16)
        diagonal[both, :] = jnp.concatenate([pairs[0][1], pairs[1][1]], 0).astype(BF16)
    own = jnp.where(side == 0, extra_low, extra_high)
    other = jnp.where(side == 0, extra_high, extra_low)
    mine[rows * kw :, :] = own.astype(BF16)
    theirs[rows * kw :, :] = other.astype(BF16)
    empty = jnp.zeros((kw - kh, LANES), F32)
    for source, target in ((own, straight), (other, diagonal)):
        part = jnp.where(side == 0, source[:kh], source[kw - kh :])
        target[rows * kh :, :] = jnp.concatenate([part, empty], 0).astype(BF16)


def band_kernel(mine, swap, straight, diagonal, first, second):
    odd = lax.axis_index("row") & 1
    kw = 8 * FIELDS
    rows = mine.shape[0] // kw - 1
    for out, from_end in ((first, 1 - odd), (second, odd)):
        at, extra = 0, HALO * sum(r.shape[0] // (rows + 1) for r in (mine, swap)) + 2 * HALO * HALO * FIELDS
        for source in (mine, swap, straight, diagonal):
            width = kw if source.shape[0] == (rows + 1) * kw else HALO * FIELDS
            start = pl.multiple_of(from_end * (rows - HALO) * width, 16)
            out[at : at + HALO * width, :] = source[pl.ds(start, HALO * width), :]
            out[extra : extra + 32, :] = source[rows * width : rows * width + 32, :]
            at += HALO * width
            extra += 32


def tap_matrix():
    return smooth_count(iota((LANES, LANES), 0) - iota((LANES, LANES), 1)).astype(BF16)


def border(side, first, sign, low, high):
    i, j = iota((LANES, LANES), 0), iota((LANES, LANES), 1)
    spot = (j + jnp.where(side == 0, 3, 0)) & (LANES - 1)
    ir, ic, jr, jc = i // 3, i % 3, spot // 3, spot % 3
    apart = jnp.where(side == 0, ic - jc + 3, jc - ic + 3)
    here = (ir == first + sign * jr) & (jr >= low) & (jr < high)
    return jnp.where(here, smooth_count(apart), 0.0).astype(BF16)


def weights_kernel(w_in, b_in, w_out, b_out, w1, w2, filters, *, layers, rows, hidden, slabs):
    depth = lax.axis_index("depth")
    side = depth & 1
    flipped = (lax.axis_index("row") & 1) == 0
    sign = jnp.where(flipped, -1, 1)
    filters[0] = tap_matrix()
    filters[1] = border(side, jnp.where(flipped, rows + HALO - 1, -HALO), sign, HALO, rows + HALO)
    filters[2] = border(side, jnp.where(flipped, HALO - 1, rows - HALO), sign, 0, HALO)
    filters[3] = border(side, jnp.where(flipped, rows - 1, 0), sign, 0, HALO)
    base = (depth - side) * layers
    total = slabs * layers
    width = w1.shape[2]
    window = (layers + 2 * HALO) * FIELDS
    kinds = w_in.shape[1]
    row, col = iota((kinds, width), 0), iota((kinds, width), 1)
    within = col % (2 * window)
    field = col & 3
    ending = col >= 6 * window
    pick1 = jnp.where(ending, -1, jnp.where(within < window, field, field + 4))
    pick2 = jnp.where(ending | (within >= window), -1, field + 8)
    eye = iota((hidden, hidden), 0) == iota((hidden, hidden), 1)
    bias = jnp.sum(jnp.where(eye, b_in[...], 0.0), axis=1, keepdims=True)
    part1 = dot(w_in[...], (row == pick1).astype(F32), HIGHEST)
    part2 = dot(w_in[...], (row == pick2).astype(F32), HIGHEST)
    kappa = iota((hidden, width), 1)
    part1 = jnp.where(kappa == 6 * window, bias, jnp.where(kappa == 6 * window + 1, bias, part1))
    scale = 1.0 / 64.0**3
    row_sign = jnp.where(flipped, -1.0 / 60.0, 1.0 / 60.0)
    z, place = iota((layers, width), 0), iota((layers, width), 1)
    inner = place % (2 * window)
    slope_kind = inner >= window
    last = place >= 6 * window
    slot = jnp.where(slope_kind, inner - window, inner) >> 2
    low_column = ((place >= 2 * window) & (place < 4 * window)) | (place == 6 * window + 1)
    for half in range(2):
        distance = slot - HALO - z
        center = smooth_count(distance) * scale
        slope = jnp.zeros((layers, width), F32)
        for offset, count in slope_counts:
            for sign in (1, -1):
                at = base + half * layers + z + sign * offset
                inside = ((at >= 0) & (at < total)).astype(F32)
                slope = slope + (inside * (sign * count)) * smooth_count(distance - sign * offset)
        center = jnp.where(last, 1.0, jnp.where(slope_kind, center * row_sign, center))
        product = center[None] * part1[:, None, :] + (slope * (scale / 60.0))[None] * part2[:, None, :]
        high = product.astype(BF16).astype(F32)
        chosen = jnp.where(low_column[None], product - high, high)
        w1[half] = chosen.reshape(hidden * layers, width).astype(BF16)
    outs = w_out.shape[0]
    for c in range(outs):
        values = jnp.sum(jnp.where(eye, w_out[c : c + 1, :], 0.0), axis=1, keepdims=True)
        factor = 0.5 if c < 3 else 1.0
        w2[c * hidden : (c + 1) * hidden, :] = jnp.broadcast_to(factor * values, (hidden, LANES))
    pick = iota((8, outs), 0) == iota((8, outs), 1)
    values = jnp.sum(jnp.where(pick, b_out[...], 0.0), axis=1, keepdims=True)
    values = jnp.where(iota((8, 1), 0) < 3, 0.5 * values, values)
    w2[outs * hidden :, :] = jnp.broadcast_to(values, (8, LANES))


def places(side, layers):
    kw, kh = layers * FIELDS, HALO * FIELDS
    far = kh + 2 * kw
    return ((kh + side * kw, kw), (kh + (1 - side) * kw, kw), ((1 - side) * far, kh), (side * far, kh))


def place_halo(halo, grid, edge, layers, side, flipped, taps, edges):
    kk = 2 * (layers + HALO) * FIELDS
    filtered = dot(halo[0 : HALO * kk, :], taps)
    added = dot(halo[HALO * kk :, :], edges)
    start = 0
    for index, (at, width) in enumerate(places(side, layers)):
        at = pl.ds(pl.multiple_of(at, 8), width)
        for row in range(HALO):
            grid[jnp.where(flipped, HALO - 1 - row, row), at, :] = filtered[start : start + width]
            start += width
        edge[at, :] = added[index * 32 : index * 32 + width]


def near_cut(side):
    return ((iota((16, LANES), 1) + jnp.where(side == 0, 3, 0)) & (LANES - 1)) < 3


def next_row(value, chain, ring, scale=None):
    for level in range(6):
        previous, chain[level] = chain[level], value
        if previous is None:
            return None
        value = previous + value
    if scale is not None:
        value = value * scale
    ring.append(value)
    if len(ring) < 7:
        return None
    slope = (ring[6] - ring[0]) - 9.0 * (ring[5] - ring[1]) + 45.0 * (ring[4] - ring[2])
    center = ring[3]
    ring.pop(0)
    return center, slope


def keep(kept, y, at, center, slope):
    kept[0, y, at, :], kept[2, y, at, :] = split(center)
    kept[1, y, at, :], kept[3, y, at, :] = split(slope)


def shade_rows(kept, w1, w2, out, layers, first, flipped, last):
    kw, kh = layers * FIELDS, HALO * FIELDS
    wide = 2 * LANES
    window = kw + 2 * kh
    hidden = w1.shape[1] // layers
    rest = w1.shape[2] - 6 * window
    ones = jnp.where(iota((rest, wide), 0) < 2, 1.0, 0.0).astype(BF16)
    sub = iota((layers, wide), 0)
    scale = depth_scale / (lax.axis_size("depth") * layers)

    def splat(index):
        line = w2[index : index + 1, :]
        return jnp.broadcast_to(jnp.concatenate([line, line], 1), (layers, wide))

    def target(k):
        return pl.ds(jnp.where(flipped, last - first - k, first + k), 1)

    for y in range(0, kept.shape[1], 2):
        total = jnp.zeros((1, wide), F32)
        front = jnp.ones((1, wide), F32)
        color = [jnp.zeros((layers, wide), F32) for unused in range(3)]
        for half in range(2):
            at = pl.ds(half * kw, window)
            c_high, s_high, c_low, s_low = [
                jnp.concatenate([kept[k, y, at, :], kept[k, y + 1, at, :]], 1) for k in range(4)
            ]
            stacked = jnp.concatenate([c_high, s_high, c_high, s_high, c_low, s_low, ones], 0)
            units = jnp.tanh(dot(w1[half], stacked))
            o = [splat(4 * hidden + c) for c in range(4)]
            for h in range(hidden):
                unit = units[h * layers : (h + 1) * layers]
                for c in range(4):
                    o[c] = o[c] + splat(c * hidden + h) * unit
            x = o[3]
            optical = (jnp.maximum(x, 0.0) + jnp.log(1.0 + jnp.exp(-jnp.abs(x)))) * scale
            through = optical
            for step in (1, 2, 4):
                through = through + jnp.where(sub >= step, pltpu.roll(through, step, 0), 0.0)
            through = through + total
            total = through[layers - 1 :]
            after = jnp.exp(-through)
            before = jnp.where(sub == 0, front, pltpu.roll(after, 1, 0))
            front = after[layers - 1 :]
            weight = before - after
            for c in range(3):
                color[c] = color[c] + weight * jnp.tanh(o[c])
        lines = [0.5 * (1.0 - front + jnp.sum(color[c], axis=0, keepdims=True)) for c in range(3)]
        for c, line in enumerate(lines + [front]):
            out[c, target(y), :] = line[:, :LANES]
            out[c, target(y + 1), :] = line[:, LANES:]


def filter_kernel(mine, swap, straight, diagonal, filters, grid, edge, *, layers, rows):
    side = lax.axis_index("depth") & 1
    flipped = (lax.axis_index("row") & 1) == 0
    for source, (at, width) in zip((mine, swap, straight, diagonal), places(side, layers)):
        at = pl.ds(pl.multiple_of(at, 8), width)
        filtered = dot(source[0 : rows * width, :], filters[0])
        for row in range(rows):
            grid[jnp.where(flipped, rows - 1 - row, row), at, :] = filtered[row * width : (row + 1) * width]
        edge[at, :] = dot(source[rows * width : rows * width + 32, :], filters[1])[:width]


def most_kernel(own_grid, own_edge, halo, w1, w2, filters, out, state, grid, edge, kept, *, layers, rows):
    side = lax.axis_index("depth") & 1
    flipped = (lax.axis_index("row") & 1) == 0
    kk = 2 * (layers + HALO) * FIELDS
    place_halo(halo, grid, edge, layers, side, flipped, filters[0], filters[2])
    near = near_cut(side)

    def filter_rows(group, carry):
        at = pl.ds(pl.multiple_of(group * 16, 16), 16)
        halo_edge, edges = edge[at, :], own_edge[at, :]
        chain, ring = [None] * 6, []
        for r in range(rows + HALO):
            turned = pltpu.roll(halo_edge if r < HALO else edges, (-3 * r) % LANES, 1)
            value = grid[r, at, :] if r < HALO else own_grid[r - HALO, at, :]
            given = next_row(value + jnp.where(near, turned, 0.0), chain, ring)
            if given is not None:
                keep(kept, r - 2 * HALO, at, *given)
        for index, value in enumerate(chain + ring):
            state[index, at, :] = value
        return carry

    lax.fori_loop(0, kk // 16, filter_rows, 0, unroll=kk // 16)
    shade_rows(kept, w1, w2, out, layers, 0, flipped, rows - 1)


def rest_kernel(halo, w1, w2, filters, state, done, out, grid, edge, kept, *, layers, rows):
    out[...] = done[...]
    side = lax.axis_index("depth") & 1
    band = lax.axis_index("row")
    flipped = (band & 1) == 0
    kk = 2 * (layers + HALO) * FIELDS
    place_halo(halo, grid, edge, layers, side, flipped, filters[0], filters[3])
    near = near_cut(side)
    outside = jnp.where(flipped, band == 0, band == lax.axis_size("row") - 1)
    inside = jnp.where(outside, 0.0, 1.0)

    def filter_rows(group, carry):
        at = pl.ds(pl.multiple_of(group * 16, 16), 16)
        edges = edge[at, :]
        values = [state[index, at, :] for index in range(12)]
        chain, ring = values[:6], values[6:]
        for r in range(HALO):
            turned = pltpu.roll(edges, (-3 * r) % LANES, 1)
            value = grid[r, at, :] + jnp.where(near, turned, 0.0)
            keep(kept, r, at, *next_row(value, chain, ring, inside if r >= 3 else None))
        return carry

    lax.fori_loop(0, kk // 16, filter_rows, 0, unroll=kk // 16)
    shade_rows(kept, w1, w2, out, layers, rows - HALO, flipped, rows - 1)


def call(kernel, out_shape, operands, scratch=(), flops=0, name=None):
    vmem = pl.BlockSpec(memory_space=pltpu.VMEM)
    return pl.pallas_call(
        kernel,
        out_shape=out_shape,
        in_specs=[vmem] * len(operands),
        out_specs=jax.tree.map(lambda unused: vmem, out_shape),
        scratch_shapes=list(scratch),
        compiler_params=pltpu.CompilerParams(vmem_limit_bytes=40 * 2**20),
        cost_estimate=pl.CostEstimate(flops=flops, bytes_accessed=2**20, transcendentals=0),
        name=name,
    )(*operands)


def combine(front, back):
    is_color = lax.broadcasted_iota(jnp.int32, front.shape, 0) < 3
    return jnp.where(is_color, front, 0.0) + front[3:4] * back


def local(fields, w_in, b_in, w_out, b_out):
    layers, rows, columns = fields.shape[1:]
    hidden = w_in.shape[0]
    slabs = lax.axis_size("depth")
    bands = lax.axis_size("row")
    me = lax.axis_index("depth")
    side = me & 1
    kw, kh = layers * FIELDS, HALO * FIELDS
    kk = 2 * (kw + kh)
    shape = jax.ShapeDtypeStruct
    mine, theirs, own_halo, other_halo = call(
        pack_kernel,
        [
            shape(((rows + 1) * kw, LANES), BF16),
            shape(((rows + 1) * kw, LANES), BF16),
            shape((rows * kh + kw, LANES), BF16),
            shape((rows * kh + kw, LANES), BF16),
        ],
        (fields,),
        [pltpu.VMEM((rows * (kw + 4), LANES), F32)] * 2,
        name="pack",
    )
    swap_pairs = [(i, i ^ 1) for i in range(slabs)]
    odd, even = range(1, slabs, 2), range(0, slabs, 2)
    diagonal_pairs = [(i, i + 1) for i in odd if i + 1 < slabs] + [(i, i - 1) for i in even if i]
    straight_pairs = [(i, i + 2) for i in odd if i + 2 < slabs] + [(i, i - 2) for i in even if i]
    swap = lax.ppermute(theirs, "depth", swap_pairs)
    diagonal = lax.ppermute(other_halo, "depth", diagonal_pairs)
    straight = lax.ppermute(own_halo, "depth", straight_pairs)
    swap, straight, diagonal = lax.optimization_barrier((swap, straight, diagonal))

    width = -(-(6 * (kw + 2 * kh) + 2) // 256) * 256
    w1, w2, filters = call(
        functools.partial(weights_kernel, layers=layers, rows=rows, hidden=hidden, slabs=slabs),
        [
            shape((2, layers * hidden, width), BF16),
            shape((4 * hidden + 8, LANES), F32),
            shape((4, LANES, LANES), BF16),
        ],
        (w_in, b_in[None], w_out, b_out[None]),
        flops=10**8,
        name="weights",
    )
    mine, w1, w2, filters = lax.optimization_barrier((mine, w1, w2, filters))
    message = shape((HALO * kk + 4 * 32, LANES), BF16)
    first, second = call(band_kernel, [message, message], (mine, swap, straight, diagonal), name="band")
    within = [(i, i ^ 1) for i in range(bands)]
    across = [(i, i + 1) for i in range(1, bands - 1, 2)] + [(i + 1, i) for i in range(1, bands - 1, 2)]
    second = lax.ppermute(second, "row", across)
    first = lax.ppermute(first, "row", within)

    own_grid, own_edge = call(
        functools.partial(filter_kernel, layers=layers, rows=rows),
        [shape((rows, kk, LANES), F32), shape((kk, LANES), F32)],
        (mine, swap, straight, diagonal, filters),
        flops=10**9,
        name="filter",
    )
    image = shape((4, rows, LANES), F32)
    current, state = call(
        functools.partial(most_kernel, layers=layers, rows=rows),
        [image, shape((12, kk, LANES), F32)],
        (own_grid, own_edge, first, w1, w2, filters),
        [
            pltpu.VMEM((HALO, kk, LANES), F32),
            pltpu.VMEM((kk, LANES), F32),
            pltpu.VMEM((4, rows - HALO, kk, LANES), BF16),
        ],
        flops=10**10,
        name="shade_most",
    )
    current = call(
        functools.partial(rest_kernel, layers=layers, rows=rows),
        image,
        (second, w1, w2, filters, state, current),
        [
            pltpu.VMEM((HALO, kk, LANES), F32),
            pltpu.VMEM((kk, LANES), F32),
            pltpu.VMEM((4, HALO, kk, LANES), BF16),
        ],
        flops=10**9,
        name="shade_rest",
    )
    step = 2
    while step < slabs:
        received = lax.ppermute(current, "depth", [(i, i ^ step) for i in range(slabs)])
        behind = (me & step) != 0
        current = combine(jnp.where(behind, received, current), jnp.where(behind, current, received))
        step *= 2
    other = lax.ppermute(current, "depth", swap_pairs)
    first_half = jnp.where(side == 0, current, other)
    second_half = jnp.where(side == 0, other, current)
    whole = jnp.concatenate([first_half, second_half], 2)
    is_color = lax.broadcasted_iota(jnp.int32, whole.shape, 0) < 3
    return jnp.where(is_color, whole, 1.0 - whole)


def solution(mesh):
    return jax.shard_map(
        local,
        mesh=mesh,
        in_specs=(P(None, "depth", "row", None), P(), P(), P(), P()),
        out_specs=P(None, "row", None),
        check_vma=False,
    )
```

```python
import functools

import jax
import jax.numpy as jnp
from jax import lax
from jax.experimental import pallas as pl
from jax.experimental.pallas import tpu as pltpu
from jax.sharding import PartitionSpec as P

FIELDS = 4
HALO = 6
LANES = 128
HIGHEST = lax.Precision.HIGHEST
F32 = jnp.float32
BF16 = jnp.bfloat16
depth_scale = 2.0
smooth_counts = (20.0, 15.0, 6.0, 1.0)
slope_counts = ((1, 45.0), (2, -9.0), (3, 1.0))


def dot(a, b, precision=None):
    return jnp.dot(a, b, preferred_element_type=F32, precision=precision)


def iota(shape, dim):
    return lax.broadcasted_iota(jnp.int32, shape, dim)


def smooth_count(distance):
    d = jnp.abs(distance)
    out = jnp.where(d == 0, smooth_counts[0], 0.0)
    for place in (1, 2, 3):
        out = jnp.where(d == place, smooth_counts[place], out)
    return out.astype(F32)


def split(x):
    high = x.astype(BF16)
    return high, (x - high.astype(F32)).astype(BF16)


def pack_kernel(fields, mine, theirs, straight, diagonal, left, right):
    side = lax.axis_index("depth") & 1
    layers, rows = fields.shape[1], fields.shape[2]
    kw, kh = layers * FIELDS, HALO * FIELDS
    pitch = left.shape[0] // rows
    for layer in range(layers):
        for field in range(FIELDS):
            plane = fields[field, layer].astype(F32)
            place = pl.ds(layer * FIELDS + field, rows, stride=pitch)
            left[place, :] = plane[:, :LANES]
            right[place, :] = plane[:, LANES:]
    lane = iota((kw, LANES), 1)
    shift = pl.multiple_of(side * (kw - kh), 8)

    def halves(row, start, count):
        a = left[pl.ds(row * pitch + start, count), :]
        b = right[pl.ds(row * pitch + start, count), :]
        return jnp.where(side == 0, a, b), jnp.where(side == 0, b, a)

    extra_low = jnp.zeros((kw, LANES), F32)
    extra_high = jnp.zeros((kw, LANES), F32)
    for row in range(0, rows, 2):
        pairs = []
        for r in (row, row + 1):
            a = left[pl.ds(r * pitch, kw), :]
            b = right[pl.ds(r * pitch, kw), :]
            inside = (lane >= 3 * r) & (lane < 3 * r + 3)
            extra_low = jnp.where(inside, pltpu.roll(b, (3 * r) % LANES, 1), extra_low)
            extra_high = jnp.where(inside, pltpu.roll(a, (3 * r + 3) % LANES, 1), extra_high)
            own = jnp.where(side == 0, a, b)
            other = jnp.where(side == 0, b, a)
            mine[pl.ds(r * kw, kw), :] = own.astype(BF16)
            theirs[pl.ds(r * kw, kw), :] = other.astype(BF16)
            pairs.append(halves(r, shift, kh))
        both = pl.ds(row * kh, 2 * kh)
        straight[both, :] = jnp.concatenate([pairs[0][0], pairs[1][0]], 0).astype(BF16)
        diagonal[both, :] = jnp.concatenate([pairs[0][1], pairs[1][1]], 0).astype(BF16)
    own = jnp.where(side == 0, extra_low, extra_high)
    other = jnp.where(side == 0, extra_high, extra_low)
    mine[rows * kw :, :] = own.astype(BF16)
    theirs[rows * kw :, :] = other.astype(BF16)
    empty = jnp.zeros((kw - kh, LANES), F32)
    for source, target in ((own, straight), (other, diagonal)):
        part = jnp.where(side == 0, source[:kh], source[kw - kh :])
        target[rows * kh :, :] = jnp.concatenate([part, empty], 0).astype(BF16)


def band_kernel(mine, swap, straight, diagonal, first, second):
    odd = lax.axis_index("row") & 1
    kw = 8 * FIELDS
    rows = mine.shape[0] // kw - 1
    for out, from_end in ((first, 1 - odd), (second, odd)):
        at, extra = 0, HALO * sum(r.shape[0] // (rows + 1) for r in (mine, swap)) + 2 * HALO * HALO * FIELDS
        for source in (mine, swap, straight, diagonal):
            width = kw if source.shape[0] == (rows + 1) * kw else HALO * FIELDS
            start = pl.multiple_of(from_end * (rows - HALO) * width, 16)
            out[at : at + HALO * width, :] = source[pl.ds(start, HALO * width), :]
            out[extra : extra + 32, :] = source[rows * width : rows * width + 32, :]
            at += HALO * width
            extra += 32


def tap_matrix():
    return smooth_count(iota((LANES, LANES), 0) - iota((LANES, LANES), 1)).astype(BF16)


def border(side, first, sign, low, high):
    i, j = iota((LANES, LANES), 0), iota((LANES, LANES), 1)
    spot = (j + jnp.where(side == 0, 3, 0)) & (LANES - 1)
    ir, ic, jr, jc = i // 3, i % 3, spot // 3, spot % 3
    apart = jnp.where(side == 0, ic - jc + 3, jc - ic + 3)
    here = (ir == first + sign * jr) & (jr >= low) & (jr < high)
    return jnp.where(here, smooth_count(apart), 0.0).astype(BF16)


def weights_kernel(w_in, b_in, w_out, b_out, w1, w2, filters, *, layers, rows, hidden, slabs):
    depth = lax.axis_index("depth")
    side = depth & 1
    flipped = (lax.axis_index("row") & 1) == 0
    sign = jnp.where(flipped, -1, 1)
    filters[0] = tap_matrix()
    filters[1] = border(side, jnp.where(flipped, rows + HALO - 1, -HALO), sign, HALO, rows + HALO)
    filters[2] = border(side, jnp.where(flipped, HALO - 1, rows - HALO), sign, 0, HALO)
    filters[3] = border(side, jnp.where(flipped, rows - 1, 0), sign, 0, HALO)
    base = (depth - side) * layers
    total = slabs * layers
    width = w1.shape[2]
    window = (layers + 2 * HALO) * FIELDS
    kinds = w_in.shape[1]
    row, col = iota((kinds, width), 0), iota((kinds, width), 1)
    within = col % (2 * window)
    field = col & 3
    ending = col >= 6 * window
    pick1 = jnp.where(ending, -1, jnp.where(within < window, field, field + 4))
    pick2 = jnp.where(ending | (within >= window), -1, field + 8)
    eye = iota((hidden, hidden), 0) == iota((hidden, hidden), 1)
    bias = jnp.sum(jnp.where(eye, b_in[...], 0.0), axis=1, keepdims=True)
    part1 = dot(w_in[...], (row == pick1).astype(F32), HIGHEST)
    part2 = dot(w_in[...], (row == pick2).astype(F32), HIGHEST)
    kappa = iota((hidden, width), 1)
    part1 = jnp.where(kappa == 6 * window, bias, jnp.where(kappa == 6 * window + 1, bias, part1))
    scale = 1.0 / 64.0**3
    row_sign = jnp.where(flipped, -1.0 / 60.0, 1.0 / 60.0)
    z, place = iota((layers, width), 0), iota((layers, width), 1)
    inner = place % (2 * window)
    slope_kind = inner >= window
    last = place >= 6 * window
    slot = jnp.where(slope_kind, inner - window, inner) >> 2
    low_column = ((place >= 2 * window) & (place < 4 * window)) | (place == 6 * window + 1)
    for half in range(2):
        distance = slot - HALO - z
        center = smooth_count(distance) * scale
        slope = jnp.zeros((layers, width), F32)
        for offset, count in slope_counts:
            for sign in (1, -1):
                at = base + half * layers + z + sign * offset
                inside = ((at >= 0) & (at < total)).astype(F32)
                slope = slope + (inside * (sign * count)) * smooth_count(distance - sign * offset)
        center = jnp.where(last, 1.0, jnp.where(slope_kind, center * row_sign, center))
        product = center[None] * part1[:, None, :] + (slope * (scale / 60.0))[None] * part2[:, None, :]
        high = product.astype(BF16).astype(F32)
        chosen = jnp.where(low_column[None], product - high, high)
        w1[half] = chosen.reshape(hidden * layers, width).astype(BF16)
    outs = w_out.shape[0]
    for c in range(outs):
        values = jnp.sum(jnp.where(eye, w_out[c : c + 1, :], 0.0), axis=1, keepdims=True)
        factor = 0.5 if c < 3 else 1.0
        w2[c * hidden : (c + 1) * hidden, :] = jnp.broadcast_to(factor * values, (hidden, LANES))
    pick = iota((8, outs), 0) == iota((8, outs), 1)
    values = jnp.sum(jnp.where(pick, b_out[...], 0.0), axis=1, keepdims=True)
    values = jnp.where(iota((8, 1), 0) < 3, 0.5 * values, values)
    w2[outs * hidden :, :] = jnp.broadcast_to(values, (8, LANES))


def places(side, layers):
    kw, kh = layers * FIELDS, HALO * FIELDS
    far = kh + 2 * kw
    return ((kh + side * kw, kw), (kh + (1 - side) * kw, kw), ((1 - side) * far, kh), (side * far, kh))


def place_halo(halo, grid, edge, layers, side, flipped, taps, edges):
    kk = 2 * (layers + HALO) * FIELDS
    filtered = dot(halo[0 : HALO * kk, :], taps)
    added = dot(halo[HALO * kk :, :], edges)
    start = 0
    for index, (at, width) in enumerate(places(side, layers)):
        at = pl.ds(pl.multiple_of(at, 8), width)
        for row in range(HALO):
            grid[jnp.where(flipped, HALO - 1 - row, row), at, :] = filtered[start : start + width]
            start += width
        edge[at, :] = added[index * 32 : index * 32 + width]


def near_cut(side):
    return ((iota((16, LANES), 1) + jnp.where(side == 0, 3, 0)) & (LANES - 1)) < 3


def next_row(value, chain, ring, scale=None):
    for level in range(6):
        previous, chain[level] = chain[level], value
        if previous is None:
            return None
        value = previous + value
    if scale is not None:
        value = value * scale
    ring.append(value)
    if len(ring) < 7:
        return None
    slope = (ring[6] - ring[0]) - 9.0 * (ring[5] - ring[1]) + 45.0 * (ring[4] - ring[2])
    center = ring[3]
    ring.pop(0)
    return center, slope


def keep(kept, y, at, center, slope):
    kept[0, y, at, :], kept[2, y, at, :] = split(center)
    kept[1, y, at, :], kept[3, y, at, :] = split(slope)


def shade_rows(kept, w1, w2, out, layers, first, flipped, last):
    kw, kh = layers * FIELDS, HALO * FIELDS
    wide = 2 * LANES
    window = kw + 2 * kh
    hidden = w1.shape[1] // layers
    rest = w1.shape[2] - 6 * window
    ones = jnp.where(iota((rest, wide), 0) < 2, 1.0, 0.0).astype(BF16)
    sub = iota((layers, wide), 0)
    scale = depth_scale / (lax.axis_size("depth") * layers)

    def splat(index):
        line = w2[index : index + 1, :]
        return jnp.broadcast_to(jnp.concatenate([line, line], 1), (layers, wide))

    def target(k):
        return pl.ds(jnp.where(flipped, last - first - k, first + k), 1)

    for y in range(0, kept.shape[1], 2):
        total = jnp.zeros((1, wide), F32)
        front = jnp.ones((1, wide), F32)
        color = [jnp.zeros((layers, wide), F32) for unused in range(3)]
        for half in range(2):
            at = pl.ds(half * kw, window)
            c_high, s_high, c_low, s_low = [
                jnp.concatenate([kept[k, y, at, :], kept[k, y + 1, at, :]], 1) for k in range(4)
            ]
            stacked = jnp.concatenate([c_high, s_high, c_high, s_high, c_low, s_low, ones], 0)
            units = jnp.tanh(dot(w1[half], stacked))
            o = [splat(4 * hidden + c) for c in range(4)]
            for h in range(hidden):
                unit = units[h * layers : (h + 1) * layers]
                for c in range(4):
                    o[c] = o[c] + splat(c * hidden + h) * unit
            x = o[3]
            optical = jnp.log(1.0 + jnp.exp(x)) * scale
            through = optical
            for step in (1, 2, 4):
                through = through + jnp.where(sub >= step, pltpu.roll(through, step, 0), 0.0)
            through = through + total if half else through
            total = through[layers - 1 :]
            after = jnp.exp(-through)
            before = jnp.where(sub == 0, front, pltpu.roll(after, 1, 0))
            front = after[layers - 1 :]
            weight = before - after
            for c in range(3):
                color[c] = color[c] + weight * jnp.tanh(o[c])
        lines = [0.5 * (1.0 - front + jnp.sum(color[c], axis=0, keepdims=True)) for c in range(3)]
        for c, line in enumerate(lines + [front]):
            out[c, target(y), :] = line[:, :LANES]
            out[c, target(y + 1), :] = line[:, LANES:]


def filter_kernel(mine, swap, straight, diagonal, filters, grid, edge, *, layers, rows):
    side = lax.axis_index("depth") & 1
    flipped = (lax.axis_index("row") & 1) == 0
    for source, (at, width) in zip((mine, swap, straight, diagonal), places(side, layers)):
        at = pl.ds(pl.multiple_of(at, 8), width)
        filtered = dot(source[0 : rows * width, :], filters[0])
        for row in range(rows):
            grid[jnp.where(flipped, rows - 1 - row, row), at, :] = filtered[row * width : (row + 1) * width]
        edge[at, :] = dot(source[rows * width : rows * width + 32, :], filters[1])[:width]


def most_kernel(own_grid, own_edge, halo, w1, w2, filters, out, state, grid, edge, kept, *, layers, rows):
    side = lax.axis_index("depth") & 1
    flipped = (lax.axis_index("row") & 1) == 0
    kk = 2 * (layers + HALO) * FIELDS
    place_halo(halo, grid, edge, layers, side, flipped, filters[0], filters[2])
    near = near_cut(side)

    def filter_rows(group, carry):
        at = pl.ds(pl.multiple_of(group * 16, 16), 16)
        halo_edge, edges = edge[at, :], own_edge[at, :]
        chain, ring = [None] * 6, []
        for r in range(rows + HALO):
            turned = pltpu.roll(halo_edge if r < HALO else edges, (-3 * r) % LANES, 1)
            value = grid[r, at, :] if r < HALO else own_grid[r - HALO, at, :]
            given = next_row(value + jnp.where(near, turned, 0.0), chain, ring)
            if given is not None:
                keep(kept, r - 2 * HALO, at, *given)
        for index, value in enumerate(chain + ring):
            state[index, at, :] = value
        return carry

    lax.fori_loop(0, kk // 16, filter_rows, 0, unroll=kk // 16)
    shade_rows(kept, w1, w2, out, layers, 0, flipped, rows - 1)


def rest_kernel(halo, w1, w2, filters, state, done, out, grid, edge, kept, *, layers, rows):
    out[...] = done[...]
    side = lax.axis_index("depth") & 1
    band = lax.axis_index("row")
    flipped = (band & 1) == 0
    kk = 2 * (layers + HALO) * FIELDS
    place_halo(halo, grid, edge, layers, side, flipped, filters[0], filters[3])
    near = near_cut(side)
    outside = jnp.where(flipped, band == 0, band == lax.axis_size("row") - 1)
    inside = jnp.where(outside, 0.0, 1.0)

    def filter_rows(group, carry):
        at = pl.ds(pl.multiple_of(group * 16, 16), 16)
        edges = edge[at, :]
        values = [state[index, at, :] for index in range(12)]
        chain, ring = values[:6], values[6:]
        for r in range(HALO):
            turned = pltpu.roll(edges, (-3 * r) % LANES, 1)
            value = grid[r, at, :] + jnp.where(near, turned, 0.0)
            keep(kept, r, at, *next_row(value, chain, ring, inside if r >= 3 else None))
        return carry

    lax.fori_loop(0, kk // 16, filter_rows, 0, unroll=kk // 16)
    shade_rows(kept, w1, w2, out, layers, rows - HALO, flipped, rows - 1)


def call(kernel, out_shape, operands, scratch=(), flops=0, name=None):
    vmem = pl.BlockSpec(memory_space=pltpu.VMEM)
    return pl.pallas_call(
        kernel,
        out_shape=out_shape,
        in_specs=[vmem] * len(operands),
        out_specs=jax.tree.map(lambda unused: vmem, out_shape),
        scratch_shapes=list(scratch),
        compiler_params=pltpu.CompilerParams(vmem_limit_bytes=40 * 2**20),
        cost_estimate=pl.CostEstimate(flops=flops, bytes_accessed=2**20, transcendentals=0),
        name=name,
    )(*operands)


def combine(front, back):
    is_color = lax.broadcasted_iota(jnp.int32, front.shape, 0) < 3
    return jnp.where(is_color, front, 0.0) + front[3:4] * back


def local(fields, w_in, b_in, w_out, b_out):
    layers, rows, columns = fields.shape[1:]
    hidden = w_in.shape[0]
    slabs = lax.axis_size("depth")
    bands = lax.axis_size("row")
    me = lax.axis_index("depth")
    side = me & 1
    kw, kh = layers * FIELDS, HALO * FIELDS
    kk = 2 * (kw + kh)
    shape = jax.ShapeDtypeStruct
    mine, theirs, own_halo, other_halo = call(
        pack_kernel,
        [
            shape(((rows + 1) * kw, LANES), BF16),
            shape(((rows + 1) * kw, LANES), BF16),
            shape((rows * kh + kw, LANES), BF16),
            shape((rows * kh + kw, LANES), BF16),
        ],
        (fields,),
        [pltpu.VMEM((rows * (kw + 4), LANES), F32)] * 2,
        name="pack",
    )
    swap_pairs = [(i, i ^ 1) for i in range(slabs)]
    odd, even = range(1, slabs, 2), range(0, slabs, 2)
    diagonal_pairs = [(i, i + 1) for i in odd if i + 1 < slabs] + [(i, i - 1) for i in even if i]
    straight_pairs = [(i, i + 2) for i in odd if i + 2 < slabs] + [(i, i - 2) for i in even if i]
    swap = lax.ppermute(theirs, "depth", swap_pairs)
    diagonal = lax.ppermute(other_halo, "depth", diagonal_pairs)
    straight = lax.ppermute(own_halo, "depth", straight_pairs)
    swap, straight, diagonal = lax.optimization_barrier((swap, straight, diagonal))

    width = -(-(6 * (kw + 2 * kh) + 2) // 256) * 256
    w1, w2, filters = call(
        functools.partial(weights_kernel, layers=layers, rows=rows, hidden=hidden, slabs=slabs),
        [
            shape((2, layers * hidden, width), BF16),
            shape((4 * hidden + 8, LANES), F32),
            shape((4, LANES, LANES), BF16),
        ],
        (w_in, b_in[None], w_out, b_out[None]),
        flops=10**8,
        name="weights",
    )
    mine, w1, w2, filters = lax.optimization_barrier((mine, w1, w2, filters))
    message = shape((HALO * kk + 4 * 32, LANES), BF16)
    first, second = call(band_kernel, [message, message], (mine, swap, straight, diagonal), name="band")
    within = [(i, i ^ 1) for i in range(bands)]
    across = [(i, i + 1) for i in range(1, bands - 1, 2)] + [(i + 1, i) for i in range(1, bands - 1, 2)]
    second = lax.ppermute(second, "row", across)
    first = lax.ppermute(first, "row", within)

    own_grid, own_edge = call(
        functools.partial(filter_kernel, layers=layers, rows=rows),
        [shape((rows, kk, LANES), F32), shape((kk, LANES), F32)],
        (mine, swap, straight, diagonal, filters),
        flops=10**9,
        name="filter",
    )
    image = shape((4, rows, LANES), F32)
    current, state = call(
        functools.partial(most_kernel, layers=layers, rows=rows),
        [image, shape((12, kk, LANES), F32)],
        (own_grid, own_edge, first, w1, w2, filters),
        [
            pltpu.VMEM((HALO, kk, LANES), F32),
            pltpu.VMEM((kk, LANES), F32),
            pltpu.VMEM((4, rows - HALO, kk, LANES), BF16),
        ],
        flops=10**10,
        name="shade_most",
    )
    current = call(
        functools.partial(rest_kernel, layers=layers, rows=rows),
        image,
        (second, w1, w2, filters, state, current),
        [
            pltpu.VMEM((HALO, kk, LANES), F32),
            pltpu.VMEM((kk, LANES), F32),
            pltpu.VMEM((4, HALO, kk, LANES), BF16),
        ],
        flops=10**9,
        name="shade_rest",
    )
    step = 2
    while step < slabs:
        received = lax.ppermute(current, "depth", [(i, i ^ step) for i in range(slabs)])
        behind = (me & step) != 0
        current = combine(jnp.where(behind, received, current), jnp.where(behind, current, received))
        step *= 2
    other = lax.ppermute(current, "depth", swap_pairs)
    first_half = jnp.where(side == 0, current, other)
    second_half = jnp.where(side == 0, other, current)
    whole = jnp.concatenate([first_half, second_half], 2)
    is_color = lax.broadcasted_iota(jnp.int32, whole.shape, 0) < 3
    return jnp.where(is_color, whole, 1.0 - whole)


def solution(mesh):
    return jax.shard_map(
        local,
        mesh=mesh,
        in_specs=(P(None, "depth", "row", None), P(), P(), P(), P()),
        out_specs=P(None, "row", None),
        check_vma=False,
    )
```
